32 devices in a mesh: batch: 2 (over x), lat: 4 (over z), lon: 4 (over y, core).
Axes of the slice: x: 2, y: 2, z: 4, core: 2. Of those that a mesh axis runs over, the one named last changes fastest.
Arguments:
- inputs: bfloat16 [8, 64, 128, 128], P('batch', 'lat', 'lon'), may hold values from -22 to 22
- kernels: bfloat16 [4, 3, 3, 128, 128], replicated, may hold values from -0.1875 to 0.1875
- biases: float32 [4, 128], replicated, may hold values from -3 to 3
- gains: float32 [4, 128], replicated, may hold values from 0.1 to 1.9
- offsets: float32 [4, 128], replicated, may hold values from -2 to 2
- keep_masks: int32 [4, 8, 64, 128, 128], P(None, 'batch', 'lat', 'lon'), may hold values 0 or 1
- cotangent: bfloat16 [8, 64, 128, 128], P('batch', 'lat', 'lon'), may hold values from -6 to 6
Outputs:
- output: bfloat16 [8, 64, 128, 128], P('batch', 'lat', 'lon')
- input_grad: float32 [8, 64, 128, 128], P('batch', 'lat', 'lon')
- kernel_grad: float32 [4, 3, 3, 128, 128], replicated
- bias_grad: float32 [4, 128], replicated
- gain_grad: float32 [4, 128], replicated
- offset_grad: float32 [4, 128], replicated
The draws below stay inside these ranges and needn't reach their ends.
All inputs are finite; a program needn't handle non-finite values. No bound on the sum of `keep_masks` on one device may be relied on, other than what follows from the above.
Results may differ from the reference program's by a relative error of at most 0.0065.
Values may be sent and summed in bfloat16 or wider, within the bound.
No kernel may reach another device: no remote copies, remote signals or barrier semaphores. Data moves between devices by JAX's collectives and lax.ppermute only.
A program may use at most 128 MiB of HBM per device.

```python
import math
import jax
import jax.numpy as jnp
from jax import lax

C = 128
H = 64
W = 128
LAYERS = 4
GRIDS = 8


def longitude_wave(key, amplitude):
    phase = jax.random.uniform(key, (C,), jnp.float32, -math.pi, math.pi)
    cols = jnp.arange(W, dtype=jnp.float32)
    angle = 2.0 * math.pi / W * cols[:, None] + phase[None, :]
    return amplitude * jnp.cos(angle)


def draw_inputs(key, part):
    key = jax.random.fold_in(key, 11)
    first_key = jax.random.fold_in(key, 0)
    second_key = jax.random.fold_in(key, 1)
    fourth_key = jax.random.fold_in(key, 3)
    fifth_key = jax.random.fold_in(key, 4)
    rows = jnp.arange(H, dtype=jnp.float32)
    lat_scale = 0.6 + 0.6 * rows / max(H - 1, 1)
    channel_scale = jnp.exp(jax.random.uniform(second_key, (C,), jnp.float32, math.log(0.5), math.log(2.0)))
    grid_shift = jnp.clip(jax.random.normal(fifth_key, (GRIDS, C), jnp.float32), -2.5, 2.5)
    wave = longitude_wave(fourth_key, 1.0)
    base = jnp.clip(jax.random.normal(first_key, (GRIDS, H, W, C), jnp.float32), -6.0, 6.0)
    values = base * lat_scale[None, :, None, None] + grid_shift[:, None, None, :] + wave[None, None, :, :]
    values = jnp.clip(values * channel_scale, -21.5, 21.5)
    return values.astype(jnp.bfloat16)


def draw_cotangent(key, part):
    key = jax.random.fold_in(key, 23)
    first_key, second_key, third_key = jax.random.split(key, 3)
    grid_shift = 0.8 * jnp.clip(jax.random.normal(second_key, (GRIDS, C), jnp.float32), -2.5, 2.5)
    wave = longitude_wave(third_key, 0.6)
    base = jnp.clip(jax.random.normal(first_key, (GRIDS, H, W, C), jnp.float32), -3.0, 3.0)
    values = base + grid_shift[:, None, None, :] + wave[None, None, :, :]
    values = jnp.clip(values, -5.9, 5.9)
    return values.astype(jnp.bfloat16)


def touch_ends(values, key, smallest, largest):
    longest = values.shape.index(max(values.shape))
    spots = []
    for shift in (0, 1):
        where = [jax.random.randint(jax.random.fold_in(key, axis), (), 0, length) for axis, length in enumerate(values.shape)]
        where[longest] = (where[longest] + shift) % values.shape[longest]
        spots.append(tuple(where))
    return values.at[spots[0]].set(smallest).at[spots[1]].set(largest)


def gaussian(key, extent, scale, limit, kind=jnp.bfloat16):
    entries = jax.random.normal(key, extent, jnp.float32) * scale
    return jnp.minimum(jnp.maximum(entries, -limit), limit).astype(kind)


def setup_inputs(seed: int = 0) -> dict:
    key_of = jax.random.split(jax.random.key(seed), 8)
    inputs = draw_inputs(jax.random.fold_in(key_of[7], 71), 0)
    kernels = gaussian(key_of[1], (LAYERS, 3, 3, C, C), (9 * C) ** -0.5, 0.1875)
    biases = gaussian(key_of[2], (LAYERS, C), 0.5, 3.0, jnp.float32)
    gains = jnp.clip(1.0 + 0.18 * jax.random.normal(key_of[3], (LAYERS, C), jnp.float32), 0.1, 1.9)
    offsets = gaussian(key_of[4], (LAYERS, C), 0.3, 2.0, jnp.float32)
    keep_masks = touch_ends((jax.random.randint(key_of[5], (LAYERS, GRIDS, H, W, C), 0, 10) < 9).astype(jnp.int32), jax.random.fold_in(key_of[5], 1), 0, 1)
    cotangent = draw_cotangent(jax.random.fold_in(key_of[7], 71), 0)
    return {"inputs": inputs, "kernels": kernels, "biases": biases, "gains": gains, "offsets": offsets, "keep_masks": keep_masks, "cotangent": cotangent}


eps = 1e-05
keep_rate = 0.9

@jax.custom_vjp
def low(v):
    return lax.optimization_barrier(v.astype(jnp.bfloat16)).astype(jnp.float32)

@jax.custom_vjp
def low_back(v):
    return v

def low_keep(v):
    return (low(v), None)

def low_pass(kept, grad):
    return (grad,)

def back_keep(v):
    return (v, None)

def back_low(kept, grad):
    return (low(grad),)
low.defvjp(low_keep, low_pass)
low_back.defvjp(back_keep, back_low)

def wrap_pad(field):
    widened = jnp.concatenate([field[:, :, -1:], field, field[:, :, :1]], axis=2)
    return jnp.pad(widened, ((0, 0), (1, 1), (0, 0), (0, 0)))

def convolve(field, kernel):
    return lax.conv_general_dilated(wrap_pad(field), kernel, (1, 1), 'VALID', dimension_numbers=('NHWC', 'HWIO', 'NHWC'), precision=lax.Precision.HIGHEST)

def conv_layer(field, kernel, shift_bias, gain_row, offset_row, keeper):
    pre = low_back(convolve(low(field), kernel) + shift_bias)
    act = jax.nn.silu(pre)
    center = lax.optimization_barrier(jnp.mean(act, axis=(0, 1, 2)))
    spread = lax.optimization_barrier(jnp.mean(jnp.square(act - center), axis=(0, 1, 2)))
    normed = (act - center) * lax.rsqrt(spread + eps)
    return (normed * gain_row + offset_row) * keeper * (1.0 / keep_rate)

def forward(field, kernels, biases, gains, offsets, keepers):
    for section in range(LAYERS // 2):
        first = 2 * section
        hidden = conv_layer(field, kernels[first], biases[first], gains[first], offsets[first], keepers[first])
        second = first + 1
        hidden = conv_layer(hidden, kernels[second], biases[second], gains[second], offsets[second], keepers[second])
        field = field + hidden
    return field

def reference(inputs, kernels, biases, gains, offsets, keep_masks, cotangent):
    keepers = keep_masks.astype(jnp.float32)

    def wrapped(field, kernel_all, bias_all, gain_all, offset_all):
        return forward(field, kernel_all, bias_all, gain_all, offset_all, keepers)
    result, pullback = jax.vjp(wrapped, inputs.astype(jnp.float32), kernels.astype(jnp.float32), biases.astype(jnp.float32), gains.astype(jnp.float32), offsets.astype(jnp.float32))
    grads = pullback(cotangent.astype(jnp.float32))
    return (result.astype(jnp.bfloat16), grads[0], grads[1], grads[2], grads[3], grads[4])
```

```python
import functools

import jax
import jax.numpy as jnp
from jax import lax
from jax.experimental import pallas as pl
from jax.experimental.pallas import tpu as pltpu
from jax.sharding import PartitionSpec as P

eps = 1e-05
keep_rate = 0.9
EVERY = ("batch", "lat", "lon")
EXT = 8
LANES = 128
F32 = jnp.float32
LOW = jnp.bfloat16


def partners(axis, periodic):
    count = lax.axis_size(axis)
    first = [(i, i ^ 1) for i in range(count)]
    second = []
    for i in range(count):
        j = i + 1 if i % 2 else i - 1
        if periodic:
            second.append((i, j % count))
        elif 0 <= j < count:
            second.append((i, j))
    return first, second


def trade(pair, axis, periodic):
    first, second = partners(axis, periodic)
    return lax.ppermute(pair[0], axis, first), lax.ppermute(pair[1], axis, second)


def to_all(rows):
    return lax.all_to_all(rows, EVERY, 0, 0)


def to_half(rows, devices):
    groups = [[i for i in range(devices) if i % 2 == side] for side in range(2)]
    return lax.all_to_all(rows, EVERY, 0, 0, axis_index_groups=groups)


def to_pair(block):
    return lax.ppermute(block, "lon", partners("lon", True)[0])


def sigmoid(v):
    return 0.5 * jnp.tanh(0.5 * v) + 0.5


def norm_consts(stats_ref, devices):
    stats = stats_ref[...]
    total = jnp.sum(stats, axis=0)
    center = total[0:1] * (1.0 / devices)
    apart = jnp.sum(jnp.square(stats - center[None]), axis=0)
    spread = (total[1:2] + apart[0:1]) * (1.0 / devices)
    return center, lax.rsqrt(spread + eps)


def top_sums(stats_ref, center, inv):
    stats = stats_ref[...]
    total = jnp.sum(stats, axis=0)
    apart = stats[:, 0:1, :] - center[None]
    return total[2:3], (total[3:4] + jnp.sum(apart * stats[:, 2:3, :], axis=0)) * inv


def shifted(value, width):
    return pltpu.roll(value, 1, 1), value, pltpu.roll(value, width - 1, 1)


def store_shifted(taps, row, count, value, width):
    for s, part in enumerate(shifted(value, width)):
        taps[s, pl.ds(row, count)] = part.astype(LOW)


def lay_weights(kernel_ref, layer, back, out):
    blank = jnp.zeros((3 * LANES, LANES), LOW)
    out[9 * LANES : 12 * LANES, 0:LANES] = blank
    out[0 : 3 * LANES, LANES : 2 * LANES] = blank
    for r in range(3):
        for s in range(3):
            if back:
                block = kernel_ref[layer, (2 - r) * 3 + 2 - s].astype(F32).T.astype(LOW)
            else:
                block = kernel_ref[layer, r * 3 + s]
            at = (r * 3 + s) * LANES
            out[at : at + LANES, 0:LANES] = block
            out[at + 3 * LANES : at + 4 * LANES, LANES : 2 * LANES] = block


def conv_pairs(taps, weight_ref, row, pairs, cols):
    parts = []
    for t in range(4):
        for s in range(3):
            parts.append(jnp.stack([taps[s, row - 1 + t + 2 * k, 0:cols, :] for k in range(pairs)]))
    left = jnp.concatenate(parts, axis=-1).reshape(pairs * cols, 12 * LANES)
    both = jnp.dot(left, weight_ref[...], preferred_element_type=F32)
    out = []
    for k in range(pairs):
        for h in range(2):
            out.append(both[k * cols : (k + 1) * cols, h * LANES : (h + 1) * LANES])
    return out


def chunks(lo, hi, pairs):
    at = lo
    while at < hi:
        count = min(pairs, (hi - at) // 2)
        yield at, count
        at += 2 * count


def loop_rows(lo, hi, body):
    def step(i, carry):
        body(lo + 2 * i)
        return carry

    lax.fori_loop(0, (hi - lo) // 2, step, 0, unroll=2)


def loop_grids(grids, body):
    def step(g, carry):
        body(g)
        return carry

    lax.fori_loop(0, grids, step, 0)


def fold(value):
    return jnp.sum(value.reshape(-1, 8, LANES), axis=0)


def to_row(value):
    return jnp.sum(value, axis=0, keepdims=True)


def both_ways(even, give_first, give_second):
    @pl.when(even == 1)
    def _():
        give_first(False)
        give_second(True)

    @pl.when(even == 0)
    def _():
        give_first(True)
        give_second(False)


def whichever(even, place, got_first, got_second):
    @pl.when(even == 1)
    def _():
        place(got_second, got_first)

    @pl.when(even == 0)
    def _():
        place(got_first, got_second)


def row_edges(geo, info, sources, heights, first, second):
    grids, rows = geo["G"], geo["R"]

    def give(out):
        def act(low):
            at = 0
            for src, h in zip(sources, heights):
                for g in range(grids):
                    out[g, at : at + h] = src[g, 0:h] if low else src[g, rows - h : rows]
                at += h
        return act

    both_ways(info[0], give(first), give(second))


def field_edge_kernel(geo, info, x, first, second):
    row_edges(geo, info, [x], [EXT], first, second)


def mask_edge_kernel(geo, info, masks, cot, *outs):
    grids = geo["G"]
    lows = outs[0:4]
    for k in range(4):
        for g in range(grids):
            lows[k][g] = masks[k, g].astype(F32).astype(LOW)
    row_edges(geo, info, [lows[0]], geo["heights"][1:2], outs[4], outs[5])
    row_edges(geo, info, list(lows[1:]) + [cot], geo["heights"][2:], outs[6], outs[7])


def stack_kernel(geo, heights, info, *refs):
    grids, rows, cols = geo["G"], geo["R"], geo["C"]
    count = len(heights)
    sources, got_first, got_second = refs[:count], refs[count], refs[count + 1]
    talls = refs[count + 2 : 2 * count + 2]
    first, second = refs[2 * count + 2 :]

    def place(low, high):
        at = 0
        for k, h in enumerate(heights):
            for g in range(grids):
                talls[k][g, 0:h] = low[g, at : at + h]
                talls[k][g, h + rows : 2 * h + rows] = high[g, at : at + h]
            at += h

    whichever(info[0], place, got_first, got_second)
    for k, h in enumerate(heights):
        for g in range(grids):
            talls[k][g, h : h + rows] = sources[k][g]

    def give(out):
        def act(low):
            at = 0
            for k, h in enumerate(heights):
                for g in range(grids):
                    part = talls[k][g, :, 0:EXT, :] if low else talls[k][g, :, cols - EXT : cols, :]
                    out[g, at : at + rows + 2 * h] = part
                at += rows + 2 * h
        return act

    both_ways(info[1], give(first), give(second))


def widen(geo, info, height, at, tall, got_first, got_second, out):
    cols, total = geo["C"], geo["R"] + 2 * height

    def place(low, high):
        for g in range(geo["G"]):
            right = high[g, at : at + total].astype(F32)
            left = low[g, at : at + total].astype(F32)
            out[g, :, cols:, :] = jnp.concatenate([right, left], axis=1).astype(LOW)

    whichever(info[1], place, got_first, got_second)
    for g in range(geo["G"]):
        out[g, :, 0:cols, :] = tall[g]


def forward_kernel(layer, geo, *refs):
    grids, rows, devices, width, cols = geo["G"], geo["R"], geo["D"], geo["CE"], geo["C"]
    heights = geo["heights"]
    refs = list(refs)
    info, gains, offsets, biases, kernels = (refs.pop(0) for _ in range(5))
    if layer:
        stats, pre_in = refs.pop(0), refs.pop(0)
    field = refs.pop(0) if layer == 2 else None
    members = geo["members"][layer]
    pieces = [[refs.pop(0) for _ in range(3)] for _ in members]
    sums_out = refs.pop(0)
    exts = [refs.pop(0) for _ in members]
    pre_out = refs.pop(0)
    low_out = refs.pop(0) if layer else None
    field_out = refs.pop(0) if layer == 2 else None
    taps, weight, acts, acc = refs
    lo, hi = layer + 1, geo["RE"] - 1 - layer

    lay_weights(kernels, layer, False, weight)
    for k, parts, ext in zip(members, pieces, exts):
        widen(geo, info, heights[k], geo["starts"][k], *parts, ext)
    ext = exts[0]
    if layer == 3:
        keep3, cot = exts[1], exts[2]
    if layer:
        center, inv = norm_consts(stats, devices)
        scale = inv * gains[layer - 1 : layer, :]
        shift = offsets[layer - 1 : layer, :]
    bias = biases[layer : layer + 1, :]

    def one_grid(g):
        def prepare(r):
            if layer == 0:
                value = ext[g, pl.ds(r, 2)].astype(F32)
            else:
                p = pre_in[g, pl.ds(r, 2)]
                act = p * sigmoid(p)
                kept = ext[g, pl.ds(r - layer, 2)].astype(F32) * (1.0 / keep_rate)
                value = ((act - center) * scale + shift) * kept
                if layer == 2:
                    value = value + field[g, pl.ds(r, 2)].astype(F32)
            store_shifted(taps, r, 2, value, width)
            if layer == 2:
                @pl.when((r >= EXT - 1) & (r < EXT + rows))
                def _():
                    field_out[g, pl.ds(r - (EXT - 1), 2)] = value[:, 0:cols, :]

        loop_rows(lo - 1, hi + 1, prepare)
        if layer:
            low_out[g] = taps[1, EXT - 1 : EXT + 1 + rows]
        number = rows * cols
        total = jnp.zeros((8, LANES), F32)
        for at, count in chunks(lo, hi, 5):
            for k, part in enumerate(conv_pairs(taps, weight, at, count, width)):
                part = part + bias
                pre_out[g, at + k] = part
                if EXT <= at + k < EXT + rows:
                    inner = part[0:cols]
                    act = inner * sigmoid(inner)
                    acts[at + k - EXT] = act
                    total = total + fold(act)
        mean = to_row(total) * (1.0 / number)
        square = jnp.zeros((8, LANES), F32)
        first = jnp.zeros((8, LANES), F32)
        second = jnp.zeros((8, LANES), F32)
        for k in range(rows):
            act = acts[k]
            apart = act - mean
            square = square + fold(jnp.square(apart))
            if layer == 3:
                z = cot[g, heights[5] + k, 0:cols, :].astype(F32) * keep3[g, heights[4] + k, 0:cols, :].astype(F32)
                first = first + fold(z)
                second = second + fold(z * apart)
            if layer == 0:
                p = pre_out[g, EXT + k, 0:cols, :]
                s = sigmoid(p)
                slope = s * (1.0 + p * (1.0 - s))
                first = first + fold(slope)
                second = second + fold(slope * act)
        acc[pl.ds(g, 1)] = mean
        acc[pl.ds(grids + g, 1)] = to_row(square) * (1.0 / number)
        if layer in (0, 3):
            acc[pl.ds(2 * grids + g, 1)] = to_row(first)
            acc[pl.ds(3 * grids + g, 1)] = to_row(second)

    loop_grids(grids, one_grid)
    means = acc[0:grids]
    middle = jnp.mean(means, axis=0, keepdims=True)
    away = means - middle
    spread = jnp.mean(acc[grids : 2 * grids] + jnp.square(away), axis=0, keepdims=True)
    out = [middle, spread]
    if layer == 3:
        ones = acc[2 * grids : 3 * grids]
        out.append(to_row(ones) * (1.0 / keep_rate))
        out.append(to_row(acc[3 * grids : 4 * grids] + away * ones) * (1.0 / keep_rate))
    if layer == 0:
        out += [to_row(acc[2 * grids : 3 * grids]), to_row(acc[3 * grids : 4 * grids])]
    for k, row in enumerate(out):
        sums_out[:, k : k + 1, :] = jnp.broadcast_to(row[None], (devices, 1, LANES))


def back_consts(layer, geo, stats, sums, gains):
    center, inv = norm_consts(stats, geo["D"])
    if layer == 3:
        one, two = top_sums(stats, center, inv)
    else:
        total = jnp.sum(sums[...], axis=0)
        one, two = total[0:1], total[1:2]
    pixels = float(geo["D"] * geo["G"] * geo["R"] * geo["C"])
    return center, inv, inv * gains[layer : layer + 1, :], one * (1.0 / pixels), two * (1.0 / pixels)


def backward_kernel(layer, geo, *refs):
    grids, rows, devices, width, cols = geo["G"], geo["R"], geo["D"], geo["CE"], geo["C"]
    heights = geo["heights"]
    refs = list(refs)
    info, gains, offsets, kernels, stats, sums, pre = (refs.pop(0) for _ in range(7))
    cot = refs.pop(0) if layer >= 2 else None
    if layer == 3:
        keep_top, field = refs.pop(0), refs.pop(0)
    else:
        z_in = refs.pop(0)
    if layer:
        keep, stats_below, pre_below = refs.pop(0), refs.pop(0), refs.pop(0)
        sums_out, low_out, z_out = refs.pop(0), refs.pop(0), refs.pop(0)
    else:
        grad_in = refs.pop(0)
    grad_out = refs.pop(0) if layer in (0, 2) else None
    result = refs.pop(0) if layer == 3 else None
    taps, weight = refs
    lo, hi = EXT - layer, EXT + rows + layer
    wide = width if layer else cols
    keep_off = EXT - heights[layer] if layer else 0
    cot_off = EXT - heights[5]
    top_off = EXT - heights[4]

    lay_weights(kernels, layer, True, weight)
    center, inv, scale, one, two = back_consts(layer, geo, stats, sums, gains)
    first_row, last_row = info[2], info[3]
    if layer:
        center_b, inv_b = norm_consts(stats_below, devices)

    def one_grid(g, carry):
        def prepare(r):
            p = pre[g, pl.ds(r, 2)]
            s = sigmoid(p)
            act = p * s
            normed = (act - center) * inv
            if layer == 3:
                kept = keep_top[g, pl.ds(r - top_off, 2)].astype(F32) * (1.0 / keep_rate)
                z = cot[g, pl.ds(r - cot_off, 2)].astype(F32) * kept
            else:
                z = z_in[g, pl.ds(r, 2)]
            value = scale * (z - one - normed * two) * (s * (1.0 + p * (1.0 - s)))
            real = [
                jnp.where((r + k >= first_row) & (r + k < last_row), 1.0, 0.0).astype(F32) for k in range(2)
            ]
            value = jnp.stack([value[0] * real[0], value[1] * real[1]])
            store_shifted(taps, r, 2, value, width)

        loop_rows(lo - 1, hi + 1, prepare)
        if layer == 3:
            def finish(k):
                p = pre[g, pl.ds(EXT + k, 2), 0:cols, :]
                normed = (p * sigmoid(p) - center) * inv
                kept = keep_top[g, pl.ds(EXT - top_off + k, 2), 0:cols, :].astype(F32) * (1.0 / keep_rate)
                y = (normed * gains[layer : layer + 1, :] + offsets[layer : layer + 1, :]) * kept
                result[g, pl.ds(k, 2)] = (field[g, pl.ds(k + 1, 2)] + y).astype(LOW)

            loop_rows(0, rows, finish)
        if layer == 0:
            for at, count in chunks(lo, hi, 4):
                for k, part in enumerate(conv_pairs(taps, weight, at, count, cols)):
                    grad_out[g, at + k - EXT] = grad_in[g, at + k - EXT] + part
            return carry
        first, second, third, fourth = carry
        for k in range(rows):
            row = taps[1, EXT + k, 0:cols, :]
            low_out[g, k] = row
            third = third + fold(row.astype(F32))
        for at, count in chunks(lo, hi, 5):
            for k, part in enumerate(conv_pairs(taps, weight, at, count, width)):
                r = at + k
                inner = EXT <= r < EXT + rows
                if layer == 2:
                    part = part + cot[g, r - cot_off].astype(F32)
                    if inner:
                        grad_out[g, r - EXT] = part[0:cols]
                z = part * (keep[g, r - keep_off].astype(F32) * (1.0 / keep_rate))
                z_out[g, r] = z
                if inner:
                    z = z[0:cols]
                    p = pre_below[g, r, 0:cols, :]
                    s = sigmoid(p)
                    first = first + fold(z)
                    second = second + fold(z * (p * s - center_b))
                    if layer == 1:
                        fourth = fourth + fold(z * (s * (1.0 + p * (1.0 - s))))
        return first, second, third, fourth

    zero = jnp.zeros((8, LANES), F32)
    found = lax.fori_loop(0, grids, one_grid, (zero,) * 4)
    if layer:
        out = [to_row(v) for v in found]
        out[1] = out[1] * inv_b
        for k in range(4 if layer == 1 else 3):
            sums_out[:, k : k + 1, :] = jnp.broadcast_to(out[k][None], (devices, 1, LANES))


def weight_kernel(layer, geo, *refs):
    grids, rows, cols, width = geo["G"], geo["R"], geo["C"], geo["CE"]
    refs = list(refs)
    info, low = refs.pop(0), refs.pop(0)
    if layer:
        dpre = refs.pop(0)
    else:
        gains, stats, sums, pre, z_in = (refs.pop(0) for _ in range(5))
        center, inv, scale, one, two = back_consts(layer, geo, stats, sums, gains)
    keep_half, send_half, taps, acc = refs
    low_off = 0 if layer else EXT - 1
    acc[...] = jnp.zeros(acc.shape, F32)

    def one_grid(g):
        def prepare(r):
            value = low[g, pl.ds(r + low_off, 2)].astype(F32)
            for s, part in enumerate(shifted(value, width)):
                taps[s, pl.ds(r, 2)] = part[:, 0:cols, :].astype(LOW)

        loop_rows(0, rows + 2, prepare)
        parts = [taps[s, r : r + rows] for r in range(3) for s in range(3)]
        spread = jnp.concatenate(parts, axis=-1).reshape(rows * cols, 9 * LANES)
        if layer:
            right = dpre[g].reshape(rows * cols, LANES)
        else:
            p = pre[g, EXT : EXT + rows, 0:cols, :]
            s = sigmoid(p)
            normed = (p * s - center) * inv
            z = z_in[g, EXT : EXT + rows, 0:cols, :]
            value = scale * (z - one - normed * two) * (s * (1.0 + p * (1.0 - s)))
            right = value.astype(LOW).reshape(rows * cols, LANES)
        acc[...] += lax.dot_general(right, spread, (((0,), (0,)), ((), ())), preferred_element_type=F32)

    loop_grids(grids, one_grid)
    half = 9 * LANES // 2

    def give(upper, out):
        for t in range(9):
            lo, hi = max(t * LANES, half * upper), min((t + 1) * LANES, half * (upper + 1))
            if lo < hi:
                block = acc[:, t * LANES : (t + 1) * LANES].T
                out[lo - half * upper : hi - half * upper] = block[lo - t * LANES : hi - t * LANES]

    both_ways(info[1], lambda odd: give(int(odd), keep_half), lambda odd: give(int(odd), send_half))


def share_kernel(count, kept, got, out):
    del count
    out[...] = (kept[...] + got[...]).astype(LOW)


def total_kernel(devices, got, out):
    total = jnp.sum(got[...].astype(F32), axis=0)
    out[...] = jnp.broadcast_to(total.astype(LOW)[None], out.shape)


def join_kernel(geo, info, mine, other, out):
    half = 9 * LANES // 2

    def place(low, high):
        for k in range(4):
            out[k, 0:half] = low[k].astype(F32)
            out[k, half:] = high[k].astype(F32)

    @pl.when(info[1] == 1)
    def _():
        place(mine, other)

    @pl.when(info[1] == 0)
    def _():
        place(other, mine)


def rows_kernel(geo, gains, *refs):
    stats, sums = refs[0:4], refs[4:7]
    bias_out, gain_out, offset_out = refs[7:]
    for layer in range(4):
        center, inv = norm_consts(stats[layer], geo["D"])
        if layer == 3:
            one, two = top_sums(stats[3], center, inv)
        else:
            total = jnp.sum(sums[layer][...], axis=0)
            one, two = total[0:1], total[1:2]
        offset_out[layer : layer + 1] = one
        gain_out[layer : layer + 1] = two
        if layer:
            bias_out[layer : layer + 1] = jnp.sum(sums[layer - 1][...], axis=0)[2:3]
        else:
            pixels = float(geo["D"] * geo["G"] * geo["R"] * geo["C"])
            slopes = jnp.sum(stats[0][...], axis=0)
            flat, lifted = slopes[2:3], (slopes[3:4] - center * slopes[2:3]) * inv
            bias_out[0:1] = inv * gains[0:1, :] * (total[3:4] - flat * one / pixels - lifted * two / pixels)


def call(kernel, operands, outs, scratch, flops=10**6, moved=10**6, scalars=1, final=False):
    space = pl.BlockSpec(memory_space=pltpu.VMEM)
    specs = [pl.BlockSpec(memory_space=pltpu.SMEM)] * scalars + [space] * (len(operands) - scalars)
    operands = list(operands[:scalars]) + [pltpu.with_memory_space_constraint(v, pltpu.VMEM) for v in operands[scalars:]]
    shapes = [jax.ShapeDtypeStruct(s, d) if final else pltpu.VMEM(s, d) for s, d in outs]
    return pl.pallas_call(
        kernel,
        in_specs=specs,
        out_specs=[space] * len(outs),
        out_shape=shapes,
        scratch_shapes=[pltpu.VMEM(s, d) for s, d in scratch],
        compiler_params=pltpu.CompilerParams(vmem_limit_bytes=(12 if final else 8) * 2**20),
        cost_estimate=pl.CostEstimate(flops=flops, bytes_accessed=moved, transcendentals=0),
    )(*operands)


def forward_call(layer, geo, operands):
    grids, rows, rows_ext, width, devices = geo["G"], geo["R"], geo["RE"], geo["CE"], geo["D"]
    kinds = 4 if layer in (0, 3) else 2
    outs = [((devices, kinds, LANES), F32)]
    for k in geo["members"][layer]:
        outs.append(((grids, rows + 2 * geo["heights"][k], width, LANES), LOW))
    outs.append(((grids, rows_ext, width, LANES), F32))
    if layer:
        outs.append(((grids, rows + 2, width, LANES), LOW))
    if layer == 2:
        outs.append(((grids, rows + 2, geo["C"], LANES), F32))
    scratch = [
        ((3, rows_ext, width, LANES), LOW),
        ((12 * LANES, 2 * LANES), LOW),
        ((rows, geo["C"], LANES), F32),
        ((kinds * grids, LANES), F32),
    ]
    return call(functools.partial(forward_kernel, layer, geo), operands, outs, scratch, 2 * 10**9, 8 * 10**6)


def backward_call(layer, geo, operands):
    grids, rows, rows_ext, width, devices, cols = geo["G"], geo["R"], geo["RE"], geo["CE"], geo["D"], geo["C"]
    outs = []
    if layer:
        outs.append(((devices, 4 if layer == 1 else 3, LANES), F32))
        outs.append(((grids, rows, cols, LANES), LOW))
        outs.append(((grids, rows_ext, width, LANES), F32))
    if layer in (0, 2):
        outs.append(((grids, rows, cols, LANES), F32))
    if layer == 3:
        outs.append(((grids, rows, cols, LANES), LOW))
    scratch = [((3, rows_ext, width, LANES), LOW), ((12 * LANES, 2 * LANES), LOW)]
    return call(functools.partial(backward_kernel, layer, geo), operands, outs, scratch, 2 * 10**9, 8 * 10**6)


def weight_call(layer, geo, operands):
    half = ((9 * LANES // 2, LANES), F32)
    scratch = [((3, geo["R"] + 2, geo["C"], LANES), LOW), ((LANES, 9 * LANES), F32)]
    return call(functools.partial(weight_kernel, layer, geo), operands, [half, half], scratch, 10**9, 3 * 10**6)


def local(inputs, kernels, biases, gains, offsets, keep_masks, cotangent):
    grids, rows, cols, _ = inputs.shape
    devices = lax.axis_size("batch") * lax.axis_size("lat") * lax.axis_size("lon")
    heights = [EXT, 7, 6, 5, 4, 4]
    starts = [0, 0]
    at = 0
    for k in range(2, 6):
        starts.append(at)
        at += rows + 2 * heights[k]
    geo = dict(
        G=grids, R=rows, C=cols, D=devices, RE=rows + 2 * EXT, CE=cols + 2 * EXT, heights=heights, starts=starts,
        members=[[0], [1], [2], [3, 4, 5]],
    )
    lat, lon = lax.axis_index("lat"), lax.axis_index("lon")
    info = jnp.stack(
        [
            1 - lax.rem(lat, 2),
            1 - lax.rem(lon, 2),
            jnp.where(lat == 0, EXT, 0),
            jnp.where(lat == lax.axis_size("lat") - 1, EXT + rows, rows + 2 * EXT),
        ]
    ).astype(jnp.int32)
    kernels = kernels.reshape(4, 9, LANES, LANES)

    def edges(count):
        return [((grids, count, cols, LANES), LOW)] * 2

    def stacked(sources, got, group):
        tall = [((grids, rows + 2 * heights[k], cols, LANES), LOW) for k in group]
        strip = ((grids, sum(rows + 2 * heights[k] for k in group), EXT, LANES), LOW)
        kernel = functools.partial(stack_kernel, geo, [heights[k] for k in group])
        outs = call(kernel, [info] + sources + list(got), tall + [strip, strip], [])
        return outs[:-2], outs[-2:]

    x_edges = call(functools.partial(field_edge_kernel, geo), [info, inputs], edges(EXT), [])
    x_got = trade(x_edges, "lat", False)
    whole = ((grids, rows, cols, LANES), LOW)
    outs = call(
        functools.partial(mask_edge_kernel, geo), [info, keep_masks, cotangent],
        [whole] * 4 + edges(heights[1]) + edges(sum(heights[2:])), [],
    )
    rest = list(outs[:4]) + [cotangent]
    first_got = trade(outs[4:6], "lat", False)
    later_got = trade(outs[6:8], "lat", False)
    (x_tall,), strips = stacked([inputs], x_got, [0])
    pieces = [(x_tall, *trade(strips, "lon", True))]
    (k_tall,), strips = stacked(rest[:1], first_got, [1])
    pieces.append((k_tall, *trade(strips, "lon", True)))
    talls, strips = stacked(rest[1:], later_got, [2, 3, 4, 5])
    later = trade(strips, "lon", True)
    pieces += [(tall, *later) for tall in talls]

    pres, lows, stats, exts = [None] * 4, [None] * 4, [None] * 4, [None] * 6
    field = None
    for layer in range(4):
        operands = [info, gains, offsets, biases, kernels]
        if layer:
            operands += [stats[layer - 1], pres[layer - 1]]
        if layer == 2:
            operands.append(exts[0])
        members = geo["members"][layer]
        outs = list(forward_call(layer, geo, operands + [v for k in members for v in pieces[k]]))
        stats[layer] = to_all(outs.pop(0))
        for k in members:
            exts[k] = outs.pop(0)
        pres[layer] = outs.pop(0)
        lows[layer] = outs.pop(0) if layer else exts[0]
        if layer == 2:
            field = outs.pop(0)
    keeps, keep_top, cot = exts[1:5], exts[4], exts[5]

    sums = [None] * 4
    sums[3] = stats[3]
    halves = [None] * 4
    z = grad = output = None
    for layer in (3, 2, 1):
        operands = [info, gains, offsets, kernels, stats[layer], sums[layer], pres[layer]]
        if layer >= 2:
            operands.append(cot)
        operands += [keep_top, field] if layer == 3 else [z]
        operands += [keeps[layer - 1], stats[layer - 1], pres[layer - 1]]
        outs = backward_call(layer, geo, operands)
        sums[layer - 1] = to_all(outs[0])
        z = outs[2]
        if layer == 2:
            grad = outs[3]
        if layer == 3:
            output = outs[3]
        halves[layer] = weight_call(layer, geo, [info, lows[layer], outs[1]])
    halves[0] = weight_call(0, geo, [info, lows[0], gains, stats[0], sums[0], pres[0], z])
    operands = [info, gains, offsets, kernels, stats[0], sums[0], pres[0], z, grad]
    (input_grad,) = backward_call(0, geo, operands)

    half = 9 * LANES // 2
    shares = []
    for kept, sent in halves:
        shares += call(functools.partial(share_kernel, 1), [kept, to_pair(sent)], [((half, LANES), LOW)], [], scalars=0)
    share = 4 * half // (devices // 2)
    slots = (devices // 2, share, LANES)
    got = to_half(jnp.stack(shares).reshape(slots), devices)
    (mine,) = call(functools.partial(total_kernel, devices), [got], [(slots, LOW)], [], scalars=0)
    mine = to_half(mine, devices).reshape(4, half, LANES)
    (kernel_grad,) = call(
        functools.partial(join_kernel, geo), [info, mine, to_pair(mine)], [((4, 9 * LANES, LANES), F32)], [], final=True
    )
    small = ((4, LANES), F32)
    bias_grad, gain_grad, offset_grad = call(
        functools.partial(rows_kernel, geo), [gains] + stats + sums[:3], [small] * 3, [], scalars=0, final=True
    )
    return (output, input_grad, kernel_grad.reshape(4, 3, 3, LANES, LANES), bias_grad, gain_grad, offset_grad)


def solution(mesh):
    in_specs = (
        P("batch", "lat", "lon", None),
        P(),
        P(),
        P(),
        P(),
        P(None, "batch", "lat", "lon", None),
        P("batch", "lat", "lon", None),
    )
    out_specs = (P("batch", "lat", "lon", None), P("batch", "lat", "lon", None), P(), P(), P(), P())
    return jax.shard_map(local, mesh=mesh, in_specs=in_specs, out_specs=out_specs, check_vma=False)
```

```python
import functools

import jax
import jax.numpy as jnp
from jax import lax
from jax.experimental import pallas as pl
from jax.experimental.pallas import tpu as pltpu
from jax.sharding import PartitionSpec as P

eps = 1e-05
keep_rate = 0.9
EVERY = ("batch", "lat", "lon")
EXT = 8
LANES = 128
F32 = jnp.float32
LOW = jnp.bfloat16


def partners(axis, periodic):
    count = lax.axis_size(axis)
    first = [(i, i ^ 1) for i in range(count)]
    second = []
    for i in range(count):
        j = i + 1 if i % 2 else i - 1
        if periodic:
            second.append((i, j % count))
        elif 0 <= j < count:
            second.append((i, j))
    return first, second


def trade(pair, axis, periodic):
    first, second = partners(axis, periodic)
    return lax.ppermute(pair[0], axis, first), lax.ppermute(pair[1], axis, second)


def to_all(rows):
    return lax.all_to_all(rows, EVERY, 0, 0)


def to_half(rows, devices):
    groups = [[i for i in range(devices) if i % 2 == side] for side in range(2)]
    return lax.all_to_all(rows, EVERY, 0, 0, axis_index_groups=groups)


def to_pair(block):
    return lax.ppermute(block, "lon", partners("lon", True)[0])


def sigmoid(v):
    return 0.5 * jnp.tanh(0.5 * v) + 0.5


def norm_consts(stats_ref, devices):
    stats = stats_ref[...]
    total = jnp.sum(stats, axis=0)
    center = total[0:1] * (1.0 / devices)
    apart = jnp.sum(jnp.square(stats - center[None]), axis=0)
    spread = (total[1:2] + apart[0:1]) * (1.0 / devices)
    return center, lax.rsqrt(spread + eps)


def top_sums(stats_ref, center, inv):
    stats = stats_ref[...]
    total = jnp.sum(stats, axis=0)
    apart = stats[:, 0:1, :] - center[None]
    return total[2:3], (total[3:4] + jnp.sum(apart * stats[:, 2:3, :], axis=0)) * inv


def shifted(value, width):
    return pltpu.roll(value, 1, 1), value, pltpu.roll(value, width - 1, 1)


def store_shifted(taps, slot, row, value, width):
    for s, part in enumerate(shifted(value, width)):
        taps[slot, s, pl.ds(row, 2)] = part.astype(LOW)


def lay_weights(kernel_ref, layer, back, out):
    blank = jnp.zeros((3 * LANES, LANES), LOW)
    out[9 * LANES : 12 * LANES, 0:LANES] = blank
    out[0 : 3 * LANES, LANES : 2 * LANES] = blank
    for r in range(3):
        for s in range(3):
            if back:
                block = kernel_ref[layer, (2 - r) * 3 + 2 - s].astype(F32).T.astype(LOW)
            else:
                block = kernel_ref[layer, r * 3 + s]
            at = (r * 3 + s) * LANES
            out[at : at + LANES, 0:LANES] = block
            out[at + 3 * LANES : at + 4 * LANES, LANES : 2 * LANES] = block


def conv_pairs(taps, slot, weight_ref, row, pairs, cols):
    parts = []
    for t in range(4):
        for s in range(3):
            parts.append(jnp.stack([taps[slot, s, row - 1 + t + 2 * k, 0:cols, :] for k in range(pairs)]))
    left = jnp.concatenate(parts, axis=-1).reshape(pairs * cols, 12 * LANES)
    both = jnp.dot(left, weight_ref[...], preferred_element_type=F32)
    out = []
    for k in range(pairs):
        for h in range(2):
            out.append(both[k * cols : (k + 1) * cols, h * LANES : (h + 1) * LANES])
    return out


def chunks(lo, hi, pairs):
    at = lo
    while at < hi:
        count = min(pairs, (hi - at) // 2)
        yield at, count
        at += 2 * count


def pipeline(grids, lo, hi, pairs, prepare, convolve, after):
    def step(i, carry):
        prepare(0, lo - 1 + 2 * i, 0)
        return carry

    count = (hi - lo) // 2 + 1
    lax.fori_loop(0, count, step, 0, unroll=4)
    parts = list(chunks(lo, hi, pairs))
    for g in range(grids):
        for j, (at, size) in enumerate(parts):
            if g + 1 < grids:
                for i in range(count * j // len(parts), count * (j + 1) // len(parts)):
                    prepare(g + 1, lo - 1 + 2 * i, (g + 1) % 2)
            convolve(g, at, size, g % 2)
        after(g, g % 2)


def guard(condition, act):
    if isinstance(condition, bool):
        if condition:
            act()
    else:
        pl.when(condition)(act)


def fold(value):
    return jnp.sum(value.reshape(-1, 8, LANES), axis=0)


def to_row(value):
    return jnp.sum(value, axis=0, keepdims=True)


def both_ways(even, give_first, give_second):
    @pl.when(even == 1)
    def _():
        give_first(False)
        give_second(True)

    @pl.when(even == 0)
    def _():
        give_first(True)
        give_second(False)


def whichever(even, place, got_first, got_second):
    @pl.when(even == 1)
    def _():
        place(got_second, got_first)

    @pl.when(even == 0)
    def _():
        place(got_first, got_second)


def cut_rows(geo, info, sources, heights, first, second):
    grids, rows = geo["G"], geo["R"]

    def give(out):
        def act(low):
            at = 0
            for src, h in zip(sources, heights):
                for g in range(grids):
                    out[g, at : at + h] = src[g, 0:h] if low else src[g, src.shape[1] - h :]
                at += h
        return act

    both_ways(info[0], give(first), give(second))


def cut_cols(geo, info, sources, first, second):
    grids, cols = geo["G"], geo["C"]

    def give(out):
        def act(low):
            at = 0
            for src in sources:
                for g in range(grids):
                    part = src[g, :, 0:EXT, :] if low else src[g, :, cols - EXT : cols, :]
                    out[g, at : at + src.shape[1]] = part
                at += src.shape[1]
        return act

    both_ways(info[1], give(first), give(second))


def add_rows(geo, info, sources, heights, got_first, got_second, outs):
    grids, rows = geo["G"], geo["R"]

    def place(low, high):
        at = 0
        for out, h in zip(outs, heights):
            for g in range(grids):
                out[g, 0:h] = low[g, at : at + h]
                out[g, h + rows : 2 * h + rows] = high[g, at : at + h]
            at += h

    whichever(info[0], place, got_first, got_second)
    for src, out, h in zip(sources, outs, heights):
        for g in range(grids):
            out[g, h : h + rows] = src[g]


def add_cols(geo, info, sources, starts, got_first, got_second, outs):
    cols = geo["C"]

    def place(low, high):
        for src, out, at in zip(sources, outs, starts):
            total = src.shape[1]
            for g in range(geo["G"]):
                right = high[g, at : at + total].astype(F32)
                left = low[g, at : at + total].astype(F32)
                out[g, :, cols:, :] = jnp.concatenate([right, left], axis=1).astype(LOW)

    whichever(info[1], place, got_first, got_second)
    for src, out in zip(sources, outs):
        for g in range(geo["G"]):
            out[g, :, 0:cols, :] = src[g]


def field_edge_kernel(geo, info, x, first, second, sem):
    rows = geo["R"]

    def fetch(high_out, low_out):
        copies = [
            pltpu.make_async_copy(x.at[:, rows - EXT : rows], high_out, sem.at[0]),
            pltpu.make_async_copy(x.at[:, 0:EXT], low_out, sem.at[1]),
        ]
        for c in copies:
            c.start()
        for c in copies:
            c.wait()

    @pl.when(info[0] == 1)
    def _():
        fetch(first, second)

    @pl.when(info[0] == 0)
    def _():
        fetch(second, first)


def mask_edge_kernel(geo, info, masks, cot, *outs):
    grids = geo["G"]
    lows, masked = outs[0:4], outs[4]
    for g in range(grids):
        for k in range(4):
            lows[k][g] = masks[k, g].astype(F32).astype(LOW)
        masked[g] = (cot[g].astype(F32) * masks[3, g].astype(F32)).astype(LOW)
    cut_cols(geo, info, lows[0:2], outs[5], outs[6])
    cut_rows(geo, info, [lows[2], masked, cot], geo["heights"][3:], outs[7], outs[8])


def middle_kernel(geo, info, x, x_first, x_second, mask0, mask1, m_first, m_second, *outs):
    x_tall, x_out, wides, m_out = outs[0], outs[1:3], outs[3:5], outs[5:7]
    add_rows(geo, info, [x], [EXT], x_first, x_second, [x_tall])
    cut_cols(geo, info, [x_tall], *x_out)
    add_cols(geo, info, [mask0, mask1], [0, geo["R"]], m_first, m_second, wides)
    cut_rows(geo, info, wides, geo["heights"][1:3], *m_out)


def late_kernel(geo, info, mask2, masked, cot, first, second, before, *outs):
    del before
    add_rows(geo, info, [mask2, masked, cot], geo["heights"][3:], first, second, outs[0:3])
    cut_cols(geo, info, outs[0:3], *outs[3:5])


def gate_kernel(sums, *refs):
    refs[-1][...] = sums[...]


def forward_kernel(layer, geo, *refs):
    grids, rows, devices, width, cols = geo["G"], geo["R"], geo["D"], geo["CE"], geo["C"]
    heights = geo["heights"]
    refs = list(refs)
    info, gains, offsets, biases, kernels = (refs.pop(0) for _ in range(5))
    if layer:
        stats, pre_in = refs.pop(0), refs.pop(0)
    field = refs.pop(0) if layer == 2 else None
    members = geo["members"][layer]
    sources = [refs.pop(0) for _ in members]
    got = [refs.pop(0), refs.pop(0)]
    sums_out = refs.pop(0)
    exts = [refs.pop(0) for _ in members]
    pre_out, low_out = refs.pop(0), refs.pop(0)
    field_out = refs.pop(0) if layer == 2 else None
    taps, weight, acts, acc = refs
    lo, hi = layer + 1, geo["RE"] - 1 - layer

    lay_weights(kernels, layer, False, weight)
    if layer in (0, 3):
        add_cols(geo, info, sources, geo["starts"][layer], *got, exts)
    else:
        skip = 0 if layer == 1 else heights[1]
        place = [r.at[:, skip : skip + heights[layer]] for r in got]
        add_rows(geo, info, sources, [heights[layer]], *place, exts)
    ext = exts[0]
    if layer:
        center, inv = norm_consts(stats, devices)
        scale = inv * gains[layer - 1 : layer, :]
        shift = offsets[layer - 1 : layer, :]
    bias = biases[layer : layer + 1, :]
    number = rows * cols
    totals = [jnp.zeros((8, LANES), F32)] * grids

    def prepare(g, r, slot):
        if layer == 0:
            value = ext[g, pl.ds(r, 2)].astype(F32)
        else:
            p = pre_in[g, pl.ds(r, 2)]
            act = p * sigmoid(p)
            kept = ext[g, pl.ds(r - layer, 2)].astype(F32) * (1.0 / keep_rate)
            value = ((act - center) * scale + shift) * kept
            if layer == 2:
                value = value + field[g, pl.ds(r, 2)].astype(F32)

                def save():
                    field_out[g, pl.ds(r - (EXT - 1), 2)] = value[:, 0:cols, :]

                guard((r >= EXT - 1) & (r < EXT + rows), save)
        store_shifted(taps, slot, r, value, width)

    def convolve(g, at, count, slot):
        for k, part in enumerate(conv_pairs(taps, slot, weight, at, count, width)):
            part = part + bias
            pre_out[g, at + k] = part
            if EXT <= at + k < EXT + rows:
                inner = part[0:cols]
                act = inner * sigmoid(inner)
                acts[slot, at + k - EXT] = act
                totals[g] = totals[g] + fold(act)

    def after(g, slot):
        for s in range(3):
            low_out[s, g] = taps[slot, s, EXT - 1 : EXT + 1 + rows, 0:cols, :]
        mean = to_row(totals[g]) * (1.0 / number)
        square = jnp.zeros((8, LANES), F32)
        first = jnp.zeros((8, LANES), F32)
        second = jnp.zeros((8, LANES), F32)
        for k in range(rows):
            act = acts[slot, k]
            apart = act - mean
            square = square + fold(jnp.square(apart))
            if layer == 3:
                z = exts[1][g, heights[4] + k, 0:cols, :].astype(F32)
                first = first + fold(z)
                second = second + fold(z * apart)
            if layer == 0:
                p = pre_out[g, EXT + k, 0:cols, :]
                s = sigmoid(p)
                slope = s * (1.0 + p * (1.0 - s))
                first = first + fold(slope)
                second = second + fold(slope * act)
        acc[g : g + 1] = mean
        acc[grids + g : grids + g + 1] = to_row(square) * (1.0 / number)
        if layer in (0, 3):
            acc[2 * grids + g : 2 * grids + g + 1] = to_row(first)
            acc[3 * grids + g : 3 * grids + g + 1] = to_row(second)

    pipeline(grids, lo, hi, 5, prepare, convolve, after)
    means = acc[0:grids]
    middle = jnp.mean(means, axis=0, keepdims=True)
    away = means - middle
    spread = jnp.mean(acc[grids : 2 * grids] + jnp.square(away), axis=0, keepdims=True)
    out = [middle, spread]
    if layer == 3:
        ones = acc[2 * grids : 3 * grids]
        out.append(to_row(ones) * (1.0 / keep_rate))
        out.append(to_row(acc[3 * grids : 4 * grids] + away * ones) * (1.0 / keep_rate))
    if layer == 0:
        out += [to_row(acc[2 * grids : 3 * grids]), to_row(acc[3 * grids : 4 * grids])]
    for k, row in enumerate(out):
        sums_out[:, k : k + 1, :] = jnp.broadcast_to(row[None], (devices, 1, LANES))


def back_consts(layer, geo, stats, sums, gains):
    center, inv = norm_consts(stats, geo["D"])
    if layer == 3:
        one, two = top_sums(stats, center, inv)
    else:
        total = jnp.sum(sums[...], axis=0)
        one, two = total[0:1], total[1:2]
    pixels = float(geo["D"] * geo["G"] * geo["R"] * geo["C"])
    return center, inv, inv * gains[layer : layer + 1, :], one * (1.0 / pixels), two * (1.0 / pixels)


def weight_term(geo, low, g, right, acc):
    rows, cols = geo["R"], geo["C"]
    parts = [low[s, g, r : r + rows] for r in range(3) for s in range(3)]
    spread = jnp.concatenate(parts, axis=-1).reshape(rows * cols, 9 * LANES)
    term = lax.dot_general(right, spread, (((0,), (0,)), ((), ())), preferred_element_type=F32)
    if g == 0:
        acc[...] = term
    else:
        acc[...] += term


def split_halves(info, acc, keep_half, send_half):
    half = 9 * LANES // 2

    def give(out):
        def act(upper):
            start = half if upper else 0
            for t in range(9):
                lo, hi = max(t * LANES, start), min((t + 1) * LANES, start + half)
                if lo < hi:
                    block = acc[:, t * LANES : (t + 1) * LANES].T
                    out[lo - start : hi - start] = block[lo - t * LANES : hi - t * LANES]
        return act

    both_ways(info[1], give(keep_half), give(send_half))


def backward_kernel(layer, geo, *refs):
    grids, rows, devices, width, cols = geo["G"], geo["R"], geo["D"], geo["CE"], geo["C"]
    heights = geo["heights"]
    refs = list(refs)
    info, gains, offsets, kernels, stats, sums, pre, low = (refs.pop(0) for _ in range(8))
    masked = keep_top = field = cot = z_in = None
    if layer == 3:
        masked, keep_top, field = refs.pop(0), refs.pop(0), refs.pop(0)
    else:
        z_in = refs.pop(0)
    if layer == 2:
        cot = refs.pop(0)
    keep, stats_below, pre_below = refs.pop(0), refs.pop(0), refs.pop(0)
    sums_out, keep_half, send_half, z_out = (refs.pop(0) for _ in range(4))
    grad_out = refs.pop(0) if layer == 2 else None
    result = refs.pop(0) if layer == 3 else None
    taps, weight, acc = refs
    lo, hi = EXT - layer, EXT + rows + layer
    keep_off = EXT - heights[layer]

    lay_weights(kernels, layer, True, weight)
    center, inv, scale, one, two = back_consts(layer, geo, stats, sums, gains)
    first_row, last_row = info[2], info[3]
    center_b, inv_b = norm_consts(stats_below, devices)
    sums_here = [jnp.zeros((8, LANES), F32)] * 4

    def prepare(g, r, slot):
        p = pre[g, pl.ds(r, 2)]
        s = sigmoid(p)
        normed = (p * s - center) * inv
        if layer == 3:
            z = masked[g, pl.ds(r - (EXT - heights[4]), 2)].astype(F32) * (1.0 / keep_rate)
        else:
            z = z_in[g, pl.ds(r, 2)]
        value = scale * (z - one - normed * two) * (s * (1.0 + p * (1.0 - s)))
        real = [jnp.where((r + k >= first_row) & (r + k < last_row), 1.0, 0.0).astype(F32) for k in range(2)]
        value = jnp.stack([value[0] * real[0], value[1] * real[1]])
        store_shifted(taps, slot, r, value, width)
        if layer == 3:
            def save():
                kept = keep_top[g, pl.ds(r - EXT, 2)].astype(F32) * (1.0 / keep_rate)
                y = (normed[:, 0:cols] * gains[layer : layer + 1, :] + offsets[layer : layer + 1, :]) * kept
                result[g, pl.ds(r - EXT, 2)] = (field[g, pl.ds(r - EXT + 1, 2)] + y).astype(LOW)

            guard((r >= EXT) & (r < EXT + rows), save)

    def convolve(g, at, count, slot):
        for k, part in enumerate(conv_pairs(taps, slot, weight, at, count, width)):
            r = at + k
            inner = EXT <= r < EXT + rows
            if layer == 2:
                part = part + cot[g, r - (EXT - heights[5])].astype(F32)
                if inner:
                    grad_out[g, r - EXT] = part[0:cols]
            z = part * (keep[g, r - keep_off].astype(F32) * (1.0 / keep_rate))
            z_out[g, r] = z
            if inner:
                z = z[0:cols]
                p = pre_below[g, r, 0:cols, :]
                s = sigmoid(p)
                sums_here[0] = sums_here[0] + fold(z)
                sums_here[1] = sums_here[1] + fold(z * (p * s - center_b))
                if layer == 1:
                    sums_here[3] = sums_here[3] + fold(z * (s * (1.0 + p * (1.0 - s))))

    def after(g, slot):
        right = taps[slot, 1, EXT : EXT + rows, 0:cols, :].reshape(rows * cols, LANES)
        sums_here[2] = sums_here[2] + fold(right.astype(F32))
        weight_term(geo, low, g, right, acc)

    pipeline(grids, lo, hi, 5, prepare, convolve, after)
    split_halves(info, acc, keep_half, send_half)
    out = [to_row(v) for v in sums_here]
    out[1] = out[1] * inv_b
    for k in range(4 if layer == 1 else 3):
        sums_out[:, k : k + 1, :] = jnp.broadcast_to(out[k][None], (devices, 1, LANES))


def first_weight_kernel(geo, *refs):
    grids, rows, width, cols = geo["G"], geo["R"], geo["CE"], geo["C"]
    info, gains, stats, sums, pre, low, z_in, sent, keep_half, send_both, dpre, acc = refs
    half = 9 * LANES // 2
    send_both[0:half] = sent[...]
    center, inv, scale, one, two = back_consts(0, geo, stats, sums, gains)
    first_row, last_row = info[2], info[3]

    for g in range(grids):
        for k in range(rows + 2):
            r = EXT - 1 + k
            p = pre[g, r]
            s = sigmoid(p)
            normed = (p * s - center) * inv
            value = scale * (z_in[g, r] - one - normed * two) * (s * (1.0 + p * (1.0 - s)))
            if k in (0, rows + 1):
                value = value * jnp.where((r >= first_row) & (r < last_row), 1.0, 0.0).astype(F32)
            dpre[g, k] = value.astype(LOW)
        weight_term(geo, low, g, dpre[g, 1 : rows + 1, 0:cols, :].reshape(rows * cols, LANES), acc)
    split_halves(info, acc, keep_half, send_both.at[half : 2 * half])


def input_grad_kernel(geo, kernels, dpre, grad, out, taps, weight):
    grids, rows, width, cols = geo["G"], geo["R"], geo["CE"], geo["C"]
    lay_weights(kernels, 0, True, weight)

    def prepare(g, r, slot):
        store_shifted(taps, slot, r, dpre[g, pl.ds(r, 2)].astype(F32), width)

    def convolve(g, at, count, slot):
        for k, part in enumerate(conv_pairs(taps, slot, weight, at, count, cols)):
            out[g, at + k - 1] = grad[g, at + k - 1] + part

    pipeline(grids, 1, rows + 1, 8, prepare, convolve, lambda g, slot: None)


def share_kernel(*refs):
    third, second, both, out = refs[4:]
    half = 9 * LANES // 2
    gots = [both[half : 2 * half], both[0:half], second[...], third[...]]
    for k in range(4):
        out[k * half : (k + 1) * half] = (refs[k][...] + gots[k]).astype(LOW)


def total_kernel(devices, got, out):
    total = jnp.sum(got[...].astype(F32), axis=0)
    out[...] = jnp.broadcast_to(total.astype(LOW)[None], out.shape)


def join_kernel(geo, info, mine, other, out):
    half = 9 * LANES // 2

    def place(low, high):
        for k in range(4):
            out[k, 0:half] = low[k].astype(F32)
            out[k, half:] = high[k].astype(F32)

    @pl.when(info[1] == 1)
    def _():
        place(mine, other)

    @pl.when(info[1] == 0)
    def _():
        place(other, mine)


def rows_kernel(geo, gains, *refs):
    stats, sums = refs[0:4], refs[4:7]
    bias_out, gain_out, offset_out = refs[7:]
    for layer in range(4):
        center, inv = norm_consts(stats[layer], geo["D"])
        if layer == 3:
            one, two = top_sums(stats[3], center, inv)
        else:
            total = jnp.sum(sums[layer][...], axis=0)
            one, two = total[0:1], total[1:2]
        offset_out[layer : layer + 1] = one
        gain_out[layer : layer + 1] = two
        if layer:
            bias_out[layer : layer + 1] = jnp.sum(sums[layer - 1][...], axis=0)[2:3]
        else:
            pixels = float(geo["D"] * geo["G"] * geo["R"] * geo["C"])
            slopes = jnp.sum(stats[0][...], axis=0)
            flat, lifted = slopes[2:3], (slopes[3:4] - center * slopes[2:3]) * inv
            bias_out[0:1] = inv * gains[0:1, :] * (total[3:4] - flat * one / pixels - lifted * two / pixels)


def call(kernel, operands, outs, scratch=(), flops=10**6, moved=10**6, scalars=1, final=(), outside=False):
    space = pl.BlockSpec(memory_space=pltpu.VMEM)
    specs = [pl.BlockSpec(memory_space=pltpu.SMEM)] * scalars
    operands = list(operands)
    for k in range(scalars, len(operands)):
        if outside:
            specs.append(pl.BlockSpec(memory_space=pltpu.HBM))
        else:
            specs.append(space)
            operands[k] = pltpu.with_memory_space_constraint(operands[k], pltpu.VMEM)
    shapes = [jax.ShapeDtypeStruct(s, d) if k in final else pltpu.VMEM(s, d) for k, (s, d) in enumerate(outs)]
    return pl.pallas_call(
        kernel,
        in_specs=specs,
        out_specs=[space] * len(outs),
        out_shape=shapes,
        scratch_shapes=[v if hasattr(v, "shape") and not isinstance(v, tuple) else pltpu.VMEM(*v) for v in scratch],
        compiler_params=pltpu.CompilerParams(vmem_limit_bytes=12 * 2**20),
        cost_estimate=pl.CostEstimate(flops=flops, bytes_accessed=moved, transcendentals=0),
    )(*operands)


def conv_scratch(geo, tall):
    return [((2, 3, tall, geo["CE"], LANES), LOW), ((12 * LANES, 2 * LANES), LOW)]


def forward_call(layer, geo, operands):
    grids, rows, rows_ext, width, devices, cols = geo["G"], geo["R"], geo["RE"], geo["CE"], geo["D"], geo["C"]
    kinds = 4 if layer in (0, 3) else 2
    outs = [((devices, kinds, LANES), F32)]
    for k in geo["members"][layer]:
        outs.append(((grids, rows + 2 * geo["heights"][k], width, LANES), LOW))
    outs.append(((grids, rows_ext, width, LANES), F32))
    outs.append(((3, grids, rows + 2, cols, LANES), LOW))
    if layer == 2:
        outs.append(((grids, rows + 2, cols, LANES), F32))
    scratch = conv_scratch(geo, rows_ext) + [((2, rows, cols, LANES), F32), ((kinds * grids, LANES), F32)]
    return call(functools.partial(forward_kernel, layer, geo), operands, outs, scratch, 2 * 10**9, 8 * 10**6)


def backward_call(layer, geo, operands):
    grids, rows, rows_ext, width, devices, cols = geo["G"], geo["R"], geo["RE"], geo["CE"], geo["D"], geo["C"]
    half = ((9 * LANES // 2, LANES), F32)
    outs = [((devices, 4 if layer == 1 else 3, LANES), F32), half, half, ((grids, rows_ext, width, LANES), F32)]
    if layer == 2:
        outs.append(((grids, rows, cols, LANES), F32))
    if layer == 3:
        outs.append(((grids, rows, cols, LANES), LOW))
    scratch = conv_scratch(geo, rows_ext) + [((LANES, 9 * LANES), F32)]
    return call(
        functools.partial(backward_kernel, layer, geo), operands, outs, scratch, 3 * 10**9, 8 * 10**6,
        final=(4,) if layer == 3 else (),
    )


def local(inputs, kernels, biases, gains, offsets, keep_masks, cotangent):
    grids, rows, cols, _ = inputs.shape
    devices = lax.axis_size("batch") * lax.axis_size("lat") * lax.axis_size("lon")
    heights = [EXT, 7, 6, 5, 4, 2]
    starts = [0]
    for k in (3, 4):
        starts.append(starts[-1] + rows + 2 * heights[k])
    geo = dict(
        G=grids, R=rows, C=cols, D=devices, RE=rows + 2 * EXT, CE=cols + 2 * EXT, heights=heights,
        starts={0: [0], 3: starts}, members=[[0], [1], [2], [3, 4, 5]],
    )
    lat, lon = lax.axis_index("lat"), lax.axis_index("lon")
    info = jnp.stack(
        [
            1 - lax.rem(lat, 2),
            1 - lax.rem(lon, 2),
            jnp.where(lat == 0, EXT, 0),
            jnp.where(lat == lax.axis_size("lat") - 1, EXT + rows, rows + 2 * EXT),
        ]
    ).astype(jnp.int32)
    kernels = kernels.reshape(4, 9, LANES, LANES)

    def block(tall, wide):
        return ((grids, tall, wide, LANES), LOW)

    x_edges = call(
        functools.partial(field_edge_kernel, geo), [info, inputs], [block(EXT, cols)] * 2,
        [pltpu.SemaphoreType.DMA((2,))], outside=True,
    )
    x_got = trade(x_edges, "lat", False)
    late = sum(heights[3:])
    outs = call(
        functools.partial(mask_edge_kernel, geo), [info, keep_masks, cotangent],
        [block(rows, cols)] * 5 + [block(2 * rows, EXT)] * 2 + [block(late, cols)] * 2,
    )
    low_masks, masked = outs[0:4], outs[4]
    soon_got = trade(outs[5:7], "lon", True)
    late_got = trade(outs[7:9], "lat", False)
    outs = call(
        functools.partial(middle_kernel, geo),
        [info, inputs, *x_got, low_masks[0], low_masks[1], *soon_got],
        [block(rows + 2 * EXT, cols)] + [block(rows + 2 * EXT, EXT)] * 2
        + [block(rows, cols + 2 * EXT)] * 2 + [block(heights[1] + heights[2], cols + 2 * EXT)] * 2,
    )
    pieces = [[outs[0], *trade(outs[1:3], "lon", True)]]
    halos = list(trade(outs[5:7], "lat", False))
    pieces += [[outs[3], *halos], [outs[4], *halos]]
    talls = [rows + 2 * h for h in heights[3:]]
    outs = call(
        functools.partial(late_kernel, geo), [info, low_masks[2], masked, cotangent, *late_got, outs[1]],
        [block(t, cols) for t in talls] + [block(sum(talls), EXT)] * 2,
    )
    pieces.append([*outs[0:3], *trade(outs[3:5], "lon", True)])
    halos += pieces[3][3:]

    pres, lows, stats, exts = [None] * 4, [None] * 4, [None] * 4, [None] * 6
    field = None
    for layer in range(4):
        operands = [info, gains, offsets, biases, kernels]
        if layer:
            operands += [stats[layer - 1], pres[layer - 1]]
        if layer == 2:
            operands.append(exts[0])
        outs = list(forward_call(layer, geo, operands + pieces[layer]))
        part = outs.pop(0)
        if layer == 0:
            (part,) = call(gate_kernel, [part] + halos, [(part.shape, F32)], scalars=0)
        stats[layer] = to_all(part)
        for k in geo["members"][layer]:
            exts[k] = outs.pop(0)
        pres[layer], lows[layer] = outs.pop(0), outs.pop(0)
        if layer == 2:
            field = outs.pop(0)

    sums = [None] * 4
    sums[3] = stats[3]
    kept, got = [None] * 4, []
    z = grad = output = None
    for layer in (3, 2, 1):
        operands = [info, gains, offsets, kernels, stats[layer], sums[layer], pres[layer], lows[layer]]
        operands += [exts[4], low_masks[3], field] if layer == 3 else [z]
        if layer == 2:
            operands.append(exts[5])
        operands += [exts[layer], stats[layer - 1], pres[layer - 1]]
        outs = backward_call(layer, geo, operands)
        sums[layer - 1] = to_all(outs[0])
        kept[layer], sent = outs[1], outs[2]
        if layer > 1:
            got.append(to_pair(sent))
        z = outs[3]
        if layer == 2:
            grad = outs[4]
        if layer == 3:
            output = outs[4]
    half = 9 * LANES // 2
    term = ((half, LANES), F32)
    kept[0], sent, dpre = call(
        functools.partial(first_weight_kernel, geo), [info, gains, stats[0], sums[0], pres[0], lows[0], z, sent],
        [term, ((2 * half, LANES), F32), block(rows + 2, cols + 2 * EXT)], [((LANES, 9 * LANES), F32)], 10**9, 8 * 10**6,
    )
    got.append(to_pair(sent))

    (shares,) = call(share_kernel, kept + got, [((4 * half, LANES), LOW)], scalars=0)
    slots = (devices // 2, 4 * half // (devices // 2), LANES)
    arrived = to_half(shares.reshape(slots), devices)
    (mine,) = call(functools.partial(total_kernel, devices), [arrived], [(slots, LOW)], scalars=0)
    mine = to_half(mine, devices).reshape(4, half, LANES)
    (kernel_grad,) = call(
        functools.partial(join_kernel, geo), [info, mine, to_pair(mine)], [((4, 9 * LANES, LANES), F32)], final=(0,)
    )
    (input_grad,) = call(
        functools.partial(input_grad_kernel, geo), [kernels, dpre, grad], [((grids, rows, cols, LANES), F32)],
        conv_scratch(geo, rows + 2), 10**9, 3 * 10**6, scalars=0, final=(0,),
    )
    small = ((4, LANES), F32)
    bias_grad, gain_grad, offset_grad = call(
        functools.partial(rows_kernel, geo), [gains] + stats + sums[:3], [small] * 3, scalars=0, final=(0, 1, 2)
    )
    return (output, input_grad, kernel_grad.reshape(4, 3, 3, LANES, LANES), bias_grad, gain_grad, offset_grad)


def solution(mesh):
    in_specs = (
        P("batch", "lat", "lon", None),
        P(),
        P(),
        P(),
        P(),
        P(None, "batch", "lat", "lon", None),
        P("batch", "lat", "lon", None),
    )
    out_specs = (P("batch", "lat", "lon", None), P("batch", "lat", "lon", None), P(), P(), P(), P())
    return jax.shard_map(local, mesh=mesh, in_specs=in_specs, out_specs=out_specs, check_vma=False)
```

```python
import functools

import jax
import jax.numpy as jnp
from jax import lax
from jax.experimental import pallas as pl
from jax.experimental.pallas import tpu as pltpu
from jax.sharding import PartitionSpec as P

eps = 1e-05
keep_rate = 0.9
EVERY = ("batch", "lat", "lon")
EXT = 8
LANES = 128
F32 = jnp.float32
LOW = jnp.bfloat16


def partners(axis, periodic):
    count = lax.axis_size(axis)
    first = [(i, i ^ 1) for i in range(count)]
    second = []
    for i in range(count):
        j = i + 1 if i % 2 else i - 1
        if periodic:
            second.append((i, j % count))
        elif 0 <= j < count:
            second.append((i, j))
    return first, second


def trade(pair, axis, periodic):
    first, second = partners(axis, periodic)
    return lax.ppermute(pair[0], axis, first), lax.ppermute(pair[1], axis, second)


def to_all(rows):
    return lax.all_to_all(rows, EVERY, 0, 0)


def to_half(rows, devices):
    groups = [[i for i in range(devices) if i % 2 == side] for side in range(2)]
    return lax.all_to_all(rows, EVERY, 0, 0, axis_index_groups=groups)


def to_pair(block):
    return lax.ppermute(block, "lon", partners("lon", True)[0])


def sigmoid(v):
    return 0.5 * jnp.tanh(0.5 * v) + 0.5


def silu(v):
    half = 0.5 * v
    return half + half * jnp.tanh(half)


def norm_consts(stats_ref, devices):
    stats = stats_ref[...]
    total = jnp.sum(stats, axis=0)
    center = total[0:1] * (1.0 / devices)
    apart = jnp.sum(jnp.square(stats - center[None]), axis=0)
    spread = (total[1:2] + apart[0:1]) * (1.0 / devices)
    return center, lax.rsqrt(spread + eps)


def top_sums(stats_ref, center, inv):
    stats = stats_ref[...]
    total = jnp.sum(stats, axis=0)
    apart = stats[:, 0:1, :] - center[None]
    return total[2:3], (total[3:4] + jnp.sum(apart * stats[:, 2:3, :], axis=0)) * inv


def shifted(value, width):
    return pltpu.roll(value, 1, 1), value, pltpu.roll(value, width - 1, 1)


def store_shifted(taps, slot, row, value, width):
    for s, part in enumerate(shifted(value, width)):
        taps[slot, s, pl.ds(row, 2)] = part.astype(LOW)


def lay_weights(kernel_ref, layer, back, out):
    blank = jnp.zeros((3 * LANES, LANES), LOW)
    out[9 * LANES : 12 * LANES, 0:LANES] = blank
    out[0 : 3 * LANES, LANES : 2 * LANES] = blank
    for r in range(3):
        for s in range(3):
            if back:
                block = kernel_ref[layer, (2 - r) * 3 + 2 - s].astype(F32).T.astype(LOW)
            else:
                block = kernel_ref[layer, r * 3 + s]
            at = (r * 3 + s) * LANES
            out[at : at + LANES, 0:LANES] = block
            out[at + 3 * LANES : at + 4 * LANES, LANES : 2 * LANES] = block


def conv_pairs(taps, slot, weight_ref, row, pairs, cols):
    parts = []
    for t in range(4):
        for s in range(3):
            parts.append(jnp.stack([taps[slot, s, row - 1 + t + 2 * k, 0:cols, :] for k in range(pairs)]))
    left = jnp.concatenate(parts, axis=-1).reshape(pairs * cols, 12 * LANES)
    both = jnp.dot(left, weight_ref[...], preferred_element_type=F32)
    out = []
    for k in range(pairs):
        for h in range(2):
            out.append(both[k * cols : (k + 1) * cols, h * LANES : (h + 1) * LANES])
    return out


def chunks(lo, hi, pairs):
    at = lo
    while at < hi:
        count = min(pairs, (hi - at) // 2)
        yield at, count
        at += 2 * count


def pipeline(grids, lo, hi, pairs, prepare, convolve, after):
    count = (hi - lo) // 2 + 1
    for i in range(count):
        prepare(0, lo - 1 + 2 * i, 0)
    parts = list(chunks(lo, hi, pairs))
    for g in range(grids):
        for j, (at, size) in enumerate(parts):
            if g + 1 < grids:
                for i in range(count * j // len(parts), count * (j + 1) // len(parts)):
                    prepare(g + 1, lo - 1 + 2 * i, (g + 1) % 2)
            convolve(g, at, size, g % 2)
        after(g, g % 2)


def guard(condition, act):
    if isinstance(condition, bool):
        if condition:
            act()
    else:
        pl.when(condition)(act)


def fold(value):
    return jnp.sum(value.reshape(-1, 8, LANES), axis=0)


def to_row(value):
    return jnp.sum(value, axis=0, keepdims=True)


def both_ways(even, give_first, give_second):
    @pl.when(even == 1)
    def _():
        give_first(False)
        give_second(True)

    @pl.when(even == 0)
    def _():
        give_first(True)
        give_second(False)


def whichever(even, place, got_first, got_second):
    @pl.when(even == 1)
    def _():
        place(got_second, got_first)

    @pl.when(even == 0)
    def _():
        place(got_first, got_second)


def cut_rows(geo, info, sources, heights, first, second):
    grids, rows = geo["G"], geo["R"]

    def give(out):
        def act(low):
            at = 0
            for src, h in zip(sources, heights):
                for g in range(grids):
                    out[g, at : at + h] = src[g, 0:h] if low else src[g, src.shape[1] - h :]
                at += h
        return act

    both_ways(info[0], give(first), give(second))


def cut_cols(geo, info, sources, first, second):
    grids, cols = geo["G"], geo["C"]

    def give(out):
        def act(low):
            at = 0
            for src in sources:
                for g in range(grids):
                    part = src[g, :, 0:EXT, :] if low else src[g, :, cols - EXT : cols, :]
                    out[g, at : at + src.shape[1]] = part
                at += src.shape[1]
        return act

    both_ways(info[1], give(first), give(second))


def add_rows(geo, info, sources, heights, got_first, got_second, outs):
    grids, rows = geo["G"], geo["R"]

    def place(low, high):
        at = 0
        for out, h in zip(outs, heights):
            for g in range(grids):
                out[g, 0:h] = low[g, at : at + h]
                out[g, h + rows : 2 * h + rows] = high[g, at : at + h]
            at += h

    whichever(info[0], place, got_first, got_second)
    for src, out, h in zip(sources, outs, heights):
        for g in range(grids):
            out[g, h : h + rows] = src[g]


def add_cols(geo, info, sources, starts, got_first, got_second, outs):
    cols = geo["C"]

    def place(low, high):
        for src, out, at in zip(sources, outs, starts):
            total = src.shape[1]
            for g in range(geo["G"]):
                right = high[g, at : at + total].astype(F32)
                left = low[g, at : at + total].astype(F32)
                out[g, :, cols:, :] = jnp.concatenate([right, left], axis=1).astype(LOW)

    whichever(info[1], place, got_first, got_second)
    for src, out in zip(sources, outs):
        for g in range(geo["G"]):
            out[g, :, 0:cols, :] = src[g]


def field_edge_kernel(geo, info, x, first, second, sems):
    rows = geo["R"]

    def fetch(high_out, low_out):
        copies = [
            pltpu.make_async_copy(x.at[:, rows - EXT : rows], high_out, sems.at[0]),
            pltpu.make_async_copy(x.at[:, 0:EXT], low_out, sems.at[1]),
        ]
        for c in copies:
            c.start()
        for c in copies:
            c.wait()

    @pl.when(info[0] == 1)
    def _():
        fetch(first, second)

    @pl.when(info[0] == 0)
    def _():
        fetch(second, first)


def mask_edge_kernel(geo, info, masks, first, second, near, sems):
    rows, height = geo["R"], geo["heights"][1]
    nears = [
        pltpu.make_async_copy(masks.at[0, :, 0:height], near.at[0], sems.at[0]),
        pltpu.make_async_copy(masks.at[0, :, rows - height : rows], near.at[1], sems.at[1]),
    ]
    for c in nears:
        c.start()
    for c in nears:
        c.wait()

    def give(out):
        def act(low):
            out[...] = near[0 if low else 1].astype(F32).astype(LOW)
        return act

    both_ways(info[0], give(first), give(second))


def tall_kernel(geo, heights, info, *refs):
    n = len(heights)
    talls = refs[n + 2 : 2 * n + 2]
    add_rows(geo, info, refs[:n], heights, refs[n], refs[n + 1], talls)
    cut_cols(geo, info, talls, refs[2 * n + 2], refs[2 * n + 3])


def mask_kernel(geo, masks, cot, *outs):
    for g in range(geo["G"]):
        for k in range(4):
            outs[k][g] = masks[k, g].astype(F32).astype(LOW)
        outs[4][g] = (cot[g].astype(F32) * masks[3, g].astype(F32)).astype(LOW)


def cut_kernel(geo, info, mask1, mask2, masked, cot, before, first, second):
    del before
    cut_rows(geo, info, [mask1, mask2, masked, cot], geo["heights"][2:], first, second)


def late_kernel(geo, info, mask1, mask2, masked, cot, first, second, before, *outs):
    del before
    add_rows(geo, info, [mask1, mask2, masked, cot], geo["heights"][2:], first, second, outs[0:4])
    cut_cols(geo, info, outs[0:1], *outs[4:6])


def last_kernel(geo, info, tall2, tall3, tall4, before, first, second):
    del before
    cut_cols(geo, info, [tall2, tall3, tall4], first, second)


def gate_kernel(sums, first, second, out):
    del first, second
    out[...] = sums[...]


def forward_kernel(layer, geo, *refs):
    grids, rows, devices, width, cols = geo["G"], geo["R"], geo["D"], geo["CE"], geo["C"]
    heights = geo["heights"]
    refs = list(refs)
    info, gains, offsets, biases, kernels = (refs.pop(0) for _ in range(5))
    if layer:
        stats, pre_in = refs.pop(0), refs.pop(0)
    field = refs.pop(0) if layer == 2 else None
    members = geo["members"][layer]
    sources = [refs.pop(0) for _ in members]
    got = [refs.pop(0), refs.pop(0)]
    if layer in (1, 2):
        refs.pop(0)
    sums_out = refs.pop(0)
    exts = [refs.pop(0) for _ in members]
    pre_out, low_out = refs.pop(0), refs.pop(0)
    field_out = refs.pop(0) if layer == 2 else None
    taps, weight, acts, acc = refs
    lo, hi = layer + 1, geo["RE"] - 1 - layer

    lay_weights(kernels, layer, False, weight)
    add_cols(geo, info, sources, geo["starts"][layer], *got, exts)
    ext = exts[0]
    if layer:
        center, inv = norm_consts(stats, devices)
        scale = inv * gains[layer - 1 : layer, :] * (1.0 / keep_rate)
        shift = offsets[layer - 1 : layer, :] * (1.0 / keep_rate) - center * scale
        scale = 0.5 * scale
    bias = biases[layer : layer + 1, :]
    number = rows * cols
    totals = [jnp.zeros((8, LANES), F32)] * grids

    def prepare(g, r, slot):
        if layer == 0:
            value = ext[g, pl.ds(r, 2)].astype(F32)
        else:
            p = pre_in[g, pl.ds(r, 2)]
            part = p * scale
            value = (part + part * jnp.tanh(0.5 * p) + shift) * ext[g, pl.ds(r - layer, 2)].astype(F32)
            if layer == 2:
                value = value + field[g, pl.ds(r, 2)].astype(F32)

                def save():
                    field_out[g, pl.ds(r - (EXT - 1), 2)] = value[:, 0:cols, :]

                guard((r >= EXT - 1) & (r < EXT + rows), save)
        store_shifted(taps, slot, r, value, width)

    def convolve(g, at, count, slot):
        for k, part in enumerate(conv_pairs(taps, slot, weight, at, count, width)):
            part = part + bias
            pre_out[g, at + k] = part
            if EXT <= at + k < EXT + rows:
                act = silu(part[0:cols])
                acts[slot, at + k - EXT] = act
                totals[g] = totals[g] + fold(act)

    def after(g, slot):
        for s in range(3):
            low_out[s, g] = taps[slot, s, EXT - 1 : EXT + 1 + rows, 0:cols, :]
        mean = to_row(totals[g]) * (1.0 / number)
        square = jnp.zeros((8, LANES), F32)
        first = jnp.zeros((8, LANES), F32)
        second = jnp.zeros((8, LANES), F32)
        for k in range(rows):
            act = acts[slot, k]
            apart = act - mean
            square = square + fold(jnp.square(apart))
            if layer == 3:
                z = exts[1][g, heights[4] + k, 0:cols, :].astype(F32)
                first = first + fold(z)
                second = second + fold(z * apart)
            if layer == 0:
                p = pre_out[g, EXT + k, 0:cols, :]
                s = sigmoid(p)
                slope = s + act * (1.0 - s)
                first = first + fold(slope)
                second = second + fold(slope * act)
        acc[g : g + 1] = mean
        acc[grids + g : grids + g + 1] = to_row(square) * (1.0 / number)
        if layer in (0, 3):
            acc[2 * grids + g : 2 * grids + g + 1] = to_row(first)
            acc[3 * grids + g : 3 * grids + g + 1] = to_row(second)

    pipeline(grids, lo, hi, 5, prepare, convolve, after)
    means = acc[0:grids]
    middle = jnp.mean(means, axis=0, keepdims=True)
    away = means - middle
    spread = jnp.mean(acc[grids : 2 * grids] + jnp.square(away), axis=0, keepdims=True)
    out = [middle, spread]
    if layer == 3:
        ones = acc[2 * grids : 3 * grids]
        out.append(to_row(ones) * (1.0 / keep_rate))
        out.append(to_row(acc[3 * grids : 4 * grids] + away * ones) * (1.0 / keep_rate))
    if layer == 0:
        out += [to_row(acc[2 * grids : 3 * grids]), to_row(acc[3 * grids : 4 * grids])]
    for k, row in enumerate(out):
        sums_out[:, k : k + 1, :] = jnp.broadcast_to(row[None], (devices, 1, LANES))


def back_consts(layer, geo, stats, sums, gains):
    center, inv = norm_consts(stats, geo["D"])
    if layer == 3:
        one, two = top_sums(stats, center, inv)
    else:
        total = jnp.sum(sums[...], axis=0)
        one, two = total[0:1], total[1:2]
    pixels = float(geo["D"] * geo["G"] * geo["R"] * geo["C"])
    scale = inv * gains[layer : layer + 1, :]
    tilt = scale * inv * two * (-1.0 / pixels)
    flat = scale * one * (-1.0 / pixels) - center * tilt
    return center, inv, scale * (1.0 / keep_rate), flat, tilt


def through(p, dn, scale, flat, tilt):
    s = sigmoid(p)
    act = p * s
    return (dn * scale + act * tilt + flat) * (s + act * (1.0 - s)), act


def weight_term(geo, low, g, right, acc):
    rows, cols = geo["R"], geo["C"]
    parts = [low[s, g, r : r + rows] for r in range(3) for s in range(3)]
    spread = jnp.concatenate(parts, axis=-1).reshape(rows * cols, 9 * LANES)
    term = lax.dot_general(right, spread, (((0,), (0,)), ((), ())), preferred_element_type=F32)
    if g == 0:
        acc[...] = term
    else:
        acc[...] += term


def split_halves(info, acc, keep_half, send_half):
    half = 9 * LANES // 2

    def give(out):
        def act(upper):
            start = half if upper else 0
            for t in range(9):
                lo, hi = max(t * LANES, start), min((t + 1) * LANES, start + half)
                if lo < hi:
                    block = acc[:, t * LANES : (t + 1) * LANES].T
                    out[lo - start : hi - start] = block[lo - t * LANES : hi - t * LANES]
        return act

    both_ways(info[1], give(keep_half), give(send_half))


def backward_kernel(layer, geo, *refs):
    grids, rows, devices, width, cols = geo["G"], geo["R"], geo["D"], geo["CE"], geo["C"]
    heights = geo["heights"]
    refs = list(refs)
    info, gains, offsets, kernels, stats, sums, pre, low = (refs.pop(0) for _ in range(8))
    masked = keep_top = field = cot = z_in = None
    if layer == 3:
        masked, keep_top, field = refs.pop(0), refs.pop(0), refs.pop(0)
    else:
        z_in = refs.pop(0)
    if layer == 2:
        cot = refs.pop(0)
    keep, stats_below, pre_below = refs.pop(0), refs.pop(0), refs.pop(0)
    sums_out, keep_half, send_half, z_out = (refs.pop(0) for _ in range(4))
    grad_out = refs.pop(0) if layer == 2 else None
    result = refs.pop(0) if layer == 3 else None
    taps, weight, acc = refs[:3]
    if layer == 3:
        result_out, (result, sems) = result, refs[3:]
        leaving = [pltpu.make_async_copy(result.at[g], result_out.at[g], sems.at[g]) for g in range(grids)]
    lo, hi = EXT - layer, EXT + rows + layer
    keep_off = EXT - heights[layer]

    lay_weights(kernels, layer, True, weight)
    center, inv, scale, flat, tilt = back_consts(layer, geo, stats, sums, gains)
    first_row, last_row = info[2], info[3]
    center_b, inv_b = norm_consts(stats_below, devices)
    sums_here = [jnp.zeros((8, LANES), F32)] * 4

    if layer == 3:
        lift = inv * gains[layer : layer + 1, :] * (1.0 / keep_rate)
        base = offsets[layer : layer + 1, :] * (1.0 / keep_rate) - center * lift

    def prepare(g, r, slot):
        if layer == 3:
            z = masked[g, pl.ds(r - (EXT - heights[4]), 2)].astype(F32)
        else:
            z = z_in[g, pl.ds(r, 2)]
        value, act = through(pre[g, pl.ds(r, 2)], z, scale, flat, tilt)
        if not (isinstance(r, int) and EXT <= r and r + 2 <= EXT + rows):
            real = [jnp.where((r + k >= first_row) & (r + k < last_row), 1.0, 0.0).astype(F32) for k in range(2)]
            value = jnp.stack([value[0] * real[0], value[1] * real[1]])
        store_shifted(taps, slot, r, value, width)
        if layer == 3:
            def save():
                y = (act[:, 0:cols] * lift + base) * keep_top[g, pl.ds(r - EXT, 2)].astype(F32)
                result[g, pl.ds(r - EXT, 2)] = (field[g, pl.ds(r - EXT + 1, 2)] + y).astype(LOW)

            guard((r >= EXT) & (r < EXT + rows), save)

    def convolve(g, at, count, slot):
        for k, part in enumerate(conv_pairs(taps, slot, weight, at, count, width)):
            r = at + k
            inner = EXT <= r < EXT + rows
            if layer == 2:
                part = part + cot[g, r - (EXT - heights[5])].astype(F32)
                if inner:
                    grad_out[g, r - EXT] = part[0:cols]
            z = part * keep[g, r - keep_off].astype(F32)
            z_out[g, r] = z
            if inner:
                z = z[0:cols]
                p = pre_below[g, r, 0:cols, :]
                s = sigmoid(p)
                sums_here[0] = sums_here[0] + fold(z)
                act = p * s
                sums_here[1] = sums_here[1] + fold(z * (act - center_b))
                if layer == 1:
                    sums_here[3] = sums_here[3] + fold(z * (s + act * (1.0 - s)))

    def after(g, slot):
        if layer == 3:
            leaving[g].start()
        right = taps[slot, 1, EXT : EXT + rows, 0:cols, :].reshape(rows * cols, LANES)
        sums_here[2] = sums_here[2] + fold(right.astype(F32))
        weight_term(geo, low, g, right, acc)

    pipeline(grids, lo, hi, 5, prepare, convolve, after)
    split_halves(info, acc, keep_half, send_half)
    out = [to_row(v) for v in sums_here]
    out[0] = out[0] * (1.0 / keep_rate)
    out[1] = out[1] * inv_b * (1.0 / keep_rate)
    out[3] = out[3] * (1.0 / keep_rate)
    for k in range(4 if layer == 1 else 3):
        sums_out[:, k : k + 1, :] = jnp.broadcast_to(out[k][None], (devices, 1, LANES))
    if layer == 3:
        for c in leaving:
            c.wait()


def first_weight_kernel(geo, *refs):
    grids, rows, width, cols = geo["G"], geo["R"], geo["CE"], geo["C"]
    info, gains, stats, sums, pre, low, z_in, sent, keep_half, send_both, dpre, acc = refs
    half = 9 * LANES // 2
    send_both[0:half] = sent[...]
    scale, flat, tilt = back_consts(0, geo, stats, sums, gains)[2:]
    first_row, last_row = info[2], info[3]

    for g in range(grids):
        for k in range(rows + 2):
            r = EXT - 1 + k
            value, _ = through(pre[g, r], z_in[g, r], scale, flat, tilt)
            if k in (0, rows + 1):
                value = value * jnp.where((r >= first_row) & (r < last_row), 1.0, 0.0).astype(F32)
            dpre[g, k] = value.astype(LOW)
        weight_term(geo, low, g, dpre[g, 1 : rows + 1, 0:cols, :].reshape(rows * cols, LANES), acc)
    split_halves(info, acc, keep_half, send_both.at[half : 2 * half])


def input_grad_kernel(geo, kernels, dpre, grad, gains, *refs):
    grids, rows, width, cols = geo["G"], geo["R"], geo["CE"], geo["C"]
    out, taps, weight, buffer, sems = refs[7], *refs[11:]
    leaving = [pltpu.make_async_copy(buffer.at[g], out.at[g], sems.at[g]) for g in range(grids)]
    lay_weights(kernels, 0, True, weight)

    def prepare(g, r, slot):
        store_shifted(taps, slot, r, dpre[g, pl.ds(r, 2)].astype(F32), width)

    def convolve(g, at, count, slot):
        for k, part in enumerate(conv_pairs(taps, slot, weight, at, count, cols)):
            buffer[g, at + k - 1] = grad[g, at + k - 1] + part

    pipeline(grids, 1, rows + 1, 8, prepare, convolve, lambda g, slot: leaving[g].start())
    gather_rows(geo, gains, *refs[0:7], *refs[8:11])
    for c in leaving:
        c.wait()


def share_kernel(*refs):
    third, second, both, out = refs[4:]
    half = 9 * LANES // 2
    gots = [both[half : 2 * half], both[0:half], second[...], third[...]]
    for k in range(4):
        out[k * half : (k + 1) * half] = (refs[k][...] + gots[k]).astype(LOW)


def total_kernel(devices, got, out):
    total = jnp.sum(got[...].astype(F32), axis=0)
    out[...] = jnp.broadcast_to(total.astype(LOW)[None], out.shape)


def join_kernel(geo, info, mine, other, out, buffer, sems):
    half = 9 * LANES // 2
    leaving = [pltpu.make_async_copy(buffer.at[k], out.at[k], sems.at[k]) for k in range(4)]

    def place(low, high):
        for k in range(4):
            buffer[k, 0:half] = low[k].astype(F32)
            buffer[k, half:] = high[k].astype(F32)
            leaving[k].start()

    @pl.when(info[1] == 1)
    def _():
        place(mine, other)

    @pl.when(info[1] == 0)
    def _():
        place(other, mine)

    for c in leaving:
        c.wait()


def gather_rows(geo, gains, *refs):
    stats, sums = refs[0:4], refs[4:7]
    bias_out, gain_out, offset_out = refs[7:]
    for layer in range(4):
        center, inv = norm_consts(stats[layer], geo["D"])
        if layer == 3:
            one, two = top_sums(stats[3], center, inv)
        else:
            total = jnp.sum(sums[layer][...], axis=0)
            one, two = total[0:1], total[1:2]
        offset_out[layer : layer + 1] = one
        gain_out[layer : layer + 1] = two
        if layer:
            bias_out[layer : layer + 1] = jnp.sum(sums[layer - 1][...], axis=0)[2:3]
        else:
            pixels = float(geo["D"] * geo["G"] * geo["R"] * geo["C"])
            slopes = jnp.sum(stats[0][...], axis=0)
            flat, lifted = slopes[2:3], (slopes[3:4] - center * slopes[2:3]) * inv
            bias_out[0:1] = inv * gains[0:1, :] * (total[3:4] - flat * one / pixels - lifted * two / pixels)


def call(kernel, operands, outs, scratch=(), flops=10**6, moved=10**6, scalars=1, final=(), small=(), outside=False):
    space = pl.BlockSpec(memory_space=pltpu.VMEM)
    specs = [pl.BlockSpec(memory_space=pltpu.SMEM)] * scalars
    operands = list(operands)
    for k in range(scalars, len(operands)):
        if outside:
            specs.append(pl.BlockSpec(memory_space=pltpu.HBM))
            operands[k] = pltpu.with_memory_space_constraint(operands[k], pltpu.HBM)
        else:
            specs.append(space)
            operands[k] = pltpu.with_memory_space_constraint(operands[k], pltpu.VMEM)
    plain = set(final) | set(small)
    shapes = [jax.ShapeDtypeStruct(s, d) if k in plain else pltpu.VMEM(s, d) for k, (s, d) in enumerate(outs)]
    places = [pl.BlockSpec(memory_space=pltpu.HBM) if k in final else space for k in range(len(outs))]
    return pl.pallas_call(
        kernel,
        in_specs=specs,
        out_specs=places,
        out_shape=shapes,
        scratch_shapes=[v if hasattr(v, "shape") and not isinstance(v, tuple) else pltpu.VMEM(*v) for v in scratch],
        compiler_params=pltpu.CompilerParams(vmem_limit_bytes=12 * 2**20),
        cost_estimate=pl.CostEstimate(flops=flops, bytes_accessed=moved, transcendentals=0),
    )(*operands)


def conv_scratch(geo, tall):
    return [((2, 3, tall, geo["CE"], LANES), LOW), ((12 * LANES, 2 * LANES), LOW)]


def forward_call(layer, geo, operands):
    grids, rows, rows_ext, width, devices, cols = geo["G"], geo["R"], geo["RE"], geo["CE"], geo["D"], geo["C"]
    kinds = 4 if layer in (0, 3) else 2
    outs = [((devices, kinds, LANES), F32)]
    for k in geo["members"][layer]:
        outs.append(((grids, rows + 2 * geo["heights"][k], width, LANES), LOW))
    outs.append(((grids, rows_ext, width, LANES), F32))
    outs.append(((3, grids, rows + 2, cols, LANES), LOW))
    if layer == 2:
        outs.append(((grids, rows + 2, cols, LANES), F32))
    scratch = conv_scratch(geo, rows_ext) + [((2, rows, cols, LANES), F32), ((kinds * grids, LANES), F32)]
    return call(functools.partial(forward_kernel, layer, geo), operands, outs, scratch, 2 * 10**9, 8 * 10**6)


def backward_call(layer, geo, operands):
    grids, rows, rows_ext, width, devices, cols = geo["G"], geo["R"], geo["RE"], geo["CE"], geo["D"], geo["C"]
    half = ((9 * LANES // 2, LANES), F32)
    outs = [((devices, 4 if layer == 1 else 3, LANES), F32), half, half, ((grids, rows_ext, width, LANES), F32)]
    if layer == 2:
        outs.append(((grids, rows, cols, LANES), F32))
    if layer == 3:
        outs.append(((grids, rows, cols, LANES), LOW))
    scratch = conv_scratch(geo, rows_ext) + [((LANES, 9 * LANES), F32)]
    if layer == 3:
        scratch += [((grids, rows, cols, LANES), LOW), pltpu.SemaphoreType.DMA((grids,))]
    return call(
        functools.partial(backward_kernel, layer, geo), operands, outs, scratch, 3 * 10**9, 8 * 10**6,
        final=(4,) if layer == 3 else (),
    )


def local(inputs, kernels, biases, gains, offsets, keep_masks, cotangent):
    grids, rows, cols, _ = inputs.shape
    devices = lax.axis_size("batch") * lax.axis_size("lat") * lax.axis_size("lon")
    heights = [EXT, 7, 6, 5, 4, 2]
    starts = [0]
    for k in (3, 4):
        starts.append(starts[-1] + rows + 2 * heights[k])
    geo = dict(
        G=grids, R=rows, C=cols, D=devices, RE=rows + 2 * EXT, CE=cols + 2 * EXT, heights=heights,
        starts=[[0], [0], [0], starts], members=[[0], [1], [2], [3, 4, 5]],
    )
    lat, lon = lax.axis_index("lat"), lax.axis_index("lon")
    info = jnp.stack(
        [
            1 - lax.rem(lat, 2),
            1 - lax.rem(lon, 2),
            jnp.where(lat == 0, EXT, 0),
            jnp.where(lat == lax.axis_size("lat") - 1, EXT + rows, rows + 2 * EXT),
        ]
    ).astype(jnp.int32)
    kernels = kernels.reshape(4, 9, LANES, LANES)

    def block(tall, wide):
        return ((grids, tall, wide, LANES), LOW)

    x_height, soon, late = heights[0], heights[1], sum(heights[2:])
    pair_sems = pltpu.SemaphoreType.DMA((2,))
    outs = call(
        functools.partial(field_edge_kernel, geo), [info, inputs], [block(x_height, cols)] * 2, [pair_sems], outside=True
    )
    x_got = trade(outs, "lat", False)
    outs = call(
        functools.partial(mask_edge_kernel, geo), [info, keep_masks], [block(soon, cols)] * 2,
        [((2, grids, soon, cols, LANES), jnp.int32), pair_sems], outside=True,
    )
    soon_got = trade(outs, "lat", False)
    outs = call(
        functools.partial(tall_kernel, geo, heights[:1]), [info, inputs, *x_got],
        [block(rows + 2 * x_height, cols)] + [block(rows + 2 * x_height, EXT)] * 2,
    )
    pieces = [[outs[0], *trade(outs[1:3], "lon", True)]]
    outs = call(functools.partial(mask_kernel, geo), [keep_masks, cotangent], [block(rows, cols)] * 5, scalars=0)
    low_masks, masked = list(outs[0:4]), outs[4]
    outs = call(
        functools.partial(tall_kernel, geo, heights[1:2]), [info, low_masks[0], *soon_got],
        [block(rows + 2 * soon, cols)] + [block(rows + 2 * soon, EXT)] * 2,
    )
    pieces.append([outs[0], *trade(outs[1:3], "lon", True)])
    edges = call(
        functools.partial(cut_kernel, geo), [info, low_masks[1], low_masks[2], masked, cotangent, outs[1]],
        [block(late, cols)] * 2,
    )
    late_got = trade(edges, "lat", False)
    talls = [rows + 2 * h for h in heights[2:]]

    pres, lows, stats, exts = [None] * 4, [None] * 4, [None] * 4, [None] * 6
    field = order = None
    for layer in range(4):
        operands = [info, gains, offsets, biases, kernels]
        if layer:
            operands += [stats[layer - 1], pres[layer - 1]]
        if layer == 2:
            operands.append(exts[0])
        operands += pieces[layer]
        if layer in (1, 2):
            operands.append(order)
        outs = list(forward_call(layer, geo, operands))
        part = outs.pop(0)
        if layer < 2:
            (part,) = call(gate_kernel, [part] + pieces[layer + 1][1:], [(part.shape, F32)], scalars=0)
        stats[layer] = to_all(part)
        if layer == 0:
            ends = call(
                functools.partial(late_kernel, geo), [info] + low_masks[1:3] + [masked, cotangent, *late_got, stats[0]],
                [block(t, cols) for t in talls] + [block(talls[0], EXT)] * 2,
            )
            pieces.append([ends[0], *trade(ends[4:6], "lon", True)])
            order = ends[4]
        if layer == 1:
            edges = call(
                functools.partial(last_kernel, geo), [info, *ends[1:4], stats[1]], [block(sum(talls[1:]), EXT)] * 2
            )
            pieces.append([*ends[1:4], *trade(edges, "lon", True)])
            order = edges[0]
        for k in geo["members"][layer]:
            exts[k] = outs.pop(0)
        pres[layer], lows[layer] = outs.pop(0), outs.pop(0)
        if layer == 2:
            field = outs.pop(0)

    sums = [None] * 4
    sums[3] = stats[3]
    kept, got = [None] * 4, []
    z = grad = output = None
    for layer in (3, 2, 1):
        operands = [info, gains, offsets, kernels, stats[layer], sums[layer], pres[layer], lows[layer]]
        operands += [exts[4], low_masks[3], field] if layer == 3 else [z]
        if layer == 2:
            operands.append(exts[5])
        operands += [exts[layer], stats[layer - 1], pres[layer - 1]]
        outs = backward_call(layer, geo, operands)
        sums[layer - 1] = to_all(outs[0])
        kept[layer], sent = outs[1], outs[2]
        if layer > 1:
            got.append(to_pair(sent))
        z = outs[3]
        if layer == 2:
            grad = outs[4]
        if layer == 3:
            output = outs[4]
    half = 9 * LANES // 2
    term = ((half, LANES), F32)
    kept[0], sent, dpre = call(
        functools.partial(first_weight_kernel, geo), [info, gains, stats[0], sums[0], pres[0], lows[0], z, sent],
        [term, ((2 * half, LANES), F32), block(rows + 2, cols + 2 * EXT)], [((LANES, 9 * LANES), F32)], 10**9, 8 * 10**6,
    )
    got.append(to_pair(sent))

    (shares,) = call(share_kernel, kept + got, [((4 * half, LANES), LOW)], scalars=0)
    slots = (devices // 2, 4 * half // (devices // 2), LANES)
    arrived = to_half(shares.reshape(slots), devices)
    (mine,) = call(functools.partial(total_kernel, devices), [arrived], [(slots, LOW)], scalars=0)
    mine = to_half(mine, devices).reshape(4, half, LANES)
    (kernel_grad,) = call(
        functools.partial(join_kernel, geo), [info, mine, to_pair(mine)], [((4, 9 * LANES, LANES), F32)],
        [((4, 9 * LANES, LANES), F32), pltpu.SemaphoreType.DMA((4,))], final=(0,),
    )
    small = ((4, LANES), F32)
    field_like = ((grids, rows, cols, LANES), F32)
    input_grad, bias_grad, gain_grad, offset_grad = call(
        functools.partial(input_grad_kernel, geo), [kernels, dpre, grad, gains] + stats + sums[:3],
        [field_like] + [small] * 3, conv_scratch(geo, rows + 2) + [field_like, pltpu.SemaphoreType.DMA((grids,))],
        10**9, 3 * 10**6, scalars=0, final=(0,), small=(1, 2, 3),
    )
    return (output, input_grad, kernel_grad.reshape(4, 3, 3, LANES, LANES), bias_grad, gain_grad, offset_grad)


def solution(mesh):
    in_specs = (
        P("batch", "lat", "lon", None),
        P(),
        P(),
        P(),
        P(),
        P(None, "batch", "lat", "lon", None),
        P("batch", "lat", "lon", None),
    )
    out_specs = (P("batch", "lat", "lon", None), P("batch", "lat", "lon", None), P(), P(), P(), P())
    return jax.shard_map(local, mesh=mesh, in_specs=in_specs, out_specs=out_specs, check_vma=False)
```

```python
import functools

import jax
import jax.numpy as jnp
from jax import lax
from jax.experimental import pallas as pl
from jax.experimental.pallas import tpu as pltpu
from jax.sharding import PartitionSpec as P

eps = 1e-05
keep_rate = 0.9
EVERY = ("batch", "lat", "lon")
EXT = 8
LANES = 128
F32 = jnp.float32
LOW = jnp.bfloat16


def partners(axis, periodic):
    count = lax.axis_size(axis)
    first = [(i, i ^ 1) for i in range(count)]
    second = []
    for i in range(count):
        j = i + 1 if i % 2 else i - 1
        if periodic:
            second.append((i, j % count))
        elif 0 <= j < count:
            second.append((i, j))
    return first, second


def trade(pair, axis, periodic):
    first, second = partners(axis, periodic)
    return lax.ppermute(pair[0], axis, first), lax.ppermute(pair[1], axis, second)


def to_all(rows):
    return lax.all_to_all(rows, EVERY, 0, 0)


def to_half(rows, devices):
    groups = [[i for i in range(devices) if i % 2 == side] for side in range(2)]
    return lax.all_to_all(rows, EVERY, 0, 0, axis_index_groups=groups)


def to_pair(block):
    return lax.ppermute(block, "lon", partners("lon", True)[0])


def sigmoid(v):
    return 0.5 * jnp.tanh(0.5 * v) + 0.5


def silu(v):
    half = 0.5 * v
    return half + half * jnp.tanh(half)


def norm_consts(stats_ref, devices):
    stats = stats_ref[...]
    total = jnp.sum(stats, axis=0)
    center = total[0:1] * (1.0 / devices)
    apart = jnp.sum(jnp.square(stats - center[None]), axis=0)
    spread = (total[1:2] + apart[0:1]) * (1.0 / devices)
    return center, lax.rsqrt(spread + eps)


def top_sums(stats_ref, center, inv):
    stats = stats_ref[...]
    total = jnp.sum(stats, axis=0)
    apart = stats[:, 0:1, :] - center[None]
    return total[2:3], (total[3:4] + jnp.sum(apart * stats[:, 2:3, :], axis=0)) * inv


def shifted(value, width):
    return pltpu.roll(value, 1, 1), value, pltpu.roll(value, width - 1, 1)


def store_shifted(taps, slot, row, value, width, inner=None):
    for s, part in enumerate(shifted(value, width)):
        part = part.astype(LOW)
        taps[slot, s, pl.ds(row, 2)] = part
        if inner is not None:
            for k in range(2):
                at = row + k - (EXT - 1)
                if 0 <= at < inner.shape[2]:
                    inner[s, slot, at] = part[k, 0 : inner.shape[3]]


def lay_weights(kernel_ref, layer, back, out):
    blank = jnp.zeros((3 * LANES, LANES), LOW)
    out[9 * LANES : 12 * LANES, 0:LANES] = blank
    out[0 : 3 * LANES, LANES : 2 * LANES] = blank
    for r in range(3):
        for s in range(3):
            if back:
                block = kernel_ref[layer, (2 - r) * 3 + 2 - s].astype(F32).T.astype(LOW)
            else:
                block = kernel_ref[layer, r * 3 + s]
            at = (r * 3 + s) * LANES
            out[at : at + LANES, 0:LANES] = block
            out[at + 3 * LANES : at + 4 * LANES, LANES : 2 * LANES] = block


def even_parts(lo, hi, most):
    pairs = (hi - lo) // 2
    count = -(-pairs // most)
    out = []
    for k in range(count):
        start, stop = pairs * k // count, pairs * (k + 1) // count
        out.append((lo + 2 * start, stop - start))
    return out


def pipeline(grids, lo, hi, taps, weight, cols, prepare, emit, after, finish, extra=None, take=None, extra_totals=()):
    parts = even_parts(lo, hi, 5)
    count = len(parts)

    def body(*refs):
        totals, more = refs[: 2 * count], refs[2 * count :]
        staged = [0, 0]

        def push(unit, tile):
            staged[unit] = 1 - staged[unit]
            pltpu.matmul_push_rhs(tile, staged[unit], unit)
            return staged[unit]

        def operand(g, part, k):
            start, size = parts[part]
            halves = []
            for unit in (2 * k, 2 * k + 1):
                t, s = divmod(unit, 3)
                halves.append(jnp.concatenate([taps[g, s, start - 1 + t + 2 * n, 0:cols, :] for n in range(size)], axis=0))
            return jnp.concatenate(halves, axis=-1)

        def product(first, unit, part, k):
            def act():
                at = push(unit, weight[k * 2 * LANES : (k + 1) * 2 * LANES, :])
                pltpu.matmul_acc_lhs(totals[unit * count + part], operand(first + unit, part, k), load_staged_rhs=at)
            return act

        def collect(first, part):
            def act():
                start, size = parts[part]
                for unit in range(2):
                    both = pltpu.matmul_pop(totals[unit * count + part])
                    for n in range(size):
                        for h in range(2):
                            emit(first + unit, start + 2 * n + h, both[n * cols : (n + 1) * cols, h * LANES : (h + 1) * LANES])
            return act

        def rows_before(part):
            start, size = parts[part]
            return start + 2 * size + 1

        def ready(first, start, stop):
            return [functools.partial(prepare, first + unit, r) for r in range(start, stop, 2) for unit in range(2)]

        for task in ready(0, lo - 1, rows_before(0)):
            task()
        waiting = []

        def run(steps, tasks):
            done = 0
            for n, step in enumerate(steps):
                step()
                if n == 3:
                    while waiting:
                        waiting.pop(0)()
                while done < len(tasks) * (n + 1) // len(steps):
                    tasks[done]()
                    done += 1

        for first in range(0, grids, 2):
            last = first + 2 >= grids
            ahead = [] if last else ready(first + 2, lo - 1, hi + 1)
            if extra and last:
                run(extra(first, push, more), [])
                ahead = take(more)
            for part in range(count):
                tasks = []
                if first == 0 and part + 1 < count:
                    tasks += ready(0, rows_before(part), rows_before(part + 1))
                tasks += ahead[len(ahead) * part // count : len(ahead) * (part + 1) // count]
                run([product(first, unit, part, k) for k in range(6) for unit in range(2)], tasks)
                waiting.append(collect(first, part))
            waiting += [functools.partial(after, first + unit) for unit in range(2)]
            if extra and not last:
                run(extra(first, push, more), [])
        while waiting:
            waiting.pop(0)()
        finish()

    totals = [pltpu.ACC(unit)((size * cols, 2 * LANES), F32) for unit in range(2) for _, size in parts]
    pl.run_scoped(body, *totals, *extra_totals)


def guard(condition, act):
    if isinstance(condition, bool):
        if condition:
            act()
    else:
        pl.when(condition)(act)


def gather(sums, k, value):
    sums[k] = value if sums[k] is None else sums[k] + value


def fold(value):
    return jnp.sum(value.reshape(-1, 8, LANES), axis=0)


def to_row(value):
    return jnp.sum(value, axis=0, keepdims=True)


def both_ways(even, give_first, give_second):
    @pl.when(even == 1)
    def _():
        give_first(False)
        give_second(True)

    @pl.when(even == 0)
    def _():
        give_first(True)
        give_second(False)


def whichever(even, place, got_first, got_second):
    @pl.when(even == 1)
    def _():
        place(got_second, got_first)

    @pl.when(even == 0)
    def _():
        place(got_first, got_second)


def cut_rows(geo, info, sources, heights, first, second):
    grids, rows = geo["G"], geo["R"]

    def give(out):
        def act(low):
            at = 0
            for src, h in zip(sources, heights):
                for g in range(grids):
                    out[g, at : at + h] = src[g, 0:h] if low else src[g, src.shape[1] - h :]
                at += h
        return act

    both_ways(info[0], give(first), give(second))


def cut_cols(geo, info, sources, first, second):
    grids, cols = geo["G"], geo["C"]

    def give(out):
        def act(low):
            at = 0
            for src in sources:
                for g in range(grids):
                    part = src[g, :, 0:EXT, :] if low else src[g, :, cols - EXT : cols, :]
                    out[g, at : at + src.shape[1]] = part
                at += src.shape[1]
        return act

    both_ways(info[1], give(first), give(second))


def add_rows(geo, info, sources, heights, got_first, got_second, outs):
    grids, rows = geo["G"], geo["R"]

    def place(low, high):
        at = 0
        for out, h in zip(outs, heights):
            for g in range(grids):
                out[g, 0:h] = low[g, at : at + h]
                out[g, h + rows : 2 * h + rows] = high[g, at : at + h]
            at += h

    whichever(info[0], place, got_first, got_second)
    for src, out, h in zip(sources, outs, heights):
        for g in range(grids):
            out[g, h : h + rows] = src[g]


def add_sides(geo, info, starts, got_first, got_second, outs):
    def place(low, high):
        for out, at in zip(outs, starts):
            total = out.shape[1]
            for g in range(geo["G"]):
                right = high[g, at : at + total].astype(F32)
                left = low[g, at : at + total].astype(F32)
                out[g] = jnp.concatenate([right, left], axis=1).astype(LOW)

    whichever(info[1], place, got_first, got_second)


def across(pair, g, rows):
    parts = [ref[g, rows].astype(F32) for ref in pair]
    return jnp.concatenate(parts, axis=parts[0].ndim - 2)


def field_edge_kernel(geo, info, x, first, second, sems):
    rows = geo["R"]

    def fetch(high_out, low_out):
        copies = [
            pltpu.make_async_copy(x.at[:, rows - EXT : rows], high_out, sems.at[0]),
            pltpu.make_async_copy(x.at[:, 0:EXT], low_out, sems.at[1]),
        ]
        for c in copies:
            c.start()
        for c in copies:
            c.wait()

    @pl.when(info[0] == 1)
    def _():
        fetch(first, second)

    @pl.when(info[0] == 0)
    def _():
        fetch(second, first)


def mask_edge_kernel(geo, info, masks, first, second, near, sems):
    rows, height = geo["R"], geo["heights"][1]
    nears = [
        pltpu.make_async_copy(masks.at[0, :, 0:height], near.at[0], sems.at[0]),
        pltpu.make_async_copy(masks.at[0, :, rows - height : rows], near.at[1], sems.at[1]),
    ]
    for c in nears:
        c.start()
    for c in nears:
        c.wait()

    def give(out):
        def act(low):
            out[...] = near[0 if low else 1].astype(F32).astype(LOW)
        return act

    both_ways(info[0], give(first), give(second))


def tall_kernel(geo, heights, info, *refs):
    n = len(heights)
    talls = refs[n + 2 : 2 * n + 2]
    add_rows(geo, info, refs[:n], heights, refs[n], refs[n + 1], talls)
    cut_cols(geo, info, talls, refs[2 * n + 2], refs[2 * n + 3])


def mask_kernel(geo, masks, cot, *outs):
    for g in range(geo["G"]):
        for k in range(4):
            outs[k][g] = masks[k, g].astype(F32).astype(LOW)
        outs[4][g] = (cot[g].astype(F32) * masks[3, g].astype(F32)).astype(LOW)


def cut_kernel(geo, info, mask1, mask2, masked, cot, before, first, second):
    del before
    cut_rows(geo, info, [mask1, mask2, masked, cot], geo["heights"][2:], first, second)


def weights_kernel(kernels, before, *outs):
    del before
    for layer in range(4):
        lay_weights(kernels, layer, False, outs[layer])
        lay_weights(kernels, layer, True, outs[4 + layer])


def late_kernel(geo, info, mask1, mask2, masked, cot, first, second, before, *outs):
    del before
    add_rows(geo, info, [mask1, mask2, masked, cot], geo["heights"][2:], first, second, outs[0:4])
    cut_cols(geo, info, outs[0:1], *outs[4:6])


def last_kernel(geo, info, tall2, tall3, tall4, before, first, second):
    del before
    cut_cols(geo, info, [tall2, tall3, tall4], first, second)


def gate_kernel(sums, first, second, out):
    del first, second
    out[...] = sums[...]


def forward_kernel(layer, geo, *refs):
    grids, rows, devices, width, cols = geo["G"], geo["R"], geo["D"], geo["CE"], geo["C"]
    heights = geo["heights"]
    refs = list(refs)
    info, gains, offsets, biases, weight = (refs.pop(0) for _ in range(5))
    if layer:
        stats, pre_in = refs.pop(0), refs.pop(0)
    field = [refs.pop(0), refs.pop(0)] if layer == 2 else None
    members = geo["members"][layer]
    sources = [refs.pop(0) for _ in members]
    got = [refs.pop(0), refs.pop(0)]
    if layer in (1, 2):
        refs.pop(0)
    sums_out = refs.pop(0)
    side_outs = [refs.pop(0) for _ in members]
    pre_out, low_out = refs.pop(0), refs.pop(0)
    field_out = refs.pop(0) if layer == 2 else None
    taps, acts, acc = refs
    lo, hi = layer + 1, geo["RE"] - 1 - layer

    add_sides(geo, info, geo["starts"][layer], *got, side_outs)
    ext = [sources[0], side_outs[0]]
    if layer:
        center, inv = norm_consts(stats, devices)
        scale = inv * gains[layer - 1 : layer, :] * (1.0 / keep_rate)
        shift = offsets[layer - 1 : layer, :] * (1.0 / keep_rate) - center * scale
        scale = 0.5 * scale
    bias = biases[layer : layer + 1, :]
    number = rows * cols
    totals = [None] * grids

    def prepare(g, r):
        if layer == 0:
            value = across(ext, g, pl.ds(r, 2))
        else:
            p = pre_in[g, pl.ds(r, 2)]
            part = p * scale
            value = (part + part * jnp.tanh(0.5 * p) + shift) * across(ext, g, pl.ds(r - layer, 2))
            if layer == 2:
                value = value + across(field, g, pl.ds(r, 2))

                def save():
                    field_out[g, pl.ds(r - (EXT - 1), 2)] = value[:, 0:cols, :]

                guard((r >= EXT - 1) & (r < EXT + rows), save)
        store_shifted(taps, g, r, value, width, low_out)

    def emit(g, r, part):
        part = part + bias
        pre_out[g, r] = part
        if EXT <= r < EXT + rows:
            act = silu(part[0:cols])
            acts[g, r - EXT] = act
            gather(totals, g, fold(act))

    def after(g):
        mean = to_row(totals[g]) * (1.0 / number)
        square = jnp.zeros((8, LANES), F32)
        first = jnp.zeros((8, LANES), F32)
        second = jnp.zeros((8, LANES), F32)
        for k in range(rows):
            act = acts[g, k]
            apart = act - mean
            square = square + fold(jnp.square(apart))
            if layer == 3:
                z = sources[1][g, heights[4] + k].astype(F32)
                first = first + fold(z)
                second = second + fold(z * apart)
            if layer == 0:
                p = pre_out[g, EXT + k, 0:cols, :]
                s = sigmoid(p)
                slope = s + act * (1.0 - s)
                first = first + fold(slope)
                second = second + fold(slope * act)
        acc[g : g + 1] = mean
        acc[grids + g : grids + g + 1] = to_row(square) * (1.0 / number)
        if layer in (0, 3):
            acc[2 * grids + g : 2 * grids + g + 1] = to_row(first)
            acc[3 * grids + g : 3 * grids + g + 1] = to_row(second)

    def finish():
        means = acc[0:grids]
        middle = jnp.mean(means, axis=0, keepdims=True)
        away = means - middle
        spread = jnp.mean(acc[grids : 2 * grids] + jnp.square(away), axis=0, keepdims=True)
        out = [middle, spread]
        if layer == 3:
            ones = acc[2 * grids : 3 * grids]
            out.append(to_row(ones) * (1.0 / keep_rate))
            out.append(to_row(acc[3 * grids : 4 * grids] + away * ones) * (1.0 / keep_rate))
        if layer == 0:
            out += [to_row(acc[2 * grids : 3 * grids]), to_row(acc[3 * grids : 4 * grids])]
        for k, row in enumerate(out):
            sums_out[:, k : k + 1, :] = jnp.broadcast_to(row[None], (devices, 1, LANES))

    pipeline(grids, lo, hi, taps, weight, width, prepare, emit, after, finish)


def back_consts(layer, geo, stats, sums, gains):
    center, inv = norm_consts(stats, geo["D"])
    if layer == 3:
        one, two = top_sums(stats, center, inv)
    else:
        total = jnp.sum(sums[...], axis=0)
        one, two = total[0:1], total[1:2]
    pixels = float(geo["D"] * geo["G"] * geo["R"] * geo["C"])
    scale = inv * gains[layer : layer + 1, :]
    tilt = scale * inv * two * (-1.0 / pixels)
    flat = scale * one * (-1.0 / pixels) - center * tilt
    return center, inv, scale * (1.0 / keep_rate), flat, tilt


def through(p, dn, scale, flat, tilt):
    s = sigmoid(p)
    act = p * s
    return (dn * scale + act * tilt + flat) * (s + act * (1.0 - s)), act


def weight_term(geo, low, g, right, acc):
    rows, cols = geo["R"], geo["C"]
    parts = [low[s, g, r : r + rows] for r in range(3) for s in range(3)]
    spread = jnp.concatenate(parts, axis=-1).reshape(rows * cols, 9 * LANES)
    term = lax.dot_general(right, spread, (((0,), (0,)), ((), ())), preferred_element_type=F32)
    if g == 0:
        acc[...] = term
    else:
        acc[...] += term


def split_halves(info, acc, keep_half, send_half):
    half = 9 * LANES // 2

    def give(out):
        def act(upper):
            start = half if upper else 0
            for t in range(9):
                lo, hi = max(t * LANES, start), min((t + 1) * LANES, start + half)
                if lo < hi:
                    block = acc[:, t * LANES : (t + 1) * LANES].T
                    out[lo - start : hi - start] = block[lo - t * LANES : hi - t * LANES]
        return act

    both_ways(info[1], give(keep_half), give(send_half))


def backward_kernel(layer, geo, *refs):
    grids, rows, devices, width, cols = geo["G"], geo["R"], geo["D"], geo["CE"], geo["C"]
    heights = geo["heights"]
    refs = list(refs)
    info, gains, offsets, weight, stats, sums, pre, low = (refs.pop(0) for _ in range(8))
    masked = keep_top = field = cot = z_in = None
    if layer == 3:
        masked, keep_top, field = [refs.pop(0), refs.pop(0)], refs.pop(0), refs.pop(0)
    else:
        z_in = refs.pop(0)
    if layer == 2:
        cot = [refs.pop(0), refs.pop(0)]
    keep = [refs.pop(0), refs.pop(0)]
    stats_below, pre_below = refs.pop(0), refs.pop(0)
    sums_out, keep_half, send_half, z_out = (refs.pop(0) for _ in range(4))
    grad_out = refs.pop(0) if layer == 2 else None
    result = refs.pop(0) if layer == 3 else None
    taps, term = refs[:2]
    if layer == 3:
        result_out, (result, sems) = result, refs[2:]
        leaving = [pltpu.make_async_copy(result.at[g], result_out.at[g], sems.at[g]) for g in range(grids)]
    lo, hi = EXT - layer, EXT + rows + layer
    keep_off = EXT - heights[layer]

    center, inv, scale, flat, tilt = back_consts(layer, geo, stats, sums, gains)
    first_row, last_row = info[2], info[3]
    center_b, inv_b = norm_consts(stats_below, devices)
    sums_here = [None] * 4

    if layer == 3:
        lift = inv * gains[layer : layer + 1, :] * (1.0 / keep_rate)
        base = offsets[layer : layer + 1, :] * (1.0 / keep_rate) - center * lift

    def prepare(g, r):
        if layer == 3:
            z = across(masked, g, pl.ds(r - (EXT - heights[4]), 2))
        else:
            z = z_in[g, pl.ds(r, 2)]
        value, act = through(pre[g, pl.ds(r, 2)], z, scale, flat, tilt)
        if not (isinstance(r, int) and EXT <= r and r + 2 <= EXT + rows):
            real = [jnp.where((r + k >= first_row) & (r + k < last_row), 1.0, 0.0).astype(F32) for k in range(2)]
            value = jnp.stack([value[0] * real[0], value[1] * real[1]])
        store_shifted(taps, g, r, value, width)
        if layer == 3:
            def save():
                y = (act[:, 0:cols] * lift + base) * keep_top[g, pl.ds(r - EXT, 2)].astype(F32)
                result[g, pl.ds(r - EXT, 2)] = (field[g, pl.ds(r - EXT + 1, 2)] + y).astype(LOW)

            guard((r >= EXT) & (r < EXT + rows), save)

    def emit(g, r, part):
        inner = EXT <= r < EXT + rows
        if layer == 2:
            part = part + across(cot, g, r - (EXT - heights[5]))
            if inner:
                grad_out[g, r - EXT] = part[0:cols]
        z = part * across(keep, g, r - keep_off)
        z_out[g, r] = z
        if inner:
            z = z[0:cols]
            p = pre_below[g, r, 0:cols, :]
            s = sigmoid(p)
            act = p * s
            gather(sums_here, 0, fold(z))
            gather(sums_here, 1, fold(z * (act - center_b)))
            if layer == 1:
                gather(sums_here, 3, fold(z * (s + act * (1.0 - s))))

    def inside(g):
        return taps[g, 1, EXT : EXT + rows, 0:cols, :].reshape(rows * cols, LANES)

    def after(g):
        if layer == 3:
            leaving[g].start()
        gather(sums_here, 2, fold(inside(g).astype(F32)))

    def weight_steps(first, push, totals):
        depth = 2 * LANES // cols
        steps = []
        for g in (first, first + 1):
            for at in range(0, rows, depth):
                turned = []

                def act(n, g=g, at=at, turned=turned):
                    if not turned:
                        block = taps[g, 1, EXT + at : EXT + at + depth, 0:cols, :].reshape(2 * LANES, LANES)
                        turned.append(block.T)
                    halves = []
                    for tap in (2 * n, 2 * n + 1):
                        r, s = divmod(min(tap, 8), 3)
                        halves.append(low[s, g, at + r : at + r + depth].reshape(2 * LANES, LANES))
                    staged = push(n % 2, jnp.concatenate(halves, axis=-1))
                    pltpu.matmul_acc_lhs(totals[n], turned[0], load_staged_rhs=staged)

                steps += [functools.partial(act, n) for n in range(5)]
        return steps

    def take_term(totals):
        def act(n):
            both = pltpu.matmul_pop(totals[n])
            for tap in range(2 * n, min(2 * n + 2, 9)):
                at = (tap - 2 * n) * LANES
                term[tap * LANES : (tap + 1) * LANES] = both[:, at : at + LANES].T

        return [functools.partial(act, n) for n in range(5)]

    def finish():
        half = 9 * LANES // 2
        start = pl.multiple_of((1 - info[1]) * half, 8)
        keep_half[...] = term[pl.ds(start, half)]
        send_half[...] = term[pl.ds(pl.multiple_of(half - start, 8), half)]
        out = [to_row(sums_here[k]) for k in range(4 if layer == 1 else 3)]
        out[0] = out[0] * (1.0 / keep_rate)
        out[1] = out[1] * inv_b * (1.0 / keep_rate)
        if layer == 1:
            out[3] = out[3] * (1.0 / keep_rate)
        for k, row in enumerate(out):
            sums_out[:, k : k + 1, :] = jnp.broadcast_to(row[None], (devices, 1, LANES))
        if layer == 3:
            for c in leaving:
                c.wait()

    totals = [pltpu.ACC(n % 2)((LANES, 2 * LANES), F32) for n in range(5)]
    pipeline(grids, lo, hi, taps, weight, width, prepare, emit, after, finish, weight_steps, take_term, totals)


def first_weight_kernel(geo, *refs):
    grids, rows, width, cols = geo["G"], geo["R"], geo["CE"], geo["C"]
    info, gains, stats, sums, pre, low, z_in, sent, keep_half, send_both, dpre, acc = refs
    half = 9 * LANES // 2
    send_both[0:half] = sent[...]
    scale, flat, tilt = back_consts(0, geo, stats, sums, gains)[2:]
    first_row, last_row = info[2], info[3]

    for g in range(grids):
        for k in range(rows + 2):
            r = EXT - 1 + k
            value, _ = through(pre[g, r], z_in[g, r], scale, flat, tilt)
            if k in (0, rows + 1):
                value = value * jnp.where((r >= first_row) & (r < last_row), 1.0, 0.0).astype(F32)
            dpre[g, k] = value.astype(LOW)
        weight_term(geo, low, g, dpre[g, 1 : rows + 1, 0:cols, :].reshape(rows * cols, LANES), acc)
    split_halves(info, acc, keep_half, send_both.at[half : 2 * half])


def input_grad_kernel(geo, weight, dpre, grad, gains, *refs):
    grids, rows, width, cols = geo["G"], geo["R"], geo["CE"], geo["C"]
    out, taps, buffer, sems = refs[7], *refs[11:]
    leaving = [pltpu.make_async_copy(buffer.at[g], out.at[g], sems.at[g]) for g in range(grids)]
    def prepare(g, r):
        store_shifted(taps, g, r, dpre[g, pl.ds(r, 2)].astype(F32), width)

    def emit(g, r, part):
        buffer[g, r - 1] = grad[g, r - 1] + part

    pipeline(grids, 1, rows + 1, taps, weight, cols, prepare, emit, lambda g: leaving[g].start(), lambda: None)
    gather_rows(geo, gains, *refs[0:7], *refs[8:11])
    for c in leaving:
        c.wait()


def share_kernel(*refs):
    third, second, both, out = refs[4:]
    half = 9 * LANES // 2
    gots = [both[half : 2 * half], both[0:half], second[...], third[...]]
    for k in range(4):
        out[k * half : (k + 1) * half] = (refs[k][...] + gots[k]).astype(LOW)


def total_kernel(devices, got, out):
    total = jnp.sum(got[...].astype(F32), axis=0)
    out[...] = jnp.broadcast_to(total.astype(LOW)[None], out.shape)


def join_kernel(geo, info, mine, other, out, buffer, sems):
    half = 9 * LANES // 2
    leaving = [pltpu.make_async_copy(buffer.at[k], out.at[k], sems.at[k]) for k in range(4)]

    def place(low, high):
        for k in range(4):
            buffer[k, 0:half] = low[k].astype(F32)
            buffer[k, half:] = high[k].astype(F32)
            leaving[k].start()

    @pl.when(info[1] == 1)
    def _():
        place(mine, other)

    @pl.when(info[1] == 0)
    def _():
        place(other, mine)

    for c in leaving:
        c.wait()


def gather_rows(geo, gains, *refs):
    stats, sums = refs[0:4], refs[4:7]
    bias_out, gain_out, offset_out = refs[7:]
    for layer in range(4):
        center, inv = norm_consts(stats[layer], geo["D"])
        if layer == 3:
            one, two = top_sums(stats[3], center, inv)
        else:
            total = jnp.sum(sums[layer][...], axis=0)
            one, two = total[0:1], total[1:2]
        offset_out[layer : layer + 1] = one
        gain_out[layer : layer + 1] = two
        if layer:
            bias_out[layer : layer + 1] = jnp.sum(sums[layer - 1][...], axis=0)[2:3]
        else:
            pixels = float(geo["D"] * geo["G"] * geo["R"] * geo["C"])
            slopes = jnp.sum(stats[0][...], axis=0)
            flat, lifted = slopes[2:3], (slopes[3:4] - center * slopes[2:3]) * inv
            bias_out[0:1] = inv * gains[0:1, :] * (total[3:4] - flat * one / pixels - lifted * two / pixels)


def call(kernel, operands, outs, scratch=(), flops=10**6, moved=10**6, scalars=1, final=(), small=(), outside=False):
    space = pl.BlockSpec(memory_space=pltpu.VMEM)
    specs = [pl.BlockSpec(memory_space=pltpu.SMEM)] * scalars
    operands = list(operands)
    for k in range(scalars, len(operands)):
        if outside:
            specs.append(pl.BlockSpec(memory_space=pltpu.HBM))
            operands[k] = pltpu.with_memory_space_constraint(operands[k], pltpu.HBM)
        else:
            specs.append(space)
            operands[k] = pltpu.with_memory_space_constraint(operands[k], pltpu.VMEM)
    plain = set(final) | set(small)
    shapes = [jax.ShapeDtypeStruct(s, d) if k in plain else pltpu.VMEM(s, d) for k, (s, d) in enumerate(outs)]
    places = [pl.BlockSpec(memory_space=pltpu.HBM) if k in final else space for k in range(len(outs))]
    return pl.pallas_call(
        kernel,
        in_specs=specs,
        out_specs=places,
        out_shape=shapes,
        scratch_shapes=[v if hasattr(v, "shape") and not isinstance(v, tuple) else pltpu.VMEM(*v) for v in scratch],
        compiler_params=pltpu.CompilerParams(vmem_limit_bytes=10 * 2**20),
        cost_estimate=pl.CostEstimate(flops=flops, bytes_accessed=moved, transcendentals=0),
    )(*operands)


def conv_scratch(geo, tall):
    return [((geo["G"], 3, tall, geo["CE"], LANES), LOW)]


def forward_call(layer, geo, operands):
    grids, rows, rows_ext, width, devices, cols = geo["G"], geo["R"], geo["RE"], geo["CE"], geo["D"], geo["C"]
    kinds = 4 if layer in (0, 3) else 2
    outs = [((devices, kinds, LANES), F32)]
    for k in geo["members"][layer]:
        outs.append(((grids, rows + 2 * geo["heights"][k], 2 * EXT, LANES), LOW))
    outs.append(((grids, rows_ext, width, LANES), F32))
    outs.append(((3, grids, rows + 2, cols, LANES), LOW))
    if layer == 2:
        outs.append(((grids, rows + 2, cols, LANES), F32))
    scratch = conv_scratch(geo, rows_ext) + [((grids, rows, cols, LANES), F32), ((kinds * grids, LANES), F32)]
    return call(functools.partial(forward_kernel, layer, geo), operands, outs, scratch, 2 * 10**9, 8 * 10**6)


def backward_call(layer, geo, operands):
    grids, rows, rows_ext, width, devices, cols = geo["G"], geo["R"], geo["RE"], geo["CE"], geo["D"], geo["C"]
    half = ((9 * LANES // 2, LANES), F32)
    outs = [((devices, 4 if layer == 1 else 3, LANES), F32), half, half, ((grids, rows_ext, width, LANES), F32)]
    if layer == 2:
        outs.append(((grids, rows, cols, LANES), F32))
    if layer == 3:
        outs.append(((grids, rows, cols, LANES), LOW))
    scratch = conv_scratch(geo, rows_ext) + [((9 * LANES, LANES), F32)]
    if layer == 3:
        scratch += [((grids, rows, cols, LANES), LOW), pltpu.SemaphoreType.DMA((grids,))]
    return call(
        functools.partial(backward_kernel, layer, geo), operands, outs, scratch, 3 * 10**9, 8 * 10**6,
        final=(4,) if layer == 3 else (),
    )


def local(inputs, kernels, biases, gains, offsets, keep_masks, cotangent):
    grids, rows, cols, _ = inputs.shape
    devices = lax.axis_size("batch") * lax.axis_size("lat") * lax.axis_size("lon")
    heights = [EXT, 7, 6, 5, 4, 2]
    starts = [0]
    for k in (3, 4):
        starts.append(starts[-1] + rows + 2 * heights[k])
    geo = dict(
        G=grids, R=rows, C=cols, D=devices, RE=rows + 2 * EXT, CE=cols + 2 * EXT, heights=heights,
        starts=[[0], [0], [0], starts], members=[[0], [1], [2], [3, 4, 5]],
    )
    lat, lon = lax.axis_index("lat"), lax.axis_index("lon")
    info = jnp.stack(
        [
            1 - lax.rem(lat, 2),
            1 - lax.rem(lon, 2),
            jnp.where(lat == 0, EXT, 0),
            jnp.where(lat == lax.axis_size("lat") - 1, EXT + rows, rows + 2 * EXT),
        ]
    ).astype(jnp.int32)
    kernels = kernels.reshape(4, 9, LANES, LANES)

    def block(tall, wide):
        return ((grids, tall, wide, LANES), LOW)

    x_height, soon, late = heights[0], heights[1], sum(heights[2:])
    pair_sems = pltpu.SemaphoreType.DMA((2,))
    outs = call(
        functools.partial(field_edge_kernel, geo), [info, inputs], [block(x_height, cols)] * 2, [pair_sems], outside=True
    )
    x_got = trade(outs, "lat", False)
    outs = call(
        functools.partial(mask_edge_kernel, geo), [info, keep_masks], [block(soon, cols)] * 2,
        [((2, grids, soon, cols, LANES), jnp.int32), pair_sems], outside=True,
    )
    soon_got = trade(outs, "lat", False)
    weights = call(weights_kernel, [kernels, outs[0]], [((12 * LANES, 2 * LANES), LOW)] * 8, scalars=0)
    outs = call(
        functools.partial(tall_kernel, geo, heights[:1]), [info, inputs, *x_got],
        [block(rows + 2 * x_height, cols)] + [block(rows + 2 * x_height, EXT)] * 2,
    )
    pieces = [[outs[0], *trade(outs[1:3], "lon", True)]]
    outs = call(functools.partial(mask_kernel, geo), [keep_masks, cotangent], [block(rows, cols)] * 5, scalars=0)
    low_masks, masked = list(outs[0:4]), outs[4]
    outs = call(
        functools.partial(tall_kernel, geo, heights[1:2]), [info, low_masks[0], *soon_got],
        [block(rows + 2 * soon, cols)] + [block(rows + 2 * soon, EXT)] * 2,
    )
    pieces.append([outs[0], *trade(outs[1:3], "lon", True)])
    edges = call(
        functools.partial(cut_kernel, geo), [info, low_masks[1], low_masks[2], masked, cotangent, outs[1]],
        [block(late, cols)] * 2,
    )
    late_got = trade(edges, "lat", False)
    talls = [rows + 2 * h for h in heights[2:]]

    pres, lows, stats, exts = [None] * 4, [None] * 4, [None] * 4, [None] * 6
    field = order = None
    for layer in range(4):
        operands = [info, gains, offsets, biases, weights[layer]]
        if layer:
            operands += [stats[layer - 1], pres[layer - 1]]
        if layer == 2:
            operands += exts[0]
        operands += pieces[layer]
        if layer in (1, 2):
            operands.append(order)
        outs = list(forward_call(layer, geo, operands))
        part = outs.pop(0)
        if layer < 2:
            (part,) = call(gate_kernel, [part] + pieces[layer + 1][1:], [(part.shape, F32)], scalars=0)
        stats[layer] = to_all(part)
        if layer == 0:
            ends = call(
                functools.partial(late_kernel, geo), [info] + low_masks[1:3] + [masked, cotangent, *late_got, stats[0]],
                [block(t, cols) for t in talls] + [block(talls[0], EXT)] * 2,
            )
            pieces.append([ends[0], *trade(ends[4:6], "lon", True)])
            order = ends[4]
        if layer == 1:
            edges = call(
                functools.partial(last_kernel, geo), [info, *ends[1:4], stats[1]], [block(sum(talls[1:]), EXT)] * 2
            )
            pieces.append([*ends[1:4], *trade(edges, "lon", True)])
            order = edges[0]
        for n, k in enumerate(geo["members"][layer]):
            exts[k] = [pieces[layer][n], outs.pop(0)]
        pres[layer], lows[layer] = outs.pop(0), outs.pop(0)
        if layer == 2:
            field = outs.pop(0)

    sums = [None] * 4
    sums[3] = stats[3]
    kept, got = [None] * 4, []
    z = grad = output = None
    for layer in (3, 2, 1):
        operands = [info, gains, offsets, weights[4 + layer], stats[layer], sums[layer], pres[layer], lows[layer]]
        operands += [*exts[4], low_masks[3], field] if layer == 3 else [z]
        if layer == 2:
            operands += exts[5]
        operands += [*exts[layer], stats[layer - 1], pres[layer - 1]]
        outs = backward_call(layer, geo, operands)
        sums[layer - 1] = to_all(outs[0])
        kept[layer], sent = outs[1], outs[2]
        if layer > 1:
            got.append(to_pair(sent))
        z = outs[3]
        if layer == 2:
            grad = outs[4]
        if layer == 3:
            output = outs[4]
    half = 9 * LANES // 2
    term = ((half, LANES), F32)
    kept[0], sent, dpre = call(
        functools.partial(first_weight_kernel, geo), [info, gains, stats[0], sums[0], pres[0], lows[0], z, sent],
        [term, ((2 * half, LANES), F32), block(rows + 2, cols + 2 * EXT)], [((LANES, 9 * LANES), F32)], 10**9, 8 * 10**6,
    )
    got.append(to_pair(sent))

    (shares,) = call(share_kernel, kept + got, [((4 * half, LANES), LOW)], scalars=0)
    slots = (devices // 2, 4 * half // (devices // 2), LANES)
    arrived = to_half(shares.reshape(slots), devices)
    (mine,) = call(functools.partial(total_kernel, devices), [arrived], [(slots, LOW)], scalars=0)
    mine = to_half(mine, devices).reshape(4, half, LANES)
    (kernel_grad,) = call(
        functools.partial(join_kernel, geo), [info, mine, to_pair(mine)], [((4, 9 * LANES, LANES), F32)],
        [((4, 9 * LANES, LANES), F32), pltpu.SemaphoreType.DMA((4,))], final=(0,),
    )
    small = ((4, LANES), F32)
    field_like = ((grids, rows, cols, LANES), F32)
    input_grad, bias_grad, gain_grad, offset_grad = call(
        functools.partial(input_grad_kernel, geo), [weights[4], dpre, grad, gains] + stats + sums[:3],
        [field_like] + [small] * 3, conv_scratch(geo, rows + 2) + [field_like, pltpu.SemaphoreType.DMA((grids,))],
        10**9, 3 * 10**6, scalars=0, final=(0,), small=(1, 2, 3),
    )
    return (output, input_grad, kernel_grad.reshape(4, 3, 3, LANES, LANES), bias_grad, gain_grad, offset_grad)


def solution(mesh):
    in_specs = (
        P("batch", "lat", "lon", None),
        P(),
        P(),
        P(),
        P(),
        P(None, "batch", "lat", "lon", None),
        P("batch", "lat", "lon", None),
    )
    out_specs = (P("batch", "lat", "lon", None), P("batch", "lat", "lon", None), P(), P(), P(), P())
    return jax.shard_map(local, mesh=mesh, in_specs=in_specs, out_specs=out_specs, check_vma=False)
```

```python
import functools

import jax
import jax.numpy as jnp
from jax import lax
from jax.experimental import pallas as pl
from jax.experimental.pallas import tpu as pltpu
from jax.sharding import PartitionSpec as P

eps = 1e-05
keep_rate = 0.9
EVERY = ("batch", "lat", "lon")
EXT = 8
LANES = 128
F32 = jnp.float32
LOW = jnp.bfloat16


def partners(axis, periodic):
    count = lax.axis_size(axis)
    first = [(i, i ^ 1) for i in range(count)]
    second = []
    for i in range(count):
        j = i + 1 if i % 2 else i - 1
        if periodic:
            second.append((i, j % count))
        elif 0 <= j < count:
            second.append((i, j))
    return first, second


def trade(pair, axis, periodic):
    first, second = partners(axis, periodic)
    return lax.ppermute(pair[0], axis, first), lax.ppermute(pair[1], axis, second)


def to_all(rows):
    return lax.all_to_all(rows, EVERY, 0, 0)


def to_half(rows, devices):
    groups = [[i for i in range(devices) if i % 2 == side] for side in range(2)]
    return lax.all_to_all(rows, EVERY, 0, 0, axis_index_groups=groups)


def to_pair(block):
    return lax.ppermute(block, "lon", partners("lon", True)[0])


def sigmoid(v):
    return 0.5 * jnp.tanh(0.5 * v) + 0.5


def silu(v):
    half = 0.5 * v
    return half + half * jnp.tanh(half)


def norm_consts(stats_ref, devices):
    stats = stats_ref[...]
    total = jnp.sum(stats, axis=0)
    center = total[0:1] * (1.0 / devices)
    apart = jnp.sum(jnp.square(stats - center[None]), axis=0)
    spread = (total[1:2] + apart[0:1]) * (1.0 / devices)
    return center, lax.rsqrt(spread + eps)


def top_sums(stats_ref, center, inv):
    stats = stats_ref[...]
    total = jnp.sum(stats, axis=0)
    apart = stats[:, 0:1, :] - center[None]
    return total[2:3], (total[3:4] + jnp.sum(apart * stats[:, 2:3, :], axis=0)) * inv


def shifted(value, width):
    return pltpu.roll(value, 1, 1), value, pltpu.roll(value, width - 1, 1)


def store_shifted(taps, slot, row, value, width, inner=None):
    for s, part in enumerate(shifted(value, width)):
        part = part.astype(LOW)
        taps[slot, s, pl.ds(row, 2)] = part
        if inner is not None:
            for k in range(2):
                at = row + k - (EXT - 1)
                if 0 <= at < inner.shape[2]:
                    inner[s, slot, at] = part[k, 0 : inner.shape[3]]


def lay_weights(kernel_ref, layer, back, out):
    blank = jnp.zeros((3 * LANES, LANES), LOW)
    out[9 * LANES : 12 * LANES, 0:LANES] = blank
    out[0 : 3 * LANES, LANES : 2 * LANES] = blank
    for r in range(3):
        for s in range(3):
            if back:
                block = kernel_ref[layer, (2 - r) * 3 + 2 - s].astype(F32).T.astype(LOW)
            else:
                block = kernel_ref[layer, r * 3 + s]
            at = (r * 3 + s) * LANES
            out[at : at + LANES, 0:LANES] = block
            out[at + 3 * LANES : at + 4 * LANES, LANES : 2 * LANES] = block


def even_parts(lo, hi, most):
    pairs = (hi - lo) // 2
    count = -(-pairs // most)
    out = []
    for k in range(count):
        start, stop = pairs * k // count, pairs * (k + 1) // count
        out.append((lo + 2 * start, stop - start))
    return out


def pipeline(grids, lo, hi, taps, weight, cols, prepare, emit, after, finish, extra=None, take=None, extra_totals=()):
    parts = even_parts(lo, hi, 5)
    count = len(parts)

    def body(*refs):
        totals, more = refs[: 2 * count], refs[2 * count :]
        staged = [0, 0]

        def push(unit, tile):
            staged[unit] = 1 - staged[unit]
            pltpu.matmul_push_rhs(tile, staged[unit], unit)
            return staged[unit]

        def operand(g, part, k):
            start, size = parts[part]
            halves = []
            for unit in (2 * k, 2 * k + 1):
                t, s = divmod(unit, 3)
                halves.append(jnp.concatenate([taps[g, s, start - 1 + t + 2 * n, 0:cols, :] for n in range(size)], axis=0))
            return jnp.concatenate(halves, axis=-1)

        def product(first, unit, part, k):
            def act():
                at = push(unit, weight[k * 2 * LANES : (k + 1) * 2 * LANES, :])
                pltpu.matmul_acc_lhs(totals[unit * count + part], operand(first + unit, part, k), load_staged_rhs=at)
            return act

        def collect(first, part):
            def act():
                start, size = parts[part]
                for unit in range(2):
                    both = pltpu.matmul_pop(totals[unit * count + part])
                    for n in range(size):
                        for h in range(2):
                            emit(first + unit, start + 2 * n + h, both[n * cols : (n + 1) * cols, h * LANES : (h + 1) * LANES])
            return act

        def rows_before(part):
            start, size = parts[part]
            return start + 2 * size + 1

        def ready(first, start, stop):
            return [functools.partial(prepare, first + unit, r) for r in range(start, stop, 2) for unit in range(2)]

        for task in ready(0, lo - 1, rows_before(0)):
            task()
        waiting = []

        def run(steps, tasks):
            done = 0
            for n, step in enumerate(steps):
                step()
                if n == 3:
                    while waiting:
                        waiting.pop(0)()
                while done < len(tasks) * (n + 1) // len(steps):
                    tasks[done]()
                    done += 1

        for first in range(0, grids, 2):
            last = first + 2 >= grids
            ahead = [] if last else ready(first + 2, lo - 1, hi + 1)
            if extra and last:
                run(extra(first, push, more), [])
                ahead = take(more)
            for part in range(count):
                tasks = []
                if first == 0 and part + 1 < count:
                    tasks += ready(0, rows_before(part), rows_before(part + 1))
                tasks += ahead[len(ahead) * part // count : len(ahead) * (part + 1) // count]
                run([product(first, unit, part, k) for k in range(6) for unit in range(2)], tasks)
                waiting.append(collect(first, part))
            waiting += [functools.partial(after, first + unit) for unit in range(2)]
            if extra and not last:
                run(extra(first, push, more), [])
        while waiting:
            waiting.pop(0)()
        finish()

    totals = [pltpu.ACC(unit)((size * cols, 2 * LANES), F32) for unit in range(2) for _, size in parts]
    pl.run_scoped(body, *totals, *extra_totals)


def guard(condition, act):
    if isinstance(condition, bool):
        if condition:
            act()
    else:
        pl.when(condition)(act)


def gather(sums, k, value):
    sums[k] = value if sums[k] is None else sums[k] + value


def fold(value):
    return jnp.sum(value.reshape(-1, 8, LANES), axis=0)


def to_row(value):
    return jnp.sum(value, axis=0, keepdims=True)


def both_ways(even, give_first, give_second):
    @pl.when(even == 1)
    def _():
        give_first(False)
        give_second(True)

    @pl.when(even == 0)
    def _():
        give_first(True)
        give_second(False)


def whichever(even, place, got_first, got_second):
    @pl.when(even == 1)
    def _():
        place(got_second, got_first)

    @pl.when(even == 0)
    def _():
        place(got_first, got_second)


def cut_rows(geo, info, sources, heights, first, second):
    grids, rows = geo["G"], geo["R"]

    def give(out):
        def act(low):
            at = 0
            for src, h in zip(sources, heights):
                for g in range(grids):
                    out[g, at : at + h] = src[g, 0:h] if low else src[g, src.shape[1] - h :]
                at += h
        return act

    both_ways(info[0], give(first), give(second))


def cut_cols(geo, info, sources, first, second):
    grids, cols = geo["G"], geo["C"]

    def give(out):
        def act(low):
            at = 0
            for src in sources:
                for g in range(grids):
                    part = src[g, :, 0:EXT, :] if low else src[g, :, cols - EXT : cols, :]
                    out[g, at : at + src.shape[1]] = part
                at += src.shape[1]
        return act

    both_ways(info[1], give(first), give(second))


def add_rows(geo, info, sources, heights, got_first, got_second, outs):
    grids, rows = geo["G"], geo["R"]

    def place(low, high):
        at = 0
        for out, h in zip(outs, heights):
            for g in range(grids):
                out[g, 0:h] = low[g, at : at + h]
                out[g, h + rows : 2 * h + rows] = high[g, at : at + h]
            at += h

    whichever(info[0], place, got_first, got_second)
    for src, out, h in zip(sources, outs, heights):
        for g in range(grids):
            out[g, h : h + rows] = src[g]


def add_sides(geo, info, starts, got_first, got_second, outs):
    def place(low, high):
        for n, (out, at) in enumerate(zip(outs, starts)):
            total = out.shape[1]
            for g in range(geo["G"]):
                right = high[g, at : at + total].astype(F32)
                left = low[g, at : at + total].astype(F32)
                if n == 2:
                    right, left = pltpu.roll(right, EXT // 2, 1), pltpu.roll(left, EXT // 2, 1)
                out[g] = jnp.concatenate([right, left], axis=1).astype(LOW)

    whichever(info[1], place, got_first, got_second)


def across(pair, g, rows):
    parts = [ref[g, rows].astype(F32) for ref in pair]
    return jnp.concatenate(parts, axis=parts[0].ndim - 2)


def field_edge_kernel(geo, info, x, first, second, sems):
    rows = geo["R"]

    def fetch(high_out, low_out):
        copies = [
            pltpu.make_async_copy(x.at[:, rows - EXT : rows], high_out, sems.at[0]),
            pltpu.make_async_copy(x.at[:, 0:EXT], low_out, sems.at[1]),
        ]
        for c in copies:
            c.start()
        for c in copies:
            c.wait()

    @pl.when(info[0] == 1)
    def _():
        fetch(first, second)

    @pl.when(info[0] == 0)
    def _():
        fetch(second, first)


def mask_edge_kernel(geo, info, masks, first, second, near, sems):
    rows, height = geo["R"], geo["heights"][1]
    nears = [
        pltpu.make_async_copy(masks.at[0, :, 0:height], near.at[0], sems.at[0]),
        pltpu.make_async_copy(masks.at[0, :, rows - height : rows], near.at[1], sems.at[1]),
    ]
    for c in nears:
        c.start()
    for c in nears:
        c.wait()

    def give(out):
        def act(low):
            out[...] = near[0 if low else 1].astype(F32).astype(LOW)
        return act

    both_ways(info[0], give(first), give(second))


def tall_kernel(geo, heights, info, *refs):
    n = len(heights)
    talls = refs[n + 2 : 2 * n + 2]
    add_rows(geo, info, refs[:n], heights, refs[n], refs[n + 1], talls)
    cut_cols(geo, info, talls, refs[2 * n + 2], refs[2 * n + 3])


def mask_kernel(geo, masks, cot, *outs):
    for g in range(geo["G"]):
        for k in range(4):
            outs[k][g] = masks[k, g].astype(F32).astype(LOW)
        outs[4][g] = (cot[g].astype(F32) * masks[3, g].astype(F32)).astype(LOW)


def cut_kernel(geo, info, mask1, mask2, masked, cot, before, first, second):
    del before
    cut_rows(geo, info, [mask1, mask2, masked, cot], geo["heights"][2:], first, second)


def weights_kernel(which, kernels, before, *outs):
    del before
    for (layer, back), out in zip(which, outs):
        lay_weights(kernels, layer, back, out)


def late_kernel(geo, info, mask1, mask2, masked, cot, first, second, before, *outs):
    del before
    add_rows(geo, info, [mask1, mask2, masked, cot], geo["heights"][2:], first, second, outs[0:4])
    cut_cols(geo, info, outs[0:1], *outs[4:6])


def last_kernel(geo, info, tall2, tall3, tall4, before, first, second):
    del before
    cols, above, shared = geo["C"], tall2.shape[1], tall4.shape[1]
    extra = (tall3.shape[1] - shared) // 2
    cut_cols(geo, info, [tall2], first, second)

    def give(out):
        def act(low):
            at = pl.ds(0, EXT) if low else pl.ds(cols - EXT, EXT)
            place = lax.broadcasted_iota(jnp.int32, (shared, EXT, LANES), 1)
            near = place < EXT // 2 if low else place >= EXT // 2
            for g in range(geo["G"]):
                out[g, above : above + tall3.shape[1]] = tall3[g, :, at]
                mine = tall3[g, extra : extra + shared, at].astype(F32)
                other = pltpu.roll(tall4[g, :, at].astype(F32), EXT // 2, 1)
                out[g, above + extra : above + extra + shared] = jnp.where(near, mine, other).astype(LOW)
        return act

    both_ways(info[1], give(first), give(second))


def gate_kernel(sums, *refs):
    refs[-1][...] = sums[...]


def forward_kernel(layer, geo, *refs):
    grids, rows, devices, width, cols = geo["G"], geo["R"], geo["D"], geo["CE"], geo["C"]
    heights = geo["heights"]
    refs = list(refs)
    info, gains, offsets, biases, weight = (refs.pop(0) for _ in range(5))
    if layer:
        stats, pre_in = refs.pop(0), refs.pop(0)
    field = [refs.pop(0), refs.pop(0)] if layer == 2 else None
    members = geo["members"][layer]
    sources = [refs.pop(0) for _ in members]
    got = [refs.pop(0), refs.pop(0)]
    if layer in (1, 2):
        refs.pop(0)
    sums_out = refs.pop(0)
    side_outs = [refs.pop(0) for _ in members]
    pre_out, low_out = refs.pop(0), refs.pop(0)
    field_out = refs.pop(0) if layer == 2 else None
    taps, acts, acc = refs
    lo, hi = layer + 1, geo["RE"] - 1 - layer

    add_sides(geo, info, geo["starts"][layer], *got, side_outs)
    ext = [sources[0], side_outs[0]]
    if layer:
        center, inv = norm_consts(stats, devices)
        scale = inv * gains[layer - 1 : layer, :] * (1.0 / keep_rate)
        shift = offsets[layer - 1 : layer, :] * (1.0 / keep_rate) - center * scale
        scale = 0.5 * scale
    bias = biases[layer : layer + 1, :]
    number = rows * cols
    totals = [None] * grids

    def prepare(g, r):
        if layer == 0:
            value = across(ext, g, pl.ds(r, 2))
        else:
            p = pre_in[g, pl.ds(r, 2)]
            part = p * scale
            value = (part + part * jnp.tanh(0.5 * p) + shift) * across(ext, g, pl.ds(r - layer, 2))
            if layer == 2:
                value = value + across(field, g, pl.ds(r, 2))

                def save():
                    field_out[g, pl.ds(r - (EXT - 1), 2)] = value[:, 0:cols, :]

                guard((r >= EXT - 1) & (r < EXT + rows), save)
        store_shifted(taps, g, r, value, width, low_out)

    def emit(g, r, part):
        part = part + bias
        pre_out[g, r] = part
        if EXT <= r < EXT + rows:
            act = silu(part[0:cols])
            acts[g, r - EXT] = act
            gather(totals, g, fold(act))

    def after(g):
        mean = to_row(totals[g]) * (1.0 / number)
        square = jnp.zeros((8, LANES), F32)
        first = jnp.zeros((8, LANES), F32)
        second = jnp.zeros((8, LANES), F32)
        for k in range(rows):
            act = acts[g, k]
            apart = act - mean
            square = square + fold(jnp.square(apart))
            if layer == 3:
                z = sources[1][g, heights[4] + k].astype(F32)
                first = first + fold(z)
                second = second + fold(z * apart)
            if layer == 0:
                p = pre_out[g, EXT + k, 0:cols, :]
                s = sigmoid(p)
                slope = s + act * (1.0 - s)
                first = first + fold(slope)
                second = second + fold(slope * act)
        acc[g : g + 1] = mean
        acc[grids + g : grids + g + 1] = to_row(square) * (1.0 / number)
        if layer in (0, 3):
            acc[2 * grids + g : 2 * grids + g + 1] = to_row(first)
            acc[3 * grids + g : 3 * grids + g + 1] = to_row(second)

    def finish():
        means = acc[0:grids]
        middle = jnp.mean(means, axis=0, keepdims=True)
        away = means - middle
        spread = jnp.mean(acc[grids : 2 * grids] + jnp.square(away), axis=0, keepdims=True)
        out = [middle, spread]
        if layer == 3:
            ones = acc[2 * grids : 3 * grids]
            out.append(to_row(ones) * (1.0 / keep_rate))
            out.append(to_row(acc[3 * grids : 4 * grids] + away * ones) * (1.0 / keep_rate))
        if layer == 0:
            out += [to_row(acc[2 * grids : 3 * grids]), to_row(acc[3 * grids : 4 * grids])]
        for k, row in enumerate(out):
            sums_out[:, k : k + 1, :] = jnp.broadcast_to(row[None], (devices, 1, LANES))

    pipeline(grids, lo, hi, taps, weight, width, prepare, emit, after, finish)


def back_consts(layer, geo, stats, sums, gains):
    center, inv = norm_consts(stats, geo["D"])
    if layer == 3:
        one, two = top_sums(stats, center, inv)
    else:
        total = jnp.sum(sums[...], axis=0)
        one, two = total[0:1], total[1:2]
    pixels = float(geo["D"] * geo["G"] * geo["R"] * geo["C"])
    scale = inv * gains[layer : layer + 1, :]
    tilt = scale * inv * two * (-1.0 / pixels)
    flat = scale * one * (-1.0 / pixels) - center * tilt
    return center, inv, scale * (1.0 / keep_rate), flat, tilt


def through(p, dn, scale, flat, tilt):
    s = sigmoid(p)
    act = p * s
    return (dn * scale + act * tilt + flat) * (s + act * (1.0 - s)), act


def weight_term(geo, low, g, right, acc):
    rows, cols = geo["R"], geo["C"]
    parts = [low[s, g, r : r + rows] for r in range(3) for s in range(3)]
    spread = jnp.concatenate(parts, axis=-1).reshape(rows * cols, 9 * LANES)
    term = lax.dot_general(right, spread, (((0,), (0,)), ((), ())), preferred_element_type=F32)
    if g == 0:
        acc[...] = term
    else:
        acc[...] += term


def split_halves(info, acc, keep_half, send_half):
    half = 9 * LANES // 2

    def give(out):
        def act(upper):
            start = half if upper else 0
            for t in range(9):
                lo, hi = max(t * LANES, start), min((t + 1) * LANES, start + half)
                if lo < hi:
                    block = acc[:, t * LANES : (t + 1) * LANES].T
                    out[lo - start : hi - start] = block[lo - t * LANES : hi - t * LANES]
        return act

    both_ways(info[1], give(keep_half), give(send_half))


def backward_kernel(layer, geo, *refs):
    grids, rows, devices, width, cols = geo["G"], geo["R"], geo["D"], geo["CE"], geo["C"]
    heights = geo["heights"]
    refs = list(refs)
    info, gains, offsets, weight, stats, sums, pre, low = (refs.pop(0) for _ in range(8))
    masked = keep_top = field = cot = z_in = None
    if layer == 3:
        masked, keep_top, field = [refs.pop(0), refs.pop(0)], refs.pop(0), refs.pop(0)
    else:
        z_in = refs.pop(0)
    if layer == 2:
        cot = [refs.pop(0), refs.pop(0)]
    keep = [refs.pop(0), refs.pop(0)]
    stats_below, pre_below = refs.pop(0), refs.pop(0)
    sums_out, keep_half, send_half, z_out = (refs.pop(0) for _ in range(4))
    grad_out = refs.pop(0) if layer == 2 else None
    result = refs.pop(0) if layer == 3 else None
    taps, term = refs[:2]
    if layer == 3:
        result_out, (result, sems) = result, refs[2:]
        leaving = [pltpu.make_async_copy(result.at[g], result_out.at[g], sems.at[g]) for g in range(grids)]
    lo, hi = EXT - layer, EXT + rows + layer
    keep_off = EXT - heights[layer]

    center, inv, scale, flat, tilt = back_consts(layer, geo, stats, sums, gains)
    first_row, last_row = info[2], info[3]
    center_b, inv_b = norm_consts(stats_below, devices)
    sums_here = [None] * 4

    if layer == 3:
        lift = inv * gains[layer : layer + 1, :] * (1.0 / keep_rate)
        base = offsets[layer : layer + 1, :] * (1.0 / keep_rate) - center * lift

    def prepare(g, r):
        if layer == 3:
            z = across(masked, g, pl.ds(r - (EXT - heights[4]), 2))
        else:
            z = z_in[g, pl.ds(r, 2)]
        value, act = through(pre[g, pl.ds(r, 2)], z, scale, flat, tilt)
        if not (isinstance(r, int) and EXT <= r and r + 2 <= EXT + rows):
            real = [jnp.where((r + k >= first_row) & (r + k < last_row), 1.0, 0.0).astype(F32) for k in range(2)]
            value = jnp.stack([value[0] * real[0], value[1] * real[1]])
        store_shifted(taps, g, r, value, width)
        if layer == 3:
            def save():
                y = (act[:, 0:cols] * lift + base) * keep_top[g, pl.ds(r - EXT, 2)].astype(F32)
                result[g, pl.ds(r - EXT, 2)] = (field[g, pl.ds(r - EXT + 1, 2)] + y).astype(LOW)

            guard((r >= EXT) & (r < EXT + rows), save)

    def emit(g, r, part):
        inner = EXT <= r < EXT + rows
        if layer == 2:
            part = part + across(cot, g, r - (EXT - heights[5]))
            if inner:
                grad_out[g, r - EXT] = part[0:cols]
        z = part * across(keep, g, r - keep_off)
        z_out[g, r] = z
        if inner:
            z = z[0:cols]
            p = pre_below[g, r, 0:cols, :]
            s = sigmoid(p)
            act = p * s
            gather(sums_here, 0, fold(z))
            gather(sums_here, 1, fold(z * (act - center_b)))
            if layer == 1:
                gather(sums_here, 3, fold(z * (s + act * (1.0 - s))))

    def inside(g):
        return taps[g, 1, EXT : EXT + rows, 0:cols, :].reshape(rows * cols, LANES)

    def after(g):
        if layer == 3:
            leaving[g].start()
        gather(sums_here, 2, fold(inside(g).astype(F32)))

    def weight_steps(first, push, totals):
        depth = 2 * LANES // cols
        steps = []
        for g in (first, first + 1):
            for at in range(0, rows, depth):
                turned = []

                def act(n, g=g, at=at, turned=turned):
                    if not turned:
                        block = taps[g, 1, EXT + at : EXT + at + depth, 0:cols, :].reshape(2 * LANES, LANES)
                        turned.append(block.T)
                    halves = []
                    for tap in (2 * n, 2 * n + 1):
                        r, s = divmod(min(tap, 8), 3)
                        halves.append(low[s, g, at + r : at + r + depth].reshape(2 * LANES, LANES))
                    staged = push(n % 2, jnp.concatenate(halves, axis=-1))
                    pltpu.matmul_acc_lhs(totals[n], turned[0], load_staged_rhs=staged)

                steps += [functools.partial(act, n) for n in range(5)]
        return steps

    def take_term(totals):
        def act(n):
            both = pltpu.matmul_pop(totals[n])
            for tap in range(2 * n, min(2 * n + 2, 9)):
                at = (tap - 2 * n) * LANES
                term[tap * LANES : (tap + 1) * LANES] = both[:, at : at + LANES].T

        return [functools.partial(act, n) for n in range(5)]

    def finish():
        half = 9 * LANES // 2
        start = pl.multiple_of((1 - info[1]) * half, 8)
        keep_half[...] = term[pl.ds(start, half)]
        send_half[...] = term[pl.ds(pl.multiple_of(half - start, 8), half)]
        out = [to_row(sums_here[k]) for k in range(4 if layer == 1 else 3)]
        out[0] = out[0] * (1.0 / keep_rate)
        out[1] = out[1] * inv_b * (1.0 / keep_rate)
        if layer == 1:
            out[3] = out[3] * (1.0 / keep_rate)
        for k, row in enumerate(out):
            sums_out[:, k : k + 1, :] = jnp.broadcast_to(row[None], (devices, 1, LANES))
        if layer == 3:
            for c in leaving:
                c.wait()

    totals = [pltpu.ACC(n % 2)((LANES, 2 * LANES), F32) for n in range(5)]
    pipeline(grids, lo, hi, taps, weight, width, prepare, emit, after, finish, weight_steps, take_term, totals)


def first_weight_kernel(geo, *refs):
    grids, rows, width, cols = geo["G"], geo["R"], geo["CE"], geo["C"]
    info, gains, stats, sums, pre, low, z_in, sent, keep_half, send_both, dpre, acc = refs
    half = 9 * LANES // 2
    send_both[0:half] = sent[...]
    scale, flat, tilt = back_consts(0, geo, stats, sums, gains)[2:]
    first_row, last_row = info[2], info[3]

    for g in range(grids):
        for k in range(rows + 2):
            r = EXT - 1 + k
            value, _ = through(pre[g, r], z_in[g, r], scale, flat, tilt)
            if k in (0, rows + 1):
                value = value * jnp.where((r >= first_row) & (r < last_row), 1.0, 0.0).astype(F32)
            dpre[g, k] = value.astype(LOW)
        weight_term(geo, low, g, dpre[g, 1 : rows + 1, 0:cols, :].reshape(rows * cols, LANES), acc)
    split_halves(info, acc, keep_half, send_both.at[half : 2 * half])


def input_grad_kernel(geo, weight, dpre, grad, gains, *refs):
    grids, rows, width, cols = geo["G"], geo["R"], geo["CE"], geo["C"]
    out, taps, buffer, sems = refs[7], *refs[12:]
    refs[11][...] = jnp.zeros((4, LANES), F32)
    leaving = [pltpu.make_async_copy(buffer.at[g], out.at[g], sems.at[g]) for g in range(grids)]
    def prepare(g, r):
        store_shifted(taps, g, r, dpre[g, pl.ds(r, 2)].astype(F32), width)

    def emit(g, r, part):
        buffer[g, r - 1] = grad[g, r - 1] + part

    pipeline(grids, 1, rows + 1, taps, weight, cols, prepare, emit, lambda g: leaving[g].start(), lambda: None)
    gather_rows(geo, gains, *refs[0:7], *refs[8:11])
    for c in leaving:
        c.wait()


def share_kernel(*refs):
    third, second, both, _, out = refs[4:]
    half = 9 * LANES // 2
    gots = [both[half : 2 * half], both[0:half], second[...], third[...]]
    for k in range(4):
        out[k * half : (k + 1) * half] = (refs[k][...] + gots[k]).astype(LOW)


def total_kernel(devices, got, out):
    total = jnp.sum(got[...].astype(F32), axis=0)
    out[...] = jnp.broadcast_to(total.astype(LOW)[None], out.shape)


def join_kernel(geo, other, info, block, *refs):
    out, buffer, sems = refs[-3:]
    half = 9 * LANES // 2
    upper = info[1] if other else 1 - info[1]
    start = pl.multiple_of(upper * half, 8)
    leaving = [pltpu.make_async_copy(buffer.at[k], out.at[k, pl.ds(start, half)], sems.at[k]) for k in range(4)]
    for k in range(4):
        buffer[k] = block[k].astype(F32)
        leaving[k].start()
    for c in leaving:
        c.wait()


def gather_rows(geo, gains, *refs):
    stats, sums = refs[0:4], refs[4:7]
    bias_out, gain_out, offset_out = refs[7:]
    for layer in range(4):
        center, inv = norm_consts(stats[layer], geo["D"])
        if layer == 3:
            one, two = top_sums(stats[3], center, inv)
        else:
            total = jnp.sum(sums[layer][...], axis=0)
            one, two = total[0:1], total[1:2]
        offset_out[layer : layer + 1] = one
        gain_out[layer : layer + 1] = two
        if layer:
            bias_out[layer : layer + 1] = jnp.sum(sums[layer - 1][...], axis=0)[2:3]
        else:
            pixels = float(geo["D"] * geo["G"] * geo["R"] * geo["C"])
            slopes = jnp.sum(stats[0][...], axis=0)
            flat, lifted = slopes[2:3], (slopes[3:4] - center * slopes[2:3]) * inv
            bias_out[0:1] = inv * gains[0:1, :] * (total[3:4] - flat * one / pixels - lifted * two / pixels)


def call(kernel, operands, outs, scratch=(), flops=10**6, moved=10**6, scalars=1, final=(), small=(), outside=False, onto=None):
    space = pl.BlockSpec(memory_space=pltpu.VMEM)
    specs = [pl.BlockSpec(memory_space=pltpu.SMEM)] * scalars
    operands = list(operands)
    for k in range(scalars, len(operands)):
        if outside or k == onto:
            specs.append(pl.BlockSpec(memory_space=pltpu.HBM))
            operands[k] = pltpu.with_memory_space_constraint(operands[k], pltpu.HBM)
        else:
            specs.append(space)
            operands[k] = pltpu.with_memory_space_constraint(operands[k], pltpu.VMEM)
    plain = set(final) | set(small)
    shapes = [jax.ShapeDtypeStruct(s, d) if k in plain else pltpu.VMEM(s, d) for k, (s, d) in enumerate(outs)]
    places = [pl.BlockSpec(memory_space=pltpu.HBM) if k in final else space for k in range(len(outs))]
    return pl.pallas_call(
        kernel,
        in_specs=specs,
        out_specs=places,
        input_output_aliases={} if onto is None else {onto: 0},
        out_shape=shapes,
        scratch_shapes=[v if hasattr(v, "shape") and not isinstance(v, tuple) else pltpu.VMEM(*v) for v in scratch],
        compiler_params=pltpu.CompilerParams(vmem_limit_bytes=10 * 2**20),
        cost_estimate=pl.CostEstimate(flops=flops, bytes_accessed=moved, transcendentals=0),
    )(*operands)


def conv_scratch(geo, tall):
    return [((geo["G"], 3, tall, geo["CE"], LANES), LOW)]


def forward_call(layer, geo, operands):
    grids, rows, rows_ext, width, devices, cols = geo["G"], geo["R"], geo["RE"], geo["CE"], geo["D"], geo["C"]
    kinds = 4 if layer in (0, 3) else 2
    outs = [((devices, kinds, LANES), F32)]
    for k in geo["members"][layer]:
        outs.append(((grids, rows + 2 * geo["heights"][k], 2 * EXT, LANES), LOW))
    outs.append(((grids, rows_ext, width, LANES), F32))
    outs.append(((3, grids, rows + 2, cols, LANES), LOW))
    if layer == 2:
        outs.append(((grids, rows + 2, cols, LANES), F32))
    scratch = conv_scratch(geo, rows_ext) + [((grids, rows, cols, LANES), F32), ((kinds * grids, LANES), F32)]
    return call(functools.partial(forward_kernel, layer, geo), operands, outs, scratch, 2 * 10**9, 8 * 10**6)


def backward_call(layer, geo, operands):
    grids, rows, rows_ext, width, devices, cols = geo["G"], geo["R"], geo["RE"], geo["CE"], geo["D"], geo["C"]
    half = ((9 * LANES // 2, LANES), F32)
    outs = [((devices, 4 if layer == 1 else 3, LANES), F32), half, half, ((grids, rows_ext, width, LANES), F32)]
    if layer == 2:
        outs.append(((grids, rows, cols, LANES), F32))
    if layer == 3:
        outs.append(((grids, rows, cols, LANES), LOW))
    scratch = conv_scratch(geo, rows_ext) + [((9 * LANES, LANES), F32)]
    if layer == 3:
        scratch += [((grids, rows, cols, LANES), LOW), pltpu.SemaphoreType.DMA((grids,))]
    return call(
        functools.partial(backward_kernel, layer, geo), operands, outs, scratch, 3 * 10**9, 8 * 10**6,
        final=(4,) if layer == 3 else (),
    )


def local(inputs, kernels, biases, gains, offsets, keep_masks, cotangent):
    grids, rows, cols, _ = inputs.shape
    devices = lax.axis_size("batch") * lax.axis_size("lat") * lax.axis_size("lon")
    heights = [EXT, 7, 6, 5, 4, 2]
    above = rows + 2 * heights[3]
    starts = [0, above, above + heights[4] - heights[5]]
    geo = dict(
        G=grids, R=rows, C=cols, D=devices, RE=rows + 2 * EXT, CE=cols + 2 * EXT, heights=heights,
        starts=[[0], [0], [0], starts], members=[[0], [1], [2], [3, 4, 5]],
    )
    lat, lon = lax.axis_index("lat"), lax.axis_index("lon")
    info = jnp.stack(
        [
            1 - lax.rem(lat, 2),
            1 - lax.rem(lon, 2),
            jnp.where(lat == 0, EXT, 0),
            jnp.where(lat == lax.axis_size("lat") - 1, EXT + rows, rows + 2 * EXT),
        ]
    ).astype(jnp.int32)
    kernels = kernels.reshape(4, 9, LANES, LANES)

    def block(tall, wide):
        return ((grids, tall, wide, LANES), LOW)

    x_height, soon, late = heights[0], heights[1], sum(heights[2:])
    pair_sems = pltpu.SemaphoreType.DMA((2,))
    outs = call(
        functools.partial(field_edge_kernel, geo), [info, inputs], [block(x_height, cols)] * 2, [pair_sems], outside=True
    )
    x_got = trade(outs, "lat", False)
    outs = call(
        functools.partial(mask_edge_kernel, geo), [info, keep_masks], [block(soon, cols)] * 2,
        [((2, grids, soon, cols, LANES), jnp.int32), pair_sems], outside=True,
    )
    soon_got = trade(outs, "lat", False)

    def weights_for(which, before):
        outs = [((12 * LANES, 2 * LANES), LOW)] * len(which)
        return list(call(functools.partial(weights_kernel, which), [kernels, before], outs, scalars=0))

    weights = weights_for([(0, False), (1, False)], outs[0])
    outs = call(
        functools.partial(tall_kernel, geo, heights[:1]), [info, inputs, *x_got],
        [block(rows + 2 * x_height, cols)] + [block(rows + 2 * x_height, EXT)] * 2,
    )
    pieces = [[outs[0], *trade(outs[1:3], "lon", True)]]
    outs = call(functools.partial(mask_kernel, geo), [keep_masks, cotangent], [block(rows, cols)] * 5, scalars=0)
    low_masks, masked = list(outs[0:4]), outs[4]
    outs = call(
        functools.partial(tall_kernel, geo, heights[1:2]), [info, low_masks[0], *soon_got],
        [block(rows + 2 * soon, cols)] + [block(rows + 2 * soon, EXT)] * 2,
    )
    pieces.append([outs[0], *trade(outs[1:3], "lon", True)])
    edges = call(
        functools.partial(cut_kernel, geo), [info, low_masks[1], low_masks[2], masked, cotangent, outs[1]],
        [block(late, cols)] * 2,
    )
    late_got = trade(edges, "lat", False)
    talls = [rows + 2 * h for h in heights[2:]]

    pres, lows, stats, exts = [None] * 4, [None] * 4, [None] * 4, [None] * 6
    field = order = None
    for layer in range(4):
        operands = [info, gains, offsets, biases, weights[layer]]
        if layer:
            operands += [stats[layer - 1], pres[layer - 1]]
        if layer == 2:
            operands += exts[0]
        operands += pieces[layer]
        if layer in (1, 2):
            operands.append(order)
        outs = list(forward_call(layer, geo, operands))
        part = outs.pop(0)
        if layer < 2:
            beside = []
            if layer == 0:
                weights += weights_for([(2, False), (3, False), (0, True), (1, True), (2, True), (3, True)], part)
                beside = weights[2:]
            (part,) = call(gate_kernel, [part] + pieces[layer + 1][1:] + beside, [(part.shape, F32)], scalars=0)
        stats[layer] = to_all(part)
        if layer == 0:
            ends = call(
                functools.partial(late_kernel, geo), [info] + low_masks[1:3] + [masked, cotangent, *late_got, stats[0]],
                [block(t, cols) for t in talls] + [block(talls[0], EXT)] * 2,
            )
            pieces.append([ends[0], *trade(ends[4:6], "lon", True)])
            order = ends[4]
        if layer == 1:
            edges = call(
                functools.partial(last_kernel, geo), [info, *ends[1:4], stats[1]], [block(talls[1] + talls[2], EXT)] * 2
            )
            pieces.append([*ends[1:4], *trade(edges, "lon", True)])
            order = edges[0]
        for n, k in enumerate(geo["members"][layer]):
            exts[k] = [pieces[layer][n], outs.pop(0)]
        pres[layer], lows[layer] = outs.pop(0), outs.pop(0)
        if layer == 2:
            field = outs.pop(0)

    sums = [None] * 4
    sums[3] = stats[3]
    kept, got = [None] * 4, []
    z = grad = output = None
    for layer in (3, 2, 1):
        operands = [info, gains, offsets, weights[4 + layer], stats[layer], sums[layer], pres[layer], lows[layer]]
        operands += [*exts[4], low_masks[3], field] if layer == 3 else [z]
        if layer == 2:
            operands += exts[5]
        operands += [*exts[layer], stats[layer - 1], pres[layer - 1]]
        outs = backward_call(layer, geo, operands)
        sums[layer - 1] = to_all(outs[0])
        kept[layer], sent = outs[1], outs[2]
        if layer > 1:
            got.append(to_pair(sent))
        z = outs[3]
        if layer == 2:
            grad = outs[4]
        if layer == 3:
            output = outs[4]
    half = 9 * LANES // 2
    term = ((half, LANES), F32)
    kept[0], sent, dpre = call(
        functools.partial(first_weight_kernel, geo), [info, gains, stats[0], sums[0], pres[0], lows[0], z, sent],
        [term, ((2 * half, LANES), F32), block(rows + 2, cols + 2 * EXT)], [((LANES, 9 * LANES), F32)], 10**9, 8 * 10**6,
    )
    got.append(to_pair(sent))

    small = ((4, LANES), F32)
    field_like = ((grids, rows, cols, LANES), F32)
    input_grad, bias_grad, gain_grad, offset_grad, order = call(
        functools.partial(input_grad_kernel, geo), [weights[4], dpre, grad, gains] + stats + sums[:3],
        [field_like] + [small] * 4, conv_scratch(geo, rows + 2) + [field_like, pltpu.SemaphoreType.DMA((grids,))],
        10**9, 3 * 10**6, scalars=0, final=(0,), small=(1, 2, 3),
    )

    (shares,) = call(share_kernel, kept + got + [order], [((4 * half, LANES), LOW)], scalars=0)
    slots = (devices // 2, 4 * half // (devices // 2), LANES)
    arrived = to_half(shares.reshape(slots), devices)
    (mine,) = call(functools.partial(total_kernel, devices), [arrived], [(slots, LOW)], scalars=0)
    mine = to_half(mine, devices).reshape(4, half, LANES)
    other = to_pair(mine)
    whole = [((4, 9 * LANES, LANES), F32)]
    scratch = [((4, half, LANES), F32), pltpu.SemaphoreType.DMA((4,))]
    (kernel_grad,) = call(functools.partial(join_kernel, geo, False), [info, mine], whole, scratch, final=(0,))
    (kernel_grad,) = call(
        functools.partial(join_kernel, geo, True), [info, other, kernel_grad], whole, scratch, final=(0,), onto=2
    )
    return (output, input_grad, kernel_grad.reshape(4, 3, 3, LANES, LANES), bias_grad, gain_grad, offset_grad)


def solution(mesh):
    in_specs = (
        P("batch", "lat", "lon", None),
        P(),
        P(),
        P(),
        P(),
        P(None, "batch", "lat", "lon", None),
        P("batch", "lat", "lon", None),
    )
    out_specs = (P("batch", "lat", "lon", None), P("batch", "lat", "lon", None), P(), P(), P(), P())
    return jax.shard_map(local, mesh=mesh, in_specs=in_specs, out_specs=out_specs, check_vma=False)
```

```python
import functools

import jax
import jax.numpy as jnp
from jax import lax
from jax.experimental import pallas as pl
from jax.experimental.pallas import tpu as pltpu
from jax.sharding import PartitionSpec as P

eps = 1e-05
keep_rate = 0.9
EVERY = ("batch", "lat", "lon")
EXT = 8
LANES = 128
F32 = jnp.float32
LOW = jnp.bfloat16


def partners(axis, periodic):
    count = lax.axis_size(axis)
    first = [(i, i ^ 1) for i in range(count)]
    second = []
    for i in range(count):
        j = i + 1 if i % 2 else i - 1
        if periodic:
            second.append((i, j % count))
        elif 0 <= j < count:
            second.append((i, j))
    return first, second


def trade(pair, axis, periodic):
    first, second = partners(axis, periodic)
    return lax.ppermute(pair[0], axis, first), lax.ppermute(pair[1], axis, second)


def to_all(rows):
    return lax.all_to_all(rows, EVERY, 0, 0)


def to_half(rows, devices):
    groups = [[i for i in range(devices) if i % 2 == side] for side in range(2)]
    return lax.all_to_all(rows, EVERY, 0, 0, axis_index_groups=groups)


def to_pair(block):
    return lax.ppermute(block, "lon", partners("lon", True)[0])


def sigmoid(v):
    return 0.5 * jnp.tanh(0.5 * v) + 0.5


def silu(v):
    half = 0.5 * v
    return half + half * jnp.tanh(half)


def norm_consts(stats_ref, devices):
    stats = stats_ref[...]
    total = jnp.sum(stats, axis=0)
    center = total[0:1] * (1.0 / devices)
    apart = jnp.sum(jnp.square(stats - center[None]), axis=0)
    spread = (total[1:2] + apart[0:1]) * (1.0 / devices)
    return center, lax.rsqrt(spread + eps)


def top_sums(stats_ref, center, inv):
    stats = stats_ref[...]
    total = jnp.sum(stats, axis=0)
    apart = stats[:, 0:1, :] - center[None]
    return total[2:3], (total[3:4] + jnp.sum(apart * stats[:, 2:3, :], axis=0)) * inv


def shifted(value, width):
    return pltpu.roll(value, 1, 1), value, pltpu.roll(value, width - 1, 1)


def store_shifted(taps, slot, row, value, width, inner=None):
    for s, part in enumerate(shifted(value, width)):
        part = part.astype(LOW)
        taps[slot, s, pl.ds(row, 2)] = part
        if inner is not None:
            for k in range(2):
                at = row + k - (EXT - 1)
                if 0 <= at < inner.shape[2]:
                    inner[s, slot, at] = part[k, 0 : inner.shape[3]]


def lay_weights(kernel_ref, layer, back, out):
    blank = jnp.zeros((3 * LANES, LANES), LOW)
    out[9 * LANES : 12 * LANES, 0:LANES] = blank
    out[0 : 3 * LANES, LANES : 2 * LANES] = blank
    for r in range(3):
        for s in range(3):
            if back:
                block = kernel_ref[layer, (2 - r) * 3 + 2 - s].astype(F32).T.astype(LOW)
            else:
                block = kernel_ref[layer, r * 3 + s]
            at = (r * 3 + s) * LANES
            out[at : at + LANES, 0:LANES] = block
            out[at + 3 * LANES : at + 4 * LANES, LANES : 2 * LANES] = block


def even_parts(lo, hi, most):
    pairs = (hi - lo) // 2
    count = -(-pairs // most)
    out = []
    for k in range(count):
        start, stop = pairs * k // count, pairs * (k + 1) // count
        out.append((lo + 2 * start, stop - start))
    return out


def pusher():
    staged = [0, 0]

    def push(unit, tile):
        staged[unit] = 1 - staged[unit]
        pltpu.matmul_push_rhs(tile, staged[unit], unit)
        return staged[unit]

    return push


def pipeline(grids, lo, hi, taps, weight, cols, prepare, emit, after, finish, extra=None, take=None, extra_totals=()):
    parts = even_parts(lo, hi, 5)
    count = len(parts)

    def body(*refs):
        totals, more = refs[: 2 * count], refs[2 * count :]
        push = pusher()

        def operand(g, part, k):
            start, size = parts[part]
            halves = []
            for unit in (2 * k, 2 * k + 1):
                t, s = divmod(unit, 3)
                halves.append(jnp.concatenate([taps[g, s, start - 1 + t + 2 * n, 0:cols, :] for n in range(size)], axis=0))
            return jnp.concatenate(halves, axis=-1)

        def product(first, unit, part, k):
            def act():
                at = push(unit, weight[k * 2 * LANES : (k + 1) * 2 * LANES, :])
                pltpu.matmul_acc_lhs(totals[unit * count + part], operand(first + unit, part, k), load_staged_rhs=at)
            return act

        def collect(first, part):
            def act():
                start, size = parts[part]
                for unit in range(2):
                    both = pltpu.matmul_pop(totals[unit * count + part])
                    for n in range(size):
                        for h in range(2):
                            emit(first + unit, start + 2 * n + h, both[n * cols : (n + 1) * cols, h * LANES : (h + 1) * LANES])
            return act

        def rows_before(part):
            start, size = parts[part]
            return start + 2 * size + 1

        def ready(first, start, stop):
            return [functools.partial(prepare, first + unit, r) for r in range(start, stop, 2) for unit in range(2)]

        for task in ready(0, lo - 1, rows_before(0)):
            task()
        waiting = []

        def run(steps, tasks):
            done = 0
            for n, step in enumerate(steps):
                step()
                if n == 3:
                    while waiting:
                        waiting.pop(0)()
                while done < len(tasks) * (n + 1) // len(steps):
                    tasks[done]()
                    done += 1

        for first in range(0, grids, 2):
            last = first + 2 >= grids
            ahead = [] if last else ready(first + 2, lo - 1, hi + 1)
            if extra and last:
                run(extra(first, push, more), [])
                ahead = take(more)
            for part in range(count):
                tasks = []
                if first == 0 and part + 1 < count:
                    tasks += ready(0, rows_before(part), rows_before(part + 1))
                tasks += ahead[len(ahead) * part // count : len(ahead) * (part + 1) // count]
                run([product(first, unit, part, k) for k in range(6) for unit in range(2)], tasks)
                waiting.append(collect(first, part))
            waiting += [functools.partial(after, first + unit) for unit in range(2)]
            if extra and not last:
                run(extra(first, push, more), [])
        while waiting:
            waiting.pop(0)()
        finish()

    totals = [pltpu.ACC(unit)((size * cols, 2 * LANES), F32) for unit in range(2) for _, size in parts]
    pl.run_scoped(body, *totals, *extra_totals)


def guard(condition, act):
    if isinstance(condition, bool):
        if condition:
            act()
    else:
        pl.when(condition)(act)


def gather(sums, k, value):
    sums[k] = value if sums[k] is None else sums[k] + value


def fold(value):
    return jnp.sum(value.reshape(-1, 8, LANES), axis=0)


def to_row(value):
    return jnp.sum(value, axis=0, keepdims=True)


def both_ways(even, give_first, give_second):
    @pl.when(even == 1)
    def _():
        give_first(False)
        give_second(True)

    @pl.when(even == 0)
    def _():
        give_first(True)
        give_second(False)


def whichever(even, place, got_first, got_second):
    @pl.when(even == 1)
    def _():
        place(got_second, got_first)

    @pl.when(even == 0)
    def _():
        place(got_first, got_second)


def cut_rows(geo, info, sources, heights, first, second):
    grids, rows = geo["G"], geo["R"]

    def give(out):
        def act(low):
            at = 0
            for src, h in zip(sources, heights):
                for g in range(grids):
                    out[g, at : at + h] = src[g, 0:h] if low else src[g, src.shape[1] - h :]
                at += h
        return act

    both_ways(info[0], give(first), give(second))


def cut_cols(geo, info, sources, first, second):
    grids, cols = geo["G"], geo["C"]

    def give(out):
        def act(low):
            at = 0
            for src in sources:
                for g in range(grids):
                    part = src[g, :, 0:EXT, :] if low else src[g, :, cols - EXT : cols, :]
                    out[g, at : at + src.shape[1]] = part
                at += src.shape[1]
        return act

    both_ways(info[1], give(first), give(second))


def add_rows(geo, info, sources, heights, got_first, got_second, outs):
    grids, rows = geo["G"], geo["R"]

    def place(low, high):
        at = 0
        for out, h in zip(outs, heights):
            for g in range(grids):
                out[g, 0:h] = low[g, at : at + h]
                out[g, h + rows : 2 * h + rows] = high[g, at : at + h]
            at += h

    whichever(info[0], place, got_first, got_second)
    for src, out, h in zip(sources, outs, heights):
        for g in range(grids):
            out[g, h : h + rows] = src[g]


def add_sides(geo, info, starts, got_first, got_second, outs):
    def place(low, high):
        for n, (out, at) in enumerate(zip(outs, starts)):
            total = out.shape[1]
            for g in range(geo["G"]):
                right = high[g, at : at + total].astype(F32)
                left = low[g, at : at + total].astype(F32)
                if n == 2:
                    right, left = pltpu.roll(right, EXT // 2, 1), pltpu.roll(left, EXT // 2, 1)
                out[g] = jnp.concatenate([right, left], axis=1).astype(LOW)

    whichever(info[1], place, got_first, got_second)


def across(pair, g, rows):
    parts = [ref[g, rows].astype(F32) for ref in pair]
    return jnp.concatenate(parts, axis=parts[0].ndim - 2)


def field_edge_kernel(geo, info, x, first, second, sems):
    rows = geo["R"]

    def fetch(high_out, low_out):
        copies = [
            pltpu.make_async_copy(x.at[:, rows - EXT : rows], high_out, sems.at[0]),
            pltpu.make_async_copy(x.at[:, 0:EXT], low_out, sems.at[1]),
        ]
        for c in copies:
            c.start()
        for c in copies:
            c.wait()

    @pl.when(info[0] == 1)
    def _():
        fetch(first, second)

    @pl.when(info[0] == 0)
    def _():
        fetch(second, first)


def mask_edge_kernel(geo, info, masks, first, second, near, sems):
    rows, height = geo["R"], geo["heights"][1]
    nears = [
        pltpu.make_async_copy(masks.at[0, :, 0:height], near.at[0], sems.at[0]),
        pltpu.make_async_copy(masks.at[0, :, rows - height : rows], near.at[1], sems.at[1]),
    ]
    for c in nears:
        c.start()
    for c in nears:
        c.wait()

    def give(out):
        def act(low):
            out[...] = near[0 if low else 1].astype(F32).astype(LOW)
        return act

    both_ways(info[0], give(first), give(second))


def tall_kernel(geo, heights, info, *refs):
    n = len(heights)
    talls = refs[n + 2 : 2 * n + 2]
    add_rows(geo, info, refs[:n], heights, refs[n], refs[n + 1], talls)
    cut_cols(geo, info, talls, refs[2 * n + 2], refs[2 * n + 3])


def mask_kernel(geo, masks, cot, *outs):
    for g in range(geo["G"]):
        for k in range(4):
            outs[k][g] = masks[k, g].astype(F32).astype(LOW)
        outs[4][g] = (cot[g].astype(F32) * masks[3, g].astype(F32)).astype(LOW)


def cut_kernel(geo, info, mask1, mask2, masked, cot, before, first, second):
    del before
    cut_rows(geo, info, [mask1, mask2, masked, cot], geo["heights"][2:], first, second)


def weights_kernel(which, kernels, before, *outs):
    del before
    for (layer, back), out in zip(which, outs):
        lay_weights(kernels, layer, back, out)


def late_kernel(geo, info, mask1, mask2, masked, cot, first, second, before, *outs):
    del before
    add_rows(geo, info, [mask1, mask2, masked, cot], geo["heights"][2:], first, second, outs[0:4])
    cut_cols(geo, info, outs[0:1], *outs[4:6])


def last_kernel(geo, info, tall2, tall3, tall4, before, first, second):
    del before
    cols, above, shared = geo["C"], tall2.shape[1], tall4.shape[1]
    extra = (tall3.shape[1] - shared) // 2
    cut_cols(geo, info, [tall2], first, second)

    def give(out):
        def act(low):
            at = pl.ds(0, EXT) if low else pl.ds(cols - EXT, EXT)
            place = lax.broadcasted_iota(jnp.int32, (shared, EXT, LANES), 1)
            near = place < EXT // 2 if low else place >= EXT // 2
            for g in range(geo["G"]):
                out[g, above : above + tall3.shape[1]] = tall3[g, :, at]
                mine = tall3[g, extra : extra + shared, at].astype(F32)
                other = pltpu.roll(tall4[g, :, at].astype(F32), EXT // 2, 1)
                out[g, above + extra : above + extra + shared] = jnp.where(near, mine, other).astype(LOW)
        return act

    both_ways(info[1], give(first), give(second))


def gate_kernel(sums, *refs):
    refs[-1][...] = sums[...]


def forward_kernel(layer, geo, *refs):
    grids, rows, devices, width, cols = geo["G"], geo["R"], geo["D"], geo["CE"], geo["C"]
    heights = geo["heights"]
    refs = list(refs)
    info, gains, offsets, biases, weight = (refs.pop(0) for _ in range(5))
    if layer:
        stats, pre_in = refs.pop(0), refs.pop(0)
    field = [refs.pop(0), refs.pop(0)] if layer == 2 else None
    members = geo["members"][layer]
    sources = [refs.pop(0) for _ in members]
    got = [refs.pop(0), refs.pop(0)]
    if layer in (1, 2):
        refs.pop(0)
    sums_out = refs.pop(0)
    side_outs = [refs.pop(0) for _ in members]
    pre_out, low_out = refs.pop(0), refs.pop(0)
    field_out = refs.pop(0) if layer == 2 else None
    taps, acts, acc = refs
    lo, hi = layer + 1, geo["RE"] - 1 - layer

    add_sides(geo, info, geo["starts"][layer], *got, side_outs)
    ext = [sources[0], side_outs[0]]
    if layer:
        center, inv = norm_consts(stats, devices)
        scale = inv * gains[layer - 1 : layer, :] * (1.0 / keep_rate)
        shift = offsets[layer - 1 : layer, :] * (1.0 / keep_rate) - center * scale
        scale = 0.5 * scale
    bias = biases[layer : layer + 1, :]
    number = rows * cols
    totals = [None] * grids

    def prepare(g, r):
        if layer == 0:
            value = across(ext, g, pl.ds(r, 2))
        else:
            p = pre_in[g, pl.ds(r, 2)]
            part = p * scale
            value = (part + part * jnp.tanh(0.5 * p) + shift) * across(ext, g, pl.ds(r - layer, 2))
            if layer == 2:
                value = value + across(field, g, pl.ds(r, 2))

                def save():
                    field_out[g, pl.ds(r - (EXT - 1), 2)] = value[:, 0:cols, :]

                guard((r >= EXT - 1) & (r < EXT + rows), save)
        store_shifted(taps, g, r, value, width, low_out)

    def emit(g, r, part):
        part = part + bias
        pre_out[g, r] = part
        if EXT <= r < EXT + rows:
            act = silu(part[0:cols])
            acts[g, r - EXT] = act
            gather(totals, g, fold(act))

    def after(g):
        mean = to_row(totals[g]) * (1.0 / number)
        square = jnp.zeros((8, LANES), F32)
        first = jnp.zeros((8, LANES), F32)
        second = jnp.zeros((8, LANES), F32)
        for k in range(rows):
            act = acts[g, k]
            apart = act - mean
            square = square + fold(jnp.square(apart))
            if layer == 3:
                z = sources[1][g, heights[4] + k].astype(F32)
                first = first + fold(z)
                second = second + fold(z * apart)
            if layer == 0:
                p = pre_out[g, EXT + k, 0:cols, :]
                s = sigmoid(p)
                slope = s + act * (1.0 - s)
                first = first + fold(slope)
                second = second + fold(slope * act)
        acc[g : g + 1] = mean
        acc[grids + g : grids + g + 1] = to_row(square) * (1.0 / number)
        if layer in (0, 3):
            acc[2 * grids + g : 2 * grids + g + 1] = to_row(first)
            acc[3 * grids + g : 3 * grids + g + 1] = to_row(second)

    def finish():
        means = acc[0:grids]
        middle = jnp.mean(means, axis=0, keepdims=True)
        away = means - middle
        spread = jnp.mean(acc[grids : 2 * grids] + jnp.square(away), axis=0, keepdims=True)
        out = [middle, spread]
        if layer == 3:
            ones = acc[2 * grids : 3 * grids]
            out.append(to_row(ones) * (1.0 / keep_rate))
            out.append(to_row(acc[3 * grids : 4 * grids] + away * ones) * (1.0 / keep_rate))
        if layer == 0:
            out += [to_row(acc[2 * grids : 3 * grids]), to_row(acc[3 * grids : 4 * grids])]
        for k, row in enumerate(out):
            sums_out[:, k : k + 1, :] = jnp.broadcast_to(row[None], (devices, 1, LANES))

    pipeline(grids, lo, hi, taps, weight, width, prepare, emit, after, finish)


def back_consts(layer, geo, stats, sums, gains):
    center, inv = norm_consts(stats, geo["D"])
    if layer == 3:
        one, two = top_sums(stats, center, inv)
    else:
        total = jnp.sum(sums[...], axis=0)
        one, two = total[0:1], total[1:2]
    pixels = float(geo["D"] * geo["G"] * geo["R"] * geo["C"])
    scale = inv * gains[layer : layer + 1, :]
    tilt = scale * inv * two * (-1.0 / pixels)
    flat = scale * one * (-1.0 / pixels) - center * tilt
    return center, inv, scale * (1.0 / keep_rate), flat, tilt


def through(p, dn, scale, flat, tilt):
    s = sigmoid(p)
    act = p * s
    return (dn * scale + act * tilt + flat) * (s + act * (1.0 - s)), act


def weight_totals():
    return [pltpu.ACC(n % 2)((LANES, 2 * LANES), F32) for n in range(5)]


def weight_steps(geo, low, inside, first, push, totals):
    rows, cols = geo["R"], geo["C"]
    depth = 2 * LANES // cols
    steps = []
    for g in (first, first + 1):
        for at in range(0, rows, depth):
            turned = []

            def act(n, g=g, at=at, turned=turned):
                if not turned:
                    turned.append(inside(g, at, depth).reshape(2 * LANES, LANES).T)
                halves = []
                for tap in (2 * n, 2 * n + 1):
                    r, s = divmod(min(tap, 8), 3)
                    halves.append(low[s, g, at + r : at + r + depth].reshape(2 * LANES, LANES))
                staged = push(n % 2, jnp.concatenate(halves, axis=-1))
                pltpu.matmul_acc_lhs(totals[n], turned[0], load_staged_rhs=staged)

            steps += [functools.partial(act, n) for n in range(5)]
    return steps


def take_term(term, totals):
    def act(n):
        both = pltpu.matmul_pop(totals[n])
        for tap in range(2 * n, min(2 * n + 2, 9)):
            at = (tap - 2 * n) * LANES
            term[tap * LANES : (tap + 1) * LANES] = both[:, at : at + LANES].T

    return [functools.partial(act, n) for n in range(5)]


def split_halves(info, term, keep_half, send_half):
    half = 9 * LANES // 2
    start = pl.multiple_of((1 - info[1]) * half, 8)
    keep_half[...] = term[pl.ds(start, half)]
    send_half[...] = term[pl.ds(pl.multiple_of(half - start, 8), half)]


def backward_kernel(layer, geo, *refs):
    grids, rows, devices, width, cols = geo["G"], geo["R"], geo["D"], geo["CE"], geo["C"]
    heights = geo["heights"]
    refs = list(refs)
    info, gains, offsets, weight, stats, sums, pre, low = (refs.pop(0) for _ in range(8))
    masked = keep_top = field = cot = z_in = None
    if layer == 3:
        masked, keep_top, field = [refs.pop(0), refs.pop(0)], refs.pop(0), refs.pop(0)
    else:
        z_in = refs.pop(0)
    if layer == 2:
        cot = [refs.pop(0), refs.pop(0)]
    keep = [refs.pop(0), refs.pop(0)]
    stats_below, pre_below = refs.pop(0), refs.pop(0)
    sums_out, keep_half, send_half, z_out = (refs.pop(0) for _ in range(4))
    grad_out = refs.pop(0) if layer == 2 else None
    result = refs.pop(0) if layer == 3 else None
    taps, term = refs[:2]
    if layer == 3:
        result_out, (result, sems) = result, refs[2:]
        leaving = [pltpu.make_async_copy(result.at[g], result_out.at[g], sems.at[g]) for g in range(grids)]
    lo, hi = EXT - layer, EXT + rows + layer
    keep_off = EXT - heights[layer]

    center, inv, scale, flat, tilt = back_consts(layer, geo, stats, sums, gains)
    first_row, last_row = info[2], info[3]
    center_b, inv_b = norm_consts(stats_below, devices)
    sums_here = [None] * 4

    if layer == 3:
        lift = inv * gains[layer : layer + 1, :] * (1.0 / keep_rate)
        base = offsets[layer : layer + 1, :] * (1.0 / keep_rate) - center * lift

    def prepare(g, r):
        if layer == 3:
            z = across(masked, g, pl.ds(r - (EXT - heights[4]), 2))
        else:
            z = z_in[g, pl.ds(r, 2)]
        value, act = through(pre[g, pl.ds(r, 2)], z, scale, flat, tilt)
        if not (isinstance(r, int) and EXT <= r and r + 2 <= EXT + rows):
            real = [jnp.where((r + k >= first_row) & (r + k < last_row), 1.0, 0.0).astype(F32) for k in range(2)]
            value = jnp.stack([value[0] * real[0], value[1] * real[1]])
        store_shifted(taps, g, r, value, width)
        if layer == 3:
            def save():
                y = (act[:, 0:cols] * lift + base) * keep_top[g, pl.ds(r - EXT, 2)].astype(F32)
                result[g, pl.ds(r - EXT, 2)] = (field[g, pl.ds(r - EXT + 1, 2)] + y).astype(LOW)

            guard((r >= EXT) & (r < EXT + rows), save)

    def emit(g, r, part):
        inner = EXT <= r < EXT + rows
        if layer == 2:
            part = part + across(cot, g, r - (EXT - heights[5]))
            if inner:
                grad_out[g, r - EXT] = part[0:cols]
        z = part * across(keep, g, r - keep_off)
        z_out[g, r] = z
        if inner:
            z = z[0:cols]
            p = pre_below[g, r, 0:cols, :]
            s = sigmoid(p)
            act = p * s
            gather(sums_here, 0, fold(z))
            gather(sums_here, 1, fold(z * (act - center_b)))
            if layer == 1:
                gather(sums_here, 3, fold(z * (s + act * (1.0 - s))))

    def inside(g, at, depth):
        return taps[g, 1, EXT + at : EXT + at + depth, 0:cols, :]

    def after(g):
        if layer == 3:
            leaving[g].start()
        gather(sums_here, 2, fold(inside(g, 0, rows).astype(F32)))

    def finish():
        split_halves(info, term, keep_half, send_half)
        out = [to_row(sums_here[k]) for k in range(4 if layer == 1 else 3)]
        out[0] = out[0] * (1.0 / keep_rate)
        out[1] = out[1] * inv_b * (1.0 / keep_rate)
        if layer == 1:
            out[3] = out[3] * (1.0 / keep_rate)
        for k, row in enumerate(out):
            sums_out[:, k : k + 1, :] = jnp.broadcast_to(row[None], (devices, 1, LANES))
        if layer == 3:
            for c in leaving:
                c.wait()

    steps = functools.partial(weight_steps, geo, low, inside)
    take = functools.partial(take_term, term)
    pipeline(grids, lo, hi, taps, weight, width, prepare, emit, after, finish, steps, take, weight_totals())


def first_weight_kernel(geo, *refs):
    grids, rows, cols = geo["G"], geo["R"], geo["C"]
    info, gains, stats, sums, pre, low, z_in, sent, keep_half, send_both, dpre, term = refs
    half = 9 * LANES // 2
    send_both[0:half] = sent[...]
    scale, flat, tilt = back_consts(0, geo, stats, sums, gains)[2:]
    first_row, last_row = info[2], info[3]

    def prepare(g, k):
        r = EXT - 1 + k
        value, _ = through(pre[g, r], z_in[g, r], scale, flat, tilt)
        if k in (0, rows + 1):
            value = value * jnp.where((r >= first_row) & (r < last_row), 1.0, 0.0).astype(F32)
        dpre[g, k] = value.astype(LOW)

    def ready(first):
        return [functools.partial(prepare, first + unit, k) for k in range(rows + 2) for unit in range(2)]

    def inside(g, at, depth):
        return dpre[g, 1 + at : 1 + at + depth, 0:cols, :]

    def body(*totals):
        push = pusher()
        for task in ready(0):
            task()
        for first in range(0, grids, 2):
            tasks = ready(first + 2) if first + 2 < grids else []
            steps = weight_steps(geo, low, inside, first, push, totals)
            done = 0
            for n, step in enumerate(steps):
                step()
                while done < len(tasks) * (n + 1) // len(steps):
                    tasks[done]()
                    done += 1
        for task in take_term(term, totals):
            task()
        split_halves(info, term, keep_half, send_both.at[half : 2 * half])

    pl.run_scoped(body, *weight_totals())


def input_grad_kernel(geo, weight, dpre, grad, gains, *refs):
    out, taps = refs[7], refs[11]
    grids, rows, width, cols = geo["G"], geo["R"], geo["CE"], geo["C"]

    def prepare(g, r):
        store_shifted(taps, g, r, dpre[g, pl.ds(r, 2)].astype(F32), width)

    def emit(g, r, part):
        out[g, r - 1] = grad[g, r - 1] + part

    def finish():
        gather_rows(geo, gains, *refs[0:7], *refs[8:11])

    pipeline(grids, 1, rows + 1, taps, weight, cols, prepare, emit, lambda g: None, finish)


def share_kernel(*refs):
    third, second, both, _, out = refs[4:]
    half = 9 * LANES // 2
    gots = [both[half : 2 * half], both[0:half], second[...], third[...]]
    for k in range(4):
        out[k * half : (k + 1) * half] = (refs[k][...] + gots[k]).astype(LOW)


def total_kernel(devices, got, out):
    total = jnp.sum(got[...].astype(F32), axis=0)
    out[...] = jnp.broadcast_to(total.astype(LOW)[None], out.shape)


def write_half(upper, block, out, buffer, sems):
    half = 9 * LANES // 2
    start = pl.multiple_of(upper * half, 8)
    leaving = [pltpu.make_async_copy(buffer.at[k], out.at[k, pl.ds(start, half)], sems.at[k]) for k in range(4)]
    for k in range(4):
        buffer[k] = block[k].astype(F32)
        leaving[k].start()
    return leaving


def own_half_kernel(info, block, grad, out, grad_out, buffer, sems, grad_sem):
    leaving = write_half(1 - info[1], block, out, buffer, sems)
    leaving.append(pltpu.make_async_copy(grad, grad_out, grad_sem.at[0]))
    leaving[-1].start()
    for c in leaving:
        c.wait()


def other_half_kernel(info, block, _, out, buffer, sems):
    for c in write_half(info[1], block, out, buffer, sems):
        c.wait()


def gather_rows(geo, gains, *refs):
    stats, sums = refs[0:4], refs[4:7]
    bias_out, gain_out, offset_out = refs[7:]
    for layer in range(4):
        center, inv = norm_consts(stats[layer], geo["D"])
        if layer == 3:
            one, two = top_sums(stats[3], center, inv)
        else:
            total = jnp.sum(sums[layer][...], axis=0)
            one, two = total[0:1], total[1:2]
        offset_out[layer : layer + 1] = one
        gain_out[layer : layer + 1] = two
        if layer:
            bias_out[layer : layer + 1] = jnp.sum(sums[layer - 1][...], axis=0)[2:3]
        else:
            pixels = float(geo["D"] * geo["G"] * geo["R"] * geo["C"])
            slopes = jnp.sum(stats[0][...], axis=0)
            flat, lifted = slopes[2:3], (slopes[3:4] - center * slopes[2:3]) * inv
            bias_out[0:1] = inv * gains[0:1, :] * (total[3:4] - flat * one / pixels - lifted * two / pixels)


def call(kernel, operands, outs, scratch=(), flops=10**6, moved=10**6, scalars=1, final=(), small=(), outside=False, onto=None):
    space = pl.BlockSpec(memory_space=pltpu.VMEM)
    specs = [pl.BlockSpec(memory_space=pltpu.SMEM)] * scalars
    operands = list(operands)
    for k in range(scalars, len(operands)):
        if outside or k == onto:
            specs.append(pl.BlockSpec(memory_space=pltpu.HBM))
            operands[k] = pltpu.with_memory_space_constraint(operands[k], pltpu.HBM)
        else:
            specs.append(space)
            operands[k] = pltpu.with_memory_space_constraint(operands[k], pltpu.VMEM)
    plain = set(final) | set(small)
    shapes = [jax.ShapeDtypeStruct(s, d) if k in plain else pltpu.VMEM(s, d) for k, (s, d) in enumerate(outs)]
    places = [pl.BlockSpec(memory_space=pltpu.HBM) if k in final else space for k in range(len(outs))]
    return pl.pallas_call(
        kernel,
        in_specs=specs,
        out_specs=places,
        input_output_aliases={} if onto is None else {onto: 0},
        out_shape=shapes,
        scratch_shapes=[v if hasattr(v, "shape") and not isinstance(v, tuple) else pltpu.VMEM(*v) for v in scratch],
        compiler_params=pltpu.CompilerParams(vmem_limit_bytes=10 * 2**20),
        cost_estimate=pl.CostEstimate(flops=flops, bytes_accessed=moved, transcendentals=0),
    )(*operands)


def conv_scratch(geo, tall):
    return [((geo["G"], 3, tall, geo["CE"], LANES), LOW)]


def forward_call(layer, geo, operands):
    grids, rows, rows_ext, width, devices, cols = geo["G"], geo["R"], geo["RE"], geo["CE"], geo["D"], geo["C"]
    kinds = 4 if layer in (0, 3) else 2
    outs = [((devices, kinds, LANES), F32)]
    for k in geo["members"][layer]:
        outs.append(((grids, rows + 2 * geo["heights"][k], 2 * EXT, LANES), LOW))
    outs.append(((grids, rows_ext, width, LANES), F32))
    outs.append(((3, grids, rows + 2, cols, LANES), LOW))
    if layer == 2:
        outs.append(((grids, rows + 2, cols, LANES), F32))
    scratch = conv_scratch(geo, rows_ext) + [((grids, rows, cols, LANES), F32), ((kinds * grids, LANES), F32)]
    return call(functools.partial(forward_kernel, layer, geo), operands, outs, scratch, 2 * 10**9, 8 * 10**6)


def backward_call(layer, geo, operands):
    grids, rows, rows_ext, width, devices, cols = geo["G"], geo["R"], geo["RE"], geo["CE"], geo["D"], geo["C"]
    half = ((9 * LANES // 2, LANES), F32)
    outs = [((devices, 4 if layer == 1 else 3, LANES), F32), half, half, ((grids, rows_ext, width, LANES), F32)]
    if layer == 2:
        outs.append(((grids, rows, cols, LANES), F32))
    if layer == 3:
        outs.append(((grids, rows, cols, LANES), LOW))
    scratch = conv_scratch(geo, rows_ext) + [((9 * LANES, LANES), F32)]
    if layer == 3:
        scratch += [((grids, rows, cols, LANES), LOW), pltpu.SemaphoreType.DMA((grids,))]
    return call(
        functools.partial(backward_kernel, layer, geo), operands, outs, scratch, 3 * 10**9, 8 * 10**6,
        final=(4,) if layer == 3 else (),
    )


def local(inputs, kernels, biases, gains, offsets, keep_masks, cotangent):
    grids, rows, cols, _ = inputs.shape
    devices = lax.axis_size("batch") * lax.axis_size("lat") * lax.axis_size("lon")
    heights = [EXT, 7, 6, 5, 4, 2]
    above = rows + 2 * heights[3]
    starts = [0, above, above + heights[4] - heights[5]]
    geo = dict(
        G=grids, R=rows, C=cols, D=devices, RE=rows + 2 * EXT, CE=cols + 2 * EXT, heights=heights,
        starts=[[0], [0], [0], starts], members=[[0], [1], [2], [3, 4, 5]],
    )
    lat, lon = lax.axis_index("lat"), lax.axis_index("lon")
    info = jnp.stack(
        [
            1 - lax.rem(lat, 2),
            1 - lax.rem(lon, 2),
            jnp.where(lat == 0, EXT, 0),
            jnp.where(lat == lax.axis_size("lat") - 1, EXT + rows, rows + 2 * EXT),
        ]
    ).astype(jnp.int32)
    kernels = kernels.reshape(4, 9, LANES, LANES)

    def block(tall, wide):
        return ((grids, tall, wide, LANES), LOW)

    x_height, soon, late = heights[0], heights[1], sum(heights[2:])
    pair_sems = pltpu.SemaphoreType.DMA((2,))
    outs = call(
        functools.partial(field_edge_kernel, geo), [info, inputs], [block(x_height, cols)] * 2, [pair_sems], outside=True
    )
    x_got = trade(outs, "lat", False)
    outs = call(
        functools.partial(mask_edge_kernel, geo), [info, keep_masks], [block(soon, cols)] * 2,
        [((2, grids, soon, cols, LANES), jnp.int32), pair_sems], outside=True,
    )
    soon_got = trade(outs, "lat", False)

    def weights_for(which, before):
        outs = [((12 * LANES, 2 * LANES), LOW)] * len(which)
        return list(call(functools.partial(weights_kernel, which), [kernels, before], outs, scalars=0))

    weights = weights_for([(0, False), (1, False)], outs[0])
    outs = call(
        functools.partial(tall_kernel, geo, heights[:1]), [info, inputs, *x_got],
        [block(rows + 2 * x_height, cols)] + [block(rows + 2 * x_height, EXT)] * 2,
    )
    pieces = [[outs[0], *trade(outs[1:3], "lon", True)]]
    outs = call(functools.partial(mask_kernel, geo), [keep_masks, cotangent], [block(rows, cols)] * 5, scalars=0)
    low_masks, masked = list(outs[0:4]), outs[4]
    outs = call(
        functools.partial(tall_kernel, geo, heights[1:2]), [info, low_masks[0], *soon_got],
        [block(rows + 2 * soon, cols)] + [block(rows + 2 * soon, EXT)] * 2,
    )
    pieces.append([outs[0], *trade(outs[1:3], "lon", True)])
    edges = call(
        functools.partial(cut_kernel, geo), [info, low_masks[1], low_masks[2], masked, cotangent, outs[1]],
        [block(late, cols)] * 2,
    )
    late_got = trade(edges, "lat", False)
    talls = [rows + 2 * h for h in heights[2:]]

    pres, lows, stats, exts = [None] * 4, [None] * 4, [None] * 4, [None] * 6
    field = order = None
    for layer in range(4):
        operands = [info, gains, offsets, biases, weights[layer]]
        if layer:
            operands += [stats[layer - 1], pres[layer - 1]]
        if layer == 2:
            operands += exts[0]
        operands += pieces[layer]
        if layer in (1, 2):
            operands.append(order)
        outs = list(forward_call(layer, geo, operands))
        part = outs.pop(0)
        if layer < 2:
            beside = []
            if layer == 0:
                weights += weights_for([(2, False), (3, False), (0, True), (1, True), (2, True), (3, True)], part)
                beside = weights[2:]
            (part,) = call(gate_kernel, [part] + pieces[layer + 1][1:] + beside, [(part.shape, F32)], scalars=0)
        stats[layer] = to_all(part)
        if layer == 0:
            ends = call(
                functools.partial(late_kernel, geo), [info] + low_masks[1:3] + [masked, cotangent, *late_got, stats[0]],
                [block(t, cols) for t in talls] + [block(talls[0], EXT)] * 2,
            )
            pieces.append([ends[0], *trade(ends[4:6], "lon", True)])
            order = ends[4]
        if layer == 1:
            edges = call(
                functools.partial(last_kernel, geo), [info, *ends[1:4], stats[1]], [block(talls[1] + talls[2], EXT)] * 2
            )
            pieces.append([*ends[1:4], *trade(edges, "lon", True)])
            order = edges[0]
        for n, k in enumerate(geo["members"][layer]):
            exts[k] = [pieces[layer][n], outs.pop(0)]
        pres[layer], lows[layer] = outs.pop(0), outs.pop(0)
        if layer == 2:
            field = outs.pop(0)

    sums = [None] * 4
    sums[3] = stats[3]
    kept, got = [None] * 4, []
    z = grad = output = None
    for layer in (3, 2, 1):
        operands = [info, gains, offsets, weights[4 + layer], stats[layer], sums[layer], pres[layer], lows[layer]]
        operands += [*exts[4], low_masks[3], field] if layer == 3 else [z]
        if layer == 2:
            operands += exts[5]
        operands += [*exts[layer], stats[layer - 1], pres[layer - 1]]
        outs = backward_call(layer, geo, operands)
        sums[layer - 1] = to_all(outs[0])
        kept[layer], sent = outs[1], outs[2]
        if layer > 1:
            got.append(to_pair(sent))
        z = outs[3]
        if layer == 2:
            grad = outs[4]
        if layer == 3:
            output = outs[4]
    half = 9 * LANES // 2
    term = ((half, LANES), F32)
    kept[0], sent, dpre = call(
        functools.partial(first_weight_kernel, geo), [info, gains, stats[0], sums[0], pres[0], lows[0], z, sent],
        [term, ((2 * half, LANES), F32), block(rows + 2, cols + 2 * EXT)], [((9 * LANES, LANES), F32)], 10**9, 8 * 10**6,
    )
    got.append(to_pair(sent))

    small = ((4, LANES), F32)
    field_like = ((grids, rows, cols, LANES), F32)
    input_grad, bias_grad, gain_grad, offset_grad = call(
        functools.partial(input_grad_kernel, geo), [weights[4], dpre, grad, gains] + stats + sums[:3],
        [field_like] + [small] * 3, conv_scratch(geo, rows + 2), 10**9, 3 * 10**6, scalars=0, small=(1, 2, 3),
    )

    (shares,) = call(share_kernel, kept + got + [input_grad], [((4 * half, LANES), LOW)], scalars=0)
    slots = (devices // 2, 4 * half // (devices // 2), LANES)
    arrived = to_half(shares.reshape(slots), devices)
    (mine,) = call(functools.partial(total_kernel, devices), [arrived], [(slots, LOW)], scalars=0)
    mine = to_half(mine, devices).reshape(4, half, LANES)
    other = to_pair(mine)
    whole = ((4, 9 * LANES, LANES), F32)
    scratch = [((4, half, LANES), F32), pltpu.SemaphoreType.DMA((4,))]
    kernel_grad, input_grad = call(
        own_half_kernel, [info, mine, input_grad], [whole, field_like], scratch + [pltpu.SemaphoreType.DMA((1,))], final=(0, 1)
    )
    (kernel_grad,) = call(other_half_kernel, [info, other, kernel_grad], [whole], scratch, final=(0,), onto=2)
    return (output, input_grad, kernel_grad.reshape(4, 3, 3, LANES, LANES), bias_grad, gain_grad, offset_grad)


def solution(mesh):
    in_specs = (
        P("batch", "lat", "lon", None),
        P(),
        P(),
        P(),
        P(),
        P(None, "batch", "lat", "lon", None),
        P("batch", "lat", "lon", None),
    )
    out_specs = (P("batch", "lat", "lon", None), P("batch", "lat", "lon", None), P(), P(), P(), P())
    return jax.shard_map(local, mesh=mesh, in_specs=in_specs, out_specs=out_specs, check_vma=False)
```

```python
import functools

import jax
import jax.numpy as jnp
from jax import lax
from jax.experimental import pallas as pl
from jax.experimental.pallas import tpu as pltpu
from jax.sharding import PartitionSpec as P

eps = 1e-05
keep_rate = 0.9
EVERY = ("batch", "lat", "lon")
EXT = 8
LANES = 128
F32 = jnp.float32
LOW = jnp.bfloat16


def partners(axis, periodic):
    count = lax.axis_size(axis)
    first = [(i, i ^ 1) for i in range(count)]
    second = []
    for i in range(count):
        j = i + 1 if i % 2 else i - 1
        if periodic:
            second.append((i, j % count))
        elif 0 <= j < count:
            second.append((i, j))
    return first, second


def trade(pair, axis, periodic):
    first, second = partners(axis, periodic)
    return lax.ppermute(pair[0], axis, first), lax.ppermute(pair[1], axis, second)


def to_all(rows):
    return lax.all_to_all(rows, EVERY, 0, 0)


def to_half(rows, devices):
    groups = [[i for i in range(devices) if i % 2 == side] for side in range(2)]
    return lax.all_to_all(rows, EVERY, 0, 0, axis_index_groups=groups)


def to_pair(block):
    return lax.ppermute(block, "lon", partners("lon", True)[0])


def sigmoid(v):
    return 0.5 * jnp.tanh(0.5 * v) + 0.5


def silu(v):
    half = 0.5 * v
    return half + half * jnp.tanh(half)


def norm_consts(stats_ref, devices):
    stats = stats_ref[...]
    total = jnp.sum(stats, axis=0)
    center = total[0:1] * (1.0 / devices)
    apart = jnp.sum(jnp.square(stats - center[None]), axis=0)
    spread = (total[1:2] + apart[0:1]) * (1.0 / devices)
    return center, lax.rsqrt(spread + eps)


def top_sums(stats_ref, center, inv):
    stats = stats_ref[...]
    total = jnp.sum(stats, axis=0)
    apart = stats[:, 0:1, :] - center[None]
    return total[2:3], (total[3:4] + jnp.sum(apart * stats[:, 2:3, :], axis=0)) * inv


def shifted(value, width):
    return pltpu.roll(value, 1, 1), value, pltpu.roll(value, width - 1, 1)


def store_shifted(taps, slot, row, value, width, inner=None):
    for s, part in enumerate(shifted(value, width)):
        part = part.astype(LOW)
        taps[slot, s, pl.ds(row, 2)] = part
        if inner is not None:
            for k in range(2):
                at = row + k - (EXT - 1)
                if 0 <= at < inner.shape[2]:
                    inner[s, slot, at] = part[k, 0 : inner.shape[3]]


def lay_weights(kernel_ref, layer, back, out):
    blank = jnp.zeros((3 * LANES, LANES), LOW)
    out[9 * LANES : 12 * LANES, 0:LANES] = blank
    out[0 : 3 * LANES, LANES : 2 * LANES] = blank
    for r in range(3):
        for s in range(3):
            if back:
                block = kernel_ref[layer, (2 - r) * 3 + 2 - s].astype(F32).T.astype(LOW)
            else:
                block = kernel_ref[layer, r * 3 + s]
            at = (r * 3 + s) * LANES
            out[at : at + LANES, 0:LANES] = block
            out[at + 3 * LANES : at + 4 * LANES, LANES : 2 * LANES] = block


def even_parts(lo, hi, most):
    pairs = (hi - lo) // 2
    count = -(-pairs // most)
    out = []
    for k in range(count):
        start, stop = pairs * k // count, pairs * (k + 1) // count
        out.append((lo + 2 * start, stop - start))
    return out


def pusher():
    staged = [0, 0]

    def push(unit, tile):
        staged[unit] = 1 - staged[unit]
        pltpu.matmul_push_rhs(tile, staged[unit], unit)
        return staged[unit]

    return push


def pipeline(grids, lo, hi, taps, weight, cols, prepare, emit, after, finish, extra=None, take=None, extra_totals=()):
    parts = even_parts(lo, hi, 4)
    count = len(parts)

    def body(*refs):
        totals, more = refs[: 2 * count], refs[2 * count :]
        push = pusher()

        def operand(g, part, k):
            start, size = parts[part]
            halves = []
            for unit in (2 * k, 2 * k + 1):
                t, s = divmod(unit, 3)
                halves.append(jnp.concatenate([taps[g, s, start - 1 + t + 2 * n, 0:cols, :] for n in range(size)], axis=0))
            return jnp.concatenate(halves, axis=-1)

        def product(first, unit, part, k):
            def act():
                at = push(unit, weight[k * 2 * LANES : (k + 1) * 2 * LANES, :])
                pltpu.matmul_acc_lhs(totals[unit * count + part], operand(first + unit, part, k), load_staged_rhs=at)
            return act

        def collect(first, part):
            def act():
                start, size = parts[part]
                for unit in range(2):
                    both = pltpu.matmul_pop(totals[unit * count + part])
                    for n in range(size):
                        for h in range(2):
                            emit(first + unit, start + 2 * n + h, both[n * cols : (n + 1) * cols, h * LANES : (h + 1) * LANES])
            return act

        def rows_before(part):
            start, size = parts[part]
            return start + 2 * size + 1

        def ready(first, start, stop):
            return [functools.partial(prepare, first + unit, r) for r in range(start, stop, 2) for unit in range(2)]

        for task in ready(0, lo - 1, rows_before(0)):
            task()
        waiting = []

        def run(steps, tasks):
            done = 0
            for n, step in enumerate(steps):
                step()
                if n == 3:
                    while waiting:
                        waiting.pop(0)()
                while done < len(tasks) * (n + 1) // len(steps):
                    tasks[done]()
                    done += 1

        for first in range(0, grids, 2):
            last = first + 2 >= grids
            ahead = [] if last else ready(first + 2, lo - 1, hi + 1)
            if extra and last:
                run(extra(first, push, more), [])
                ahead = take(more)
            for part in range(count):
                tasks = []
                if first == 0 and part + 1 < count:
                    tasks += ready(0, rows_before(part), rows_before(part + 1))
                tasks += ahead[len(ahead) * part // count : len(ahead) * (part + 1) // count]
                run([product(first, unit, part, k) for k in range(6) for unit in range(2)], tasks)
                waiting.append(collect(first, part))
            waiting += [functools.partial(after, first + unit) for unit in range(2)]
            if extra and not last:
                run(extra(first, push, more), [])
        while waiting:
            waiting.pop(0)()
        finish()

    totals = [pltpu.ACC(unit)((size * cols, 2 * LANES), F32) for unit in range(2) for _, size in parts]
    pl.run_scoped(body, *totals, *extra_totals)


def guard(condition, act):
    if isinstance(condition, bool):
        if condition:
            act()
    else:
        pl.when(condition)(act)


def gather(sums, k, value):
    sums[k] = value if sums[k] is None else sums[k] + value


def fold(value):
    return jnp.sum(value.reshape(-1, 8, LANES), axis=0)


def to_row(value):
    return jnp.sum(value, axis=0, keepdims=True)


def both_ways(even, give_first, give_second):
    @pl.when(even == 1)
    def _():
        give_first(False)
        give_second(True)

    @pl.when(even == 0)
    def _():
        give_first(True)
        give_second(False)


def whichever(even, place, got_first, got_second):
    @pl.when(even == 1)
    def _():
        place(got_second, got_first)

    @pl.when(even == 0)
    def _():
        place(got_first, got_second)


def cut_rows(geo, info, sources, heights, first, second):
    grids, rows = geo["G"], geo["R"]

    def give(out):
        def act(low):
            at = 0
            for src, h in zip(sources, heights):
                for g in range(grids):
                    out[g, at : at + h] = src[g, 0:h] if low else src[g, src.shape[1] - h :]
                at += h
        return act

    both_ways(info[0], give(first), give(second))


def cut_cols(geo, info, sources, first, second):
    grids, cols = geo["G"], geo["C"]

    def give(out):
        def act(low):
            at = 0
            for src in sources:
                for g in range(grids):
                    part = src[g, :, 0:EXT, :] if low else src[g, :, cols - EXT : cols, :]
                    out[g, at : at + src.shape[1]] = part
                at += src.shape[1]
        return act

    both_ways(info[1], give(first), give(second))


def add_rows(geo, info, sources, heights, got_first, got_second, outs, start=0):
    grids, rows = geo["G"], geo["R"]

    def place(low, high):
        at = start
        for out, h in zip(outs, heights):
            for g in range(grids):
                out[g, 0:h] = low[g, at : at + h]
                out[g, h + rows : 2 * h + rows] = high[g, at : at + h]
            at += h

    whichever(info[0], place, got_first, got_second)
    for src, out, h in zip(sources, outs, heights):
        for g in range(grids):
            out[g, h : h + rows] = src[g]


def add_sides(geo, info, starts, got_first, got_second, outs):
    def place(low, high):
        for n, (out, at) in enumerate(zip(outs, starts)):
            total = out.shape[1]
            for g in range(geo["G"]):
                right = high[g, at : at + total].astype(F32)
                left = low[g, at : at + total].astype(F32)
                if n == 2:
                    right, left = pltpu.roll(right, EXT // 2, 1), pltpu.roll(left, EXT // 2, 1)
                out[g] = jnp.concatenate([right, left], axis=1).astype(LOW)

    whichever(info[1], place, got_first, got_second)


def across(pair, g, rows):
    parts = [ref[g, rows].astype(F32) for ref in pair]
    return jnp.concatenate(parts, axis=parts[0].ndim - 2)


def field_edge_kernel(geo, info, x, first, second, sems):
    rows = geo["R"]

    def fetch(high_out, low_out):
        copies = [
            pltpu.make_async_copy(x.at[:, rows - EXT : rows], high_out, sems.at[0]),
            pltpu.make_async_copy(x.at[:, 0:EXT], low_out, sems.at[1]),
        ]
        for c in copies:
            c.start()
        for c in copies:
            c.wait()

    @pl.when(info[0] == 1)
    def _():
        fetch(first, second)

    @pl.when(info[0] == 0)
    def _():
        fetch(second, first)


def mask_edge_kernel(geo, info, masks, first, second, near, sems):
    rows, height = geo["R"], geo["heights"][1]
    nears = [
        pltpu.make_async_copy(masks.at[0, :, 0:height], near.at[0], sems.at[0]),
        pltpu.make_async_copy(masks.at[0, :, rows - height : rows], near.at[1], sems.at[1]),
    ]
    for c in nears:
        c.start()
    for c in nears:
        c.wait()

    def give(out):
        def act(low):
            out[...] = near[0 if low else 1].astype(F32).astype(LOW)
        return act

    both_ways(info[0], give(first), give(second))


def tall_kernel(geo, heights, info, *refs):
    n = len(heights)
    talls = refs[n + 2 : 2 * n + 2]
    add_rows(geo, info, refs[:n], heights, refs[n], refs[n + 1], talls)
    cut_cols(geo, info, talls, refs[2 * n + 2], refs[2 * n + 3])


def mask_kernel(geo, masks, cot, *outs):
    for g in range(geo["G"]):
        for k in range(4):
            outs[k][g] = masks[k, g].astype(F32).astype(LOW)
        outs[4][g] = (cot[g].astype(F32) * masks[3, g].astype(F32)).astype(LOW)


def cut_kernel(geo, info, mask1, mask2, masked, cot, before, first, second):
    del before
    cut_rows(geo, info, [mask1, mask2, masked, cot], geo["heights"][2:], first, second)


def weights_kernel(which, kernels, before, *outs):
    del before
    for (layer, back), out in zip(which, outs):
        lay_weights(kernels, layer, back, out)


def late_kernel(geo, heights, info, *refs):
    n = len(heights)
    add_rows(geo, info, refs[:n], heights, refs[n], refs[n + 1], refs[n + 3 : 2 * n + 3], 0 if n == 1 else geo["heights"][2])
    if len(refs) > 2 * n + 3:
        cut_cols(geo, info, refs[n + 3 : n + 4], *refs[2 * n + 3 :])


def last_kernel(geo, info, tall2, tall3, tall4, before, first, second):
    del before
    cols, above, shared = geo["C"], tall2.shape[1], tall4.shape[1]
    extra = (tall3.shape[1] - shared) // 2
    cut_cols(geo, info, [tall2], first, second)

    def give(out):
        def act(low):
            at = pl.ds(0, EXT) if low else pl.ds(cols - EXT, EXT)
            place = lax.broadcasted_iota(jnp.int32, (shared, EXT, LANES), 1)
            near = place < EXT // 2 if low else place >= EXT // 2
            for g in range(geo["G"]):
                out[g, above : above + tall3.shape[1]] = tall3[g, :, at]
                mine = tall3[g, extra : extra + shared, at].astype(F32)
                other = pltpu.roll(tall4[g, :, at].astype(F32), EXT // 2, 1)
                out[g, above + extra : above + extra + shared] = jnp.where(near, mine, other).astype(LOW)
        return act

    both_ways(info[1], give(first), give(second))


def gate_kernel(sums, *refs):
    refs[-1][...] = sums[...]


def forward_kernel(layer, geo, *refs):
    grids, rows, devices, width, cols = geo["G"], geo["R"], geo["D"], geo["CE"], geo["C"]
    heights = geo["heights"]
    refs = list(refs)
    info, gains, offsets, biases, weight = (refs.pop(0) for _ in range(5))
    if layer:
        stats, pre_in = refs.pop(0), refs.pop(0)
    field = [refs.pop(0), refs.pop(0)] if layer == 2 else None
    members = geo["members"][layer]
    sources = [refs.pop(0) for _ in members]
    got = [refs.pop(0), refs.pop(0)]
    if layer in (1, 2):
        refs.pop(0)
    sums_out = refs.pop(0)
    side_outs = [refs.pop(0) for _ in members]
    pre_out, low_out = refs.pop(0), refs.pop(0)
    field_out = refs.pop(0) if layer == 2 else None
    taps, acts, acc = refs
    lo, hi = layer + 1, geo["RE"] - 1 - layer

    add_sides(geo, info, geo["starts"][layer], *got, side_outs)
    ext = [sources[0], side_outs[0]]
    if layer:
        center, inv = norm_consts(stats, devices)
        scale = inv * gains[layer - 1 : layer, :] * (1.0 / keep_rate)
        shift = offsets[layer - 1 : layer, :] * (1.0 / keep_rate) - center * scale
        scale = 0.5 * scale
    bias = biases[layer : layer + 1, :]
    number = rows * cols
    totals = [None] * grids

    def prepare(g, r):
        if layer == 0:
            value = across(ext, g, pl.ds(r, 2))
        else:
            p = pre_in[g, pl.ds(r, 2)]
            part = p * scale
            value = (part + part * jnp.tanh(0.5 * p) + shift) * across(ext, g, pl.ds(r - layer, 2))
            if layer == 2:
                value = value + across(field, g, pl.ds(r, 2))

                def save():
                    field_out[g, pl.ds(r - (EXT - 1), 2)] = value[:, 0:cols, :]

                guard((r >= EXT - 1) & (r < EXT + rows), save)
        store_shifted(taps, g, r, value, width, low_out)

    def emit(g, r, part):
        part = part + bias
        pre_out[g, r] = part
        if EXT <= r < EXT + rows:
            act = silu(part[0:cols])
            acts[g, r - EXT] = act
            gather(totals, g, fold(act))

    def after(g):
        mean = to_row(totals[g]) * (1.0 / number)
        square = jnp.zeros((8, LANES), F32)
        first = jnp.zeros((8, LANES), F32)
        second = jnp.zeros((8, LANES), F32)
        for k in range(rows):
            act = acts[g, k]
            apart = act - mean
            square = square + fold(jnp.square(apart))
            if layer == 3:
                z = sources[1][g, heights[4] + k].astype(F32)
                first = first + fold(z)
                second = second + fold(z * apart)
            if layer == 0:
                p = pre_out[g, EXT + k, 0:cols, :]
                s = sigmoid(p)
                slope = s + act * (1.0 - s)
                first = first + fold(slope)
                second = second + fold(slope * act)
        acc[g : g + 1] = mean
        acc[grids + g : grids + g + 1] = to_row(square) * (1.0 / number)
        if layer in (0, 3):
            acc[2 * grids + g : 2 * grids + g + 1] = to_row(first)
            acc[3 * grids + g : 3 * grids + g + 1] = to_row(second)

    def finish():
        means = acc[0:grids]
        middle = jnp.mean(means, axis=0, keepdims=True)
        away = means - middle
        spread = jnp.mean(acc[grids : 2 * grids] + jnp.square(away), axis=0, keepdims=True)
        out = [middle, spread]
        if layer == 3:
            ones = acc[2 * grids : 3 * grids]
            out.append(to_row(ones) * (1.0 / keep_rate))
            out.append(to_row(acc[3 * grids : 4 * grids] + away * ones) * (1.0 / keep_rate))
        if layer == 0:
            out += [to_row(acc[2 * grids : 3 * grids]), to_row(acc[3 * grids : 4 * grids])]
        for k, row in enumerate(out):
            sums_out[:, k : k + 1, :] = jnp.broadcast_to(row[None], (devices, 1, LANES))

    pipeline(grids, lo, hi, taps, weight, width, prepare, emit, after, finish)


def back_consts(layer, geo, stats, sums, gains):
    center, inv = norm_consts(stats, geo["D"])
    if layer == 3:
        one, two = top_sums(stats, center, inv)
    else:
        total = jnp.sum(sums[...], axis=0)
        one, two = total[0:1], total[1:2]
    pixels = float(geo["D"] * geo["G"] * geo["R"] * geo["C"])
    scale = inv * gains[layer : layer + 1, :]
    tilt = scale * inv * two * (-1.0 / pixels)
    flat = scale * one * (-1.0 / pixels) - center * tilt
    return center, inv, scale * (1.0 / keep_rate), flat, tilt


def through(p, dn, scale, flat, tilt):
    s = sigmoid(p)
    act = p * s
    return (dn * scale + act * tilt + flat) * (s + act * (1.0 - s)), act


def weight_totals():
    return [pltpu.ACC(n % 2)((LANES, 2 * LANES), F32) for n in range(5)]


def weight_steps(geo, low, inside, first, push, totals):
    rows, cols = geo["R"], geo["C"]
    depth = 2 * LANES // cols
    steps = []
    for g in (first, first + 1):
        for at in range(0, rows, depth):
            turned = []

            def act(n, g=g, at=at, turned=turned):
                if not turned:
                    turned.append(inside(g, at, depth).reshape(2 * LANES, LANES).T)
                halves = []
                for tap in (2 * n, 2 * n + 1):
                    r, s = divmod(min(tap, 8), 3)
                    halves.append(low[s, g, at + r : at + r + depth].reshape(2 * LANES, LANES))
                staged = push(n % 2, jnp.concatenate(halves, axis=-1))
                pltpu.matmul_acc_lhs(totals[n], turned[0], load_staged_rhs=staged)

            steps += [functools.partial(act, n) for n in range(5)]
    return steps


def take_term(term, totals):
    def act(n):
        both = pltpu.matmul_pop(totals[n])
        for tap in range(2 * n, min(2 * n + 2, 9)):
            at = (tap - 2 * n) * LANES
            term[tap * LANES : (tap + 1) * LANES] = both[:, at : at + LANES].T

    return [functools.partial(act, n) for n in range(5)]


def split_halves(info, term, keep_half, send_half):
    half = 9 * LANES // 2
    start = pl.multiple_of((1 - info[1]) * half, 8)
    keep_half[...] = term[pl.ds(start, half)]
    send_half[...] = term[pl.ds(pl.multiple_of(half - start, 8), half)]


def backward_kernel(layer, geo, *refs):
    grids, rows, devices, width, cols = geo["G"], geo["R"], geo["D"], geo["CE"], geo["C"]
    heights = geo["heights"]
    refs = list(refs)
    info, gains, offsets, weight, stats, sums, pre, low = (refs.pop(0) for _ in range(8))
    masked = keep_top = field = cot = z_in = None
    if layer == 3:
        masked, keep_top, field = [refs.pop(0), refs.pop(0)], refs.pop(0), refs.pop(0)
    else:
        z_in = refs.pop(0)
    if layer == 2:
        cot = [refs.pop(0), refs.pop(0)]
    keep = [refs.pop(0), refs.pop(0)]
    stats_below, pre_below = refs.pop(0), refs.pop(0)
    sums_out, keep_half, send_half, z_out = (refs.pop(0) for _ in range(4))
    grad_out = refs.pop(0) if layer == 2 else None
    result = refs.pop(0) if layer == 3 else None
    taps, term = refs[:2]
    if layer == 3:
        result_out, (result, sems) = result, refs[2:]
        leaving = [pltpu.make_async_copy(result.at[g], result_out.at[g], sems.at[g]) for g in range(grids)]
    lo, hi = EXT - layer, EXT + rows + layer
    keep_off = EXT - heights[layer]

    center, inv, scale, flat, tilt = back_consts(layer, geo, stats, sums, gains)
    first_row, last_row = info[2], info[3]
    center_b, inv_b = norm_consts(stats_below, devices)
    sums_here = [None] * 4

    if layer == 3:
        lift = inv * gains[layer : layer + 1, :] * (1.0 / keep_rate)
        base = offsets[layer : layer + 1, :] * (1.0 / keep_rate) - center * lift

    def prepare(g, r):
        if layer == 3:
            z = across(masked, g, pl.ds(r - (EXT - heights[4]), 2))
        else:
            z = z_in[g, pl.ds(r, 2)]
        value, act = through(pre[g, pl.ds(r, 2)], z, scale, flat, tilt)
        if not (isinstance(r, int) and EXT <= r and r + 2 <= EXT + rows):
            real = [jnp.where((r + k >= first_row) & (r + k < last_row), 1.0, 0.0).astype(F32) for k in range(2)]
            value = jnp.stack([value[0] * real[0], value[1] * real[1]])
        store_shifted(taps, g, r, value, width)
        if layer == 3:
            def save():
                y = (act[:, 0:cols] * lift + base) * keep_top[g, pl.ds(r - EXT, 2)].astype(F32)
                result[g, pl.ds(r - EXT, 2)] = (field[g, pl.ds(r - EXT + 1, 2)] + y).astype(LOW)

            guard((r >= EXT) & (r < EXT + rows), save)

    def emit(g, r, part):
        inner = EXT <= r < EXT + rows
        if layer == 2:
            part = part + across(cot, g, r - (EXT - heights[5]))
            if inner:
                grad_out[g, r - EXT] = part[0:cols]
        z = part * across(keep, g, r - keep_off)
        z_out[g, r] = z
        if inner:
            z = z[0:cols]
            p = pre_below[g, r, 0:cols, :]
            s = sigmoid(p)
            act = p * s
            gather(sums_here, 0, fold(z))
            gather(sums_here, 1, fold(z * (act - center_b)))
            if layer == 1:
                gather(sums_here, 3, fold(z * (s + act * (1.0 - s))))

    def inside(g, at, depth):
        return taps[g, 1, EXT + at : EXT + at + depth, 0:cols, :]

    def after(g):
        if layer == 3:
            leaving[g].start()
        gather(sums_here, 2, fold(inside(g, 0, rows).astype(F32)))

    def finish():
        split_halves(info, term, keep_half, send_half)
        out = [to_row(sums_here[k]) for k in range(4 if layer == 1 else 3)]
        out[0] = out[0] * (1.0 / keep_rate)
        out[1] = out[1] * inv_b * (1.0 / keep_rate)
        if layer == 1:
            out[3] = out[3] * (1.0 / keep_rate)
        for k, row in enumerate(out):
            sums_out[:, k : k + 1, :] = jnp.broadcast_to(row[None], (devices, 1, LANES))
        if layer == 3:
            for c in leaving:
                c.wait()

    steps = functools.partial(weight_steps, geo, low, inside)
    take = functools.partial(take_term, term)
    pipeline(grids, lo, hi, taps, weight, width, prepare, emit, after, finish, steps, take, weight_totals())


def first_weight_kernel(geo, *refs):
    grids, rows, cols = geo["G"], geo["R"], geo["C"]
    info, gains, stats, sums, pre, low, z_in, sent, keep_half, send_both, dpre, term = refs
    half = 9 * LANES // 2
    send_both[0:half] = sent[...]
    scale, flat, tilt = back_consts(0, geo, stats, sums, gains)[2:]
    first_row, last_row = info[2], info[3]

    def prepare(g, k):
        r = EXT - 1 + k
        value, _ = through(pre[g, r], z_in[g, r], scale, flat, tilt)
        if k in (0, rows + 1):
            value = value * jnp.where((r >= first_row) & (r < last_row), 1.0, 0.0).astype(F32)
        dpre[g, k] = value.astype(LOW)

    def ready(first):
        return [functools.partial(prepare, first + unit, k) for k in range(rows + 2) for unit in range(2)]

    def inside(g, at, depth):
        return dpre[g, 1 + at : 1 + at + depth, 0:cols, :]

    def body(*totals):
        push = pusher()
        for task in ready(0):
            task()
        for first in range(0, grids, 2):
            tasks = ready(first + 2) if first + 2 < grids else []
            steps = weight_steps(geo, low, inside, first, push, totals)
            done = 0
            for n, step in enumerate(steps):
                step()
                while done < len(tasks) * (n + 1) // len(steps):
                    tasks[done]()
                    done += 1
        for task in take_term(term, totals):
            task()
        split_halves(info, term, keep_half, send_both.at[half : 2 * half])

    pl.run_scoped(body, *weight_totals())


def input_grad_kernel(geo, weight, dpre, grad, gains, *refs):
    out, taps = refs[7], refs[11]
    grids, rows, width, cols = geo["G"], geo["R"], geo["CE"], geo["C"]

    def prepare(g, r):
        store_shifted(taps, g, r, dpre[g, pl.ds(r, 2)].astype(F32), width)

    def emit(g, r, part):
        out[g, r - 1] = grad[g, r - 1] + part

    def finish():
        gather_rows(geo, gains, *refs[0:7], *refs[8:11])

    pipeline(grids, 1, rows + 1, taps, weight, cols, prepare, emit, lambda g: None, finish)


def share_kernel(*refs):
    third, second, both, _, out = refs[4:]
    half = 9 * LANES // 2
    gots = [both[half : 2 * half], both[0:half], second[...], third[...]]
    for k in range(4):
        out[k * half : (k + 1) * half] = (refs[k][...] + gots[k]).astype(LOW)


def total_kernel(devices, got, out):
    total = jnp.sum(got[...].astype(F32), axis=0)
    out[...] = jnp.broadcast_to(total.astype(LOW)[None], out.shape)


def write_half(upper, block, out, buffer, sems):
    half = 9 * LANES // 2
    start = pl.multiple_of(upper * half, 8)
    leaving = [pltpu.make_async_copy(buffer.at[k], out.at[k, pl.ds(start, half)], sems.at[k]) for k in range(4)]
    for k in range(4):
        buffer[k] = block[k].astype(F32)
        leaving[k].start()
    return leaving


def own_half_kernel(info, block, grad, out, grad_out, buffer, sems, grad_sem):
    leaving = write_half(1 - info[1], block, out, buffer, sems)
    leaving.append(pltpu.make_async_copy(grad, grad_out, grad_sem.at[0]))
    leaving[-1].start()
    for c in leaving:
        c.wait()


def other_half_kernel(info, block, _, out, buffer, sems):
    for c in write_half(info[1], block, out, buffer, sems):
        c.wait()


def gather_rows(geo, gains, *refs):
    stats, sums = refs[0:4], refs[4:7]
    bias_out, gain_out, offset_out = refs[7:]
    for layer in range(4):
        center, inv = norm_consts(stats[layer], geo["D"])
        if layer == 3:
            one, two = top_sums(stats[3], center, inv)
        else:
            total = jnp.sum(sums[layer][...], axis=0)
            one, two = total[0:1], total[1:2]
        offset_out[layer : layer + 1] = one
        gain_out[layer : layer + 1] = two
        if layer:
            bias_out[layer : layer + 1] = jnp.sum(sums[layer - 1][...], axis=0)[2:3]
        else:
            pixels = float(geo["D"] * geo["G"] * geo["R"] * geo["C"])
            slopes = jnp.sum(stats[0][...], axis=0)
            flat, lifted = slopes[2:3], (slopes[3:4] - center * slopes[2:3]) * inv
            bias_out[0:1] = inv * gains[0:1, :] * (total[3:4] - flat * one / pixels - lifted * two / pixels)


def call(kernel, operands, outs, scratch=(), flops=10**6, moved=10**6, scalars=1, final=(), small=(), outside=False, onto=None):
    space = pl.BlockSpec(memory_space=pltpu.VMEM)
    specs = [pl.BlockSpec(memory_space=pltpu.SMEM)] * scalars
    operands = list(operands)
    for k in range(scalars, len(operands)):
        if outside or k == onto:
            specs.append(pl.BlockSpec(memory_space=pltpu.HBM))
            operands[k] = pltpu.with_memory_space_constraint(operands[k], pltpu.HBM)
        else:
            specs.append(space)
            operands[k] = pltpu.with_memory_space_constraint(operands[k], pltpu.VMEM)
    plain = set(final) | set(small)
    shapes = [jax.ShapeDtypeStruct(s, d) if k in plain else pltpu.VMEM(s, d) for k, (s, d) in enumerate(outs)]
    places = [pl.BlockSpec(memory_space=pltpu.HBM) if k in final else space for k in range(len(outs))]
    return pl.pallas_call(
        kernel,
        in_specs=specs,
        out_specs=places,
        input_output_aliases={} if onto is None else {onto: 0},
        out_shape=shapes,
        scratch_shapes=[v if hasattr(v, "shape") and not isinstance(v, tuple) else pltpu.VMEM(*v) for v in scratch],
        compiler_params=pltpu.CompilerParams(vmem_limit_bytes=10 * 2**20),
        cost_estimate=pl.CostEstimate(flops=flops, bytes_accessed=moved, transcendentals=0),
    )(*operands)


def conv_scratch(geo, tall):
    return [((geo["G"], 3, tall, geo["CE"], LANES), LOW)]


def forward_call(layer, geo, operands):
    grids, rows, rows_ext, width, devices, cols = geo["G"], geo["R"], geo["RE"], geo["CE"], geo["D"], geo["C"]
    kinds = 4 if layer in (0, 3) else 2
    outs = [((devices, kinds, LANES), F32)]
    for k in geo["members"][layer]:
        outs.append(((grids, rows + 2 * geo["heights"][k], 2 * EXT, LANES), LOW))
    outs.append(((grids, rows_ext, width, LANES), F32))
    outs.append(((3, grids, rows + 2, cols, LANES), LOW))
    if layer == 2:
        outs.append(((grids, rows + 2, cols, LANES), F32))
    scratch = conv_scratch(geo, rows_ext) + [((grids, rows, cols, LANES), F32), ((kinds * grids, LANES), F32)]
    return call(functools.partial(forward_kernel, layer, geo), operands, outs, scratch, 2 * 10**9, 8 * 10**6)


def backward_call(layer, geo, operands):
    grids, rows, rows_ext, width, devices, cols = geo["G"], geo["R"], geo["RE"], geo["CE"], geo["D"], geo["C"]
    half = ((9 * LANES // 2, LANES), F32)
    outs = [((devices, 4 if layer == 1 else 3, LANES), F32), half, half, ((grids, rows_ext, width, LANES), F32)]
    if layer == 2:
        outs.append(((grids, rows, cols, LANES), F32))
    if layer == 3:
        outs.append(((grids, rows, cols, LANES), LOW))
    scratch = conv_scratch(geo, rows_ext) + [((9 * LANES, LANES), F32)]
    if layer == 3:
        scratch += [((grids, rows, cols, LANES), LOW), pltpu.SemaphoreType.DMA((grids,))]
    return call(
        functools.partial(backward_kernel, layer, geo), operands, outs, scratch, 3 * 10**9, 8 * 10**6,
        final=(4,) if layer == 3 else (),
    )


def local(inputs, kernels, biases, gains, offsets, keep_masks, cotangent):
    grids, rows, cols, _ = inputs.shape
    devices = lax.axis_size("batch") * lax.axis_size("lat") * lax.axis_size("lon")
    heights = [EXT, 7, 6, 5, 4, 2]
    above = rows + 2 * heights[3]
    starts = [0, above, above + heights[4] - heights[5]]
    geo = dict(
        G=grids, R=rows, C=cols, D=devices, RE=rows + 2 * EXT, CE=cols + 2 * EXT, heights=heights,
        starts=[[0], [0], [0], starts], members=[[0], [1], [2], [3, 4, 5]],
    )
    lat, lon = lax.axis_index("lat"), lax.axis_index("lon")
    info = jnp.stack(
        [
            1 - lax.rem(lat, 2),
            1 - lax.rem(lon, 2),
            jnp.where(lat == 0, EXT, 0),
            jnp.where(lat == lax.axis_size("lat") - 1, EXT + rows, rows + 2 * EXT),
        ]
    ).astype(jnp.int32)
    kernels = kernels.reshape(4, 9, LANES, LANES)

    def block(tall, wide):
        return ((grids, tall, wide, LANES), LOW)

    x_height, soon, late = heights[0], heights[1], sum(heights[2:])
    pair_sems = pltpu.SemaphoreType.DMA((2,))
    outs = call(
        functools.partial(field_edge_kernel, geo), [info, inputs], [block(x_height, cols)] * 2, [pair_sems], outside=True
    )
    x_got = trade(outs, "lat", False)
    outs = call(
        functools.partial(mask_edge_kernel, geo), [info, keep_masks], [block(soon, cols)] * 2,
        [((2, grids, soon, cols, LANES), jnp.int32), pair_sems], outside=True,
    )
    soon_got = trade(outs, "lat", False)

    def weights_for(which, before):
        outs = [((12 * LANES, 2 * LANES), LOW)] * len(which)
        return list(call(functools.partial(weights_kernel, which), [kernels, before], outs, scalars=0))

    weights = weights_for([(0, False), (1, False)], outs[0])
    outs = call(
        functools.partial(tall_kernel, geo, heights[:1]), [info, inputs, *x_got],
        [block(rows + 2 * x_height, cols)] + [block(rows + 2 * x_height, EXT)] * 2,
    )
    pieces = [[outs[0], *trade(outs[1:3], "lon", True)]]
    outs = call(functools.partial(mask_kernel, geo), [keep_masks, cotangent], [block(rows, cols)] * 5, scalars=0)
    low_masks, masked = list(outs[0:4]), outs[4]
    outs = call(
        functools.partial(tall_kernel, geo, heights[1:2]), [info, low_masks[0], *soon_got],
        [block(rows + 2 * soon, cols)] + [block(rows + 2 * soon, EXT)] * 2,
    )
    pieces.append([outs[0], *trade(outs[1:3], "lon", True)])
    edges = call(
        functools.partial(cut_kernel, geo), [info, low_masks[1], low_masks[2], masked, cotangent, outs[1]],
        [block(late, cols)] * 2,
    )
    late_got = trade(edges, "lat", False)
    talls = [rows + 2 * h for h in heights[2:]]

    pres, lows, stats, exts = [None] * 4, [None] * 4, [None] * 4, [None] * 6
    field = order = last = None
    for layer in range(4):
        operands = [info, gains, offsets, biases, weights[layer]]
        if layer:
            operands += [stats[layer - 1], pres[layer - 1]]
        if layer == 2:
            operands += exts[0]
        operands += pieces[layer]
        if layer in (1, 2):
            operands.append(order)
        outs = list(forward_call(layer, geo, operands))
        part = outs.pop(0)
        if layer < 2:
            beside = []
            if layer == 0:
                weights += weights_for([(2, False), (3, False), (0, True), (1, True), (2, True), (3, True)], part)
                beside = weights[2:]
            else:
                beside = last = call(
                    functools.partial(late_kernel, geo, heights[3:]),
                    [info, low_masks[2], masked, cotangent, *late_got, part], [block(t, cols) for t in talls[1:]],
                )
            (part,) = call(gate_kernel, [part, *pieces[layer + 1][1:], *beside], [(part.shape, F32)], scalars=0)
        stats[layer] = to_all(part)
        if layer == 0:
            ends = call(
                functools.partial(late_kernel, geo, heights[2:3]), [info, low_masks[1], *late_got, stats[0]],
                [block(talls[0], cols)] + [block(talls[0], EXT)] * 2,
            )
            pieces.append([ends[0], *trade(ends[1:3], "lon", True)])
            order = ends[1]
        if layer == 1:
            edges = call(
                functools.partial(last_kernel, geo), [info, *last, stats[1]], [block(talls[1] + talls[2], EXT)] * 2
            )
            pieces.append([*last, *trade(edges, "lon", True)])
            order = edges[0]
        for n, k in enumerate(geo["members"][layer]):
            exts[k] = [pieces[layer][n], outs.pop(0)]
        pres[layer], lows[layer] = outs.pop(0), outs.pop(0)
        if layer == 2:
            field = outs.pop(0)

    sums = [None] * 4
    sums[3] = stats[3]
    kept, got = [None] * 4, []
    z = grad = output = None
    for layer in (3, 2, 1):
        operands = [info, gains, offsets, weights[4 + layer], stats[layer], sums[layer], pres[layer], lows[layer]]
        operands += [*exts[4], low_masks[3], field] if layer == 3 else [z]
        if layer == 2:
            operands += exts[5]
        operands += [*exts[layer], stats[layer - 1], pres[layer - 1]]
        outs = backward_call(layer, geo, operands)
        sums[layer - 1] = to_all(outs[0])
        kept[layer], sent = outs[1], outs[2]
        if layer > 1:
            got.append(to_pair(sent))
        z = outs[3]
        if layer == 2:
            grad = outs[4]
        if layer == 3:
            output = outs[4]
    half = 9 * LANES // 2
    term = ((half, LANES), F32)
    kept[0], sent, dpre = call(
        functools.partial(first_weight_kernel, geo), [info, gains, stats[0], sums[0], pres[0], lows[0], z, sent],
        [term, ((2 * half, LANES), F32), block(rows + 2, cols + 2 * EXT)], [((9 * LANES, LANES), F32)], 10**9, 8 * 10**6,
    )
    got.append(to_pair(sent))

    small = ((4, LANES), F32)
    field_like = ((grids, rows, cols, LANES), F32)
    input_grad, bias_grad, gain_grad, offset_grad = call(
        functools.partial(input_grad_kernel, geo), [weights[4], dpre, grad, gains] + stats + sums[:3],
        [field_like] + [small] * 3, conv_scratch(geo, rows + 2), 10**9, 3 * 10**6, scalars=0, small=(1, 2, 3),
    )

    (shares,) = call(share_kernel, kept + got + [input_grad], [((4 * half, LANES), LOW)], scalars=0)
    slots = (devices // 2, 4 * half // (devices // 2), LANES)
    arrived = to_half(shares.reshape(slots), devices)
    (mine,) = call(functools.partial(total_kernel, devices), [arrived], [(slots, LOW)], scalars=0)
    mine = to_half(mine, devices).reshape(4, half, LANES)
    other = to_pair(mine)
    whole = ((4, 9 * LANES, LANES), F32)
    scratch = [((4, half, LANES), F32), pltpu.SemaphoreType.DMA((4,))]
    kernel_grad, input_grad = call(
        own_half_kernel, [info, mine, input_grad], [whole, field_like], scratch + [pltpu.SemaphoreType.DMA((1,))], final=(0, 1)
    )
    (kernel_grad,) = call(other_half_kernel, [info, other, kernel_grad], [whole], scratch, final=(0,), onto=2)
    return (output, input_grad, kernel_grad.reshape(4, 3, 3, LANES, LANES), bias_grad, gain_grad, offset_grad)


def solution(mesh):
    in_specs = (
        P("batch", "lat", "lon", None),
        P(),
        P(),
        P(),
        P(),
        P(None, "batch", "lat", "lon", None),
        P("batch", "lat", "lon", None),
    )
    out_specs = (P("batch", "lat", "lon", None), P("batch", "lat", "lon", None), P(), P(), P(), P())
    return jax.shard_map(local, mesh=mesh, in_specs=in_specs, out_specs=out_specs, check_vma=False)
```
